32 devices in a mesh: dp: 16 (over z, y, x), stream: 2 (over core).
Axes of the slice: x: 2, y: 2, z: 4, core: 2. Of those that a mesh axis runs over, the one named last changes fastest.
Arguments:
- tokens: bfloat16 [16384, 512], P(('dp', 'stream')), may hold values from -6 to 6
- memory: bfloat16 [16384, 512], P(('dp', 'stream')), may hold values from -6 to 6
- cotangent: bfloat16 [16384, 512], P(('dp', 'stream')), may hold values from -6 to 6
- segments: int32 [16384], P(('dp', 'stream')), may hold values from 0 to 1039, as said below
- padding: int32 [16384], P(('dp', 'stream')), may hold values from 0 to 1, as said below
- priority: int32 [16384], P(('dp', 'stream')), may hold values from 0 to 4095
- threshold: int32 [16384], P(('dp', 'stream')), may hold values from 0 to 4096
- master: float32 [8192, 512], P(('dp', 'stream'))
- momentum: float32 [8192, 512], P(('dp', 'stream')), may hold values from -80 to 80
- vectors: float32 [8704], replicated
- vec_first: float32 [8704], replicated, may hold values from -224 to 224
- vec_second: float32 [8704], replicated, may hold values from 1.47456 to 5.89824
- step_count: int32 [1], replicated, may hold values from 2 to 20
Outputs:
- layer_out: bfloat16 [16384, 512], P(('dp', 'stream'))
- input_grad: float32 [16384, 512], P(('dp', 'stream'))
- memory_grad: float32 [16384, 512], P(('dp', 'stream'))
- new_momentum: float32 [8192, 512], P(('dp', 'stream'))
- new_master: float32 [8192, 512], P(('dp', 'stream'))
- new_vectors: float32 [8704], replicated
- new_vec_first: float32 [8704], replicated
- new_vec_second: float32 [8704], replicated
The draws below stay inside these ranges and needn't reach their ends.
Inputs may be any that keep to these rules, and one draw needn't show every extreme that they name: `segments`: ids never fall and never cross an aligned block of 1024 rows. A block holds one whole document of 1024 tokens (some blocks in every draw) or sentences of 16 to 44 tokens, whose last one may be cut off by the block's end. `padding`: 1 exactly on the rows of a sentence cut off by its block's end.
All inputs are finite; a program needn't handle non-finite values.
Results may differ from the reference program's by a relative error of at most 0.025.
The reference program's roundings to bfloat16 on the way count: a program that leaves them out, or rounds other values in their place, can miss the bound.
Values may be sent and summed in bfloat16 or wider, within the bound.
A program may use at most 256 MiB of HBM per device.

```python
import math
import jax
import jax.numpy as jnp
from jax import lax

D = 512
HEADS = 8
HEAD = 64
FF = 2048
SENT_MIN = 16
SENT_MAX = 44
DOC_EVERY = 8
PRIO = 4096
KROWS = 1024
TOKENS = 16384
MROWS = 8192
VEC = 8704


def layout(key):
    base_key = jax.random.fold_in(key, 11)
    len_key = jax.random.fold_in(base_key, 1)
    doc_key = jax.random.fold_in(base_key, 2)
    blocks = TOKENS // KROWS
    slot_count = KROWS // SENT_MIN + 1
    sent_len = jax.random.randint(len_key, (blocks, slot_count), SENT_MIN, SENT_MAX + 1)
    sent_ends = jnp.cumsum(sent_len, axis=1)
    places = jnp.arange(KROWS, dtype=jnp.int32)
    sentence = jnp.sum((sent_ends[:, None, :] <= places[None, :, None]).astype(jnp.int32), axis=2)
    ending = jnp.take_along_axis(sent_ends, sentence, axis=1)
    padded = (ending > KROWS).astype(jnp.int32)
    doc_shift = jax.random.randint(doc_key, (), 0, DOC_EVERY)
    doc_block = ((jnp.arange(blocks) + doc_shift) % DOC_EVERY == 0)[:, None]
    sentence = jnp.where(doc_block, 0, sentence)
    padded = jnp.where(doc_block, 0, padded)
    seg_ids = jnp.arange(blocks, dtype=jnp.int32)[:, None] * slot_count + sentence
    return (seg_ids.reshape(-1).astype(jnp.int32), padded.reshape(-1).astype(jnp.int32))


def draw_segments(key, part):
    return layout(key)[0]


def draw_padding(key, part):
    return layout(key)[1]


def draw_master(key, part):
    own_key = jax.random.fold_in(key, 5)
    total = 8 * D + 2 * FF
    noise = jnp.clip(jax.random.normal(own_key, (total, D), jnp.float32), -4.0, 4.0)
    row_ids = jnp.arange(total)
    block_ids = row_ids // D
    out_proj = ((block_ids == 3) | (block_ids == 7)) & (row_ids < 8 * D)
    scale = jnp.where(row_ids >= 8 * D + FF, FF ** (-0.5), D ** (-0.5))
    scale = jnp.where(out_proj, (D // 16) ** (-0.5), scale)
    return (noise * scale[:, None]).astype(jnp.float32)


def draw_vectors(key, part):
    own_key = jax.random.fold_in(key, 9)
    noise = jnp.clip(jax.random.normal(own_key, (13 * D + FF,), jnp.float32), -4.0, 4.0)
    slot_ids = jnp.arange(13 * D + FF) // D
    is_gain = (slot_ids == 0) | (slot_ids == 2) | (slot_ids == 4)
    return jnp.where(is_gain, 1.0 + 0.15 * noise, 0.3 * noise).astype(jnp.float32)


def place_ends(values, key, least, top_value):
    extent = values.shape
    index_at = [jax.random.randint(jax.random.fold_in(key, axis), (), 0, extent[axis]) for axis in range(len(extent))]
    values = values.at[tuple(index_at)].set(least)
    longest = extent.index(max(extent))
    index_at[longest] = (index_at[longest] + 1) % extent[longest]
    return values.at[tuple(index_at)].set(top_value)


def shard_levels(stream_key, dims, cuts, least, high):
    def one(dim, parts):
        heights = jax.random.uniform(jax.random.fold_in(jax.random.fold_in(stream_key, 6), dim), (parts,), jnp.float32, least / len(cuts), high / len(cuts))
        return jnp.repeat(jnp.exp(heights), dims[dim] // parts).reshape((-1,) + (1,) * (len(dims) - dim - 1))

    gain = one(*cuts[0])
    for cut in cuts[1:]:
        gain = gain * one(*cut)
    return gain


def bell_draw(key, shape, width, bound, shards=(), held_as=jnp.bfloat16):
    values = jax.random.normal(key, shape, jnp.float32) * width
    if len(shards) > 0:
        values = shard_levels(key, shape, shards, -0.22, 0.18) * values
    return jnp.clip(values, min=-bound, max=bound).astype(held_as)


def setup_inputs(seed: int = 0) -> dict:
    arg_keys = jax.random.split(jax.random.key(seed), 14)
    return {
        "tokens": bell_draw(arg_keys[0], (TOKENS, D), 1.0, 6.0, ((0, 32),)),
        "memory": bell_draw(arg_keys[1], (TOKENS, D), 1.0, 6.0, ((0, 32),)),
        "cotangent": bell_draw(arg_keys[2], (TOKENS, D), 1.0, 6.0, ((0, 32),)),
        "segments": draw_segments(jax.random.fold_in(arg_keys[13], 71), 0),
        "padding": draw_padding(jax.random.fold_in(arg_keys[13], 71), 0),
        "priority": place_ends(jax.random.randint(arg_keys[5], (TOKENS,), 0, PRIO), jax.random.fold_in(arg_keys[5], 1), 0, PRIO - 1).astype(jnp.int32),
        "threshold": place_ends(jax.random.randint(arg_keys[6], (TOKENS,), 0, PRIO + 1), jax.random.fold_in(arg_keys[6], 1), 0, PRIO).astype(jnp.int32),
        "master": draw_master(jax.random.fold_in(arg_keys[13], 71), 0),
        "momentum": bell_draw(arg_keys[8], (MROWS, D), (0.1 * TOKENS ** 0.5), 80.0, ((0, 32),), jnp.float32),
        "vectors": draw_vectors(jax.random.fold_in(arg_keys[13], 71), 0),
        "vec_first": bell_draw(arg_keys[10], (VEC,), (0.3 * TOKENS ** 0.5), 224.0, (), jnp.float32),
        "vec_second": jnp.clip(jnp.exp(jax.random.uniform(arg_keys[11], (VEC,), jnp.float32, math.log(1.47456), math.log(5.89824))), 1.47456, 5.89824),
        "step_count": jax.random.randint(arg_keys[12], (1,), 2, 21).astype(jnp.int32),
    }


@jax.custom_vjp
def low(v):
    return lax.optimization_barrier(v.astype(jnp.bfloat16)).astype(jnp.float32)

@jax.custom_vjp
def low_back(v):
    return v

def low_keep(v):
    return (low(v), None)

def low_pass(kept, grad):
    return (grad,)

def back_keep(v):
    return (v, None)

def back_low(kept, grad):
    return (low(grad),)
low.defvjp(low_keep, low_pass)
low_back.defvjp(back_keep, back_low)
HIGH = lax.Precision.HIGHEST
NS_A = 3.4445
NS_B = -4.775
NS_C = 2.0315
MUON_RATE = 0.8
ADAM_RATE = 0.2
ADAM_DECAY = 0.01

def matmul_hi(left_mat, right_mat):
    return jnp.dot(left_mat, right_mat, precision=HIGH)

def layer_norm(values, gain_vec, shift_vec):
    center = values - lax.optimization_barrier(jnp.mean(values, axis=-1, keepdims=True))
    spread = lax.rsqrt(lax.optimization_barrier(jnp.mean(center * center, axis=-1, keepdims=True)) + 1e-05)
    return center * spread * gain_vec + shift_vec

def attend(queries, keys_in, values_in, visible):
    row_count = queries.shape[0]
    query_heads = queries.reshape(row_count, HEADS, HEAD)
    key_heads = keys_in.reshape(keys_in.shape[0], HEADS, HEAD)
    value_heads = values_in.reshape(values_in.shape[0], HEADS, HEAD)
    scores = low_back(jnp.einsum('qhe,khe->hqk', query_heads, key_heads, precision=HIGH))
    scores = jnp.where(visible[None], scores * HEAD ** (-0.5), -1e+30)
    weights_low = low(jax.nn.softmax(scores, axis=-1))
    mixed = jnp.einsum('hqk,khe->qhe', weights_low, value_heads, precision=HIGH)
    return mixed.reshape(row_count, HEADS * HEAD)

def vector_part(vectors, position):
    return vectors[position * D:(position + 1) * D]

def block_forward(weights, vectors, tokens, memory, segments, padding, priority, threshold):
    attn_w = weights[:8 * D].reshape(8, D, D)
    w_in = weights[8 * D:8 * D + FF]
    w_out = weights[8 * D + FF:]
    place = jnp.arange(segments.shape[0])
    diagonal = place[:, None] == place[None, :]
    same_seg = segments[:, None] == segments[None, :]
    open_key = (padding == 0)[None, :]
    vis_self = same_seg & ((priority[None, :] < threshold[:, None]) & open_key | diagonal)
    vis_cross = same_seg & (open_key | diagonal)
    h_one = low(layer_norm(tokens, vector_part(vectors, 0), vector_part(vectors, 1)))
    queries = low_back(low(matmul_hi(h_one, attn_w[0]) + vector_part(vectors, 6)))
    keys_own = low_back(low(matmul_hi(h_one, attn_w[1])))
    values_own = low_back(low(matmul_hi(h_one, attn_w[2]) + vector_part(vectors, 7)))
    attn_low = low_back(low(attend(queries, keys_own, values_own, vis_self)))
    res_one = tokens + low_back(matmul_hi(attn_low, attn_w[3])) + vector_part(vectors, 8)
    h_two = low(layer_norm(res_one, vector_part(vectors, 2), vector_part(vectors, 3)))
    cross_q = low_back(low(matmul_hi(h_two, attn_w[4]) + vector_part(vectors, 9)))
    mem_keys = low_back(low(matmul_hi(memory, attn_w[5])))
    mem_values = low_back(low(matmul_hi(memory, attn_w[6]) + vector_part(vectors, 10)))
    cross_low = low_back(low(attend(cross_q, mem_keys, mem_values, vis_cross)))
    res_two = res_one + low_back(matmul_hi(cross_low, attn_w[7])) + vector_part(vectors, 11)
    h_three = low(layer_norm(res_two, vector_part(vectors, 4), vector_part(vectors, 5)))
    pre_act = low_back(matmul_hi(h_three, w_in.T) + vectors[13 * D:])
    hidden = low(jnp.maximum(pre_act, 0.0))
    return res_two + matmul_hi(hidden, w_out) + vector_part(vectors, 12)

def forward(weights, vectors, tokens, memory, segments, padding, priority, threshold):
    blocks = TOKENS // KROWS

    def shaped(array):
        return array.reshape((blocks, KROWS) + array.shape[1:])

    def one_block(carry, pieces):
        return (carry, block_forward(weights, vectors, pieces[0], pieces[1], pieces[2], pieces[3], pieces[4], pieces[5]))
    carry_out, result = lax.scan(jax.checkpoint(one_block), jnp.zeros((), jnp.float32), (shaped(tokens), shaped(memory), shaped(segments), shaped(padding), shaped(priority), shaped(threshold)))
    return result.reshape(TOKENS, D)

def orthogonalize(matrix):
    current = matrix / (jnp.sqrt(jnp.sum(matrix * matrix)) + 1e-07)
    for turn in range(5):
        gram = lax.dot_general(current, current, (((0,), (0,)), ((), ())), precision=HIGH)
        poly = NS_B * gram + NS_C * matmul_hi(gram, gram)
        current = NS_A * current + matmul_hi(current, poly)
    return current

def reference(tokens, memory, cotangent, segments, padding, priority, threshold, master, momentum, vectors, vec_first, vec_second, step_count):

    def apply_layer(master_in, vectors_in, tokens_in, memory_in):
        return forward(low(master_in), vectors_in, tokens_in, memory_in, segments, padding, priority, threshold)
    result, pullback = jax.vjp(apply_layer, master, vectors, tokens.astype(jnp.float32), memory.astype(jnp.float32))
    grad_master, grad_vec, input_grad, memory_grad = pullback(cotangent.astype(jnp.float32))
    layer_out = result.astype(jnp.bfloat16)
    new_momentum = 0.5 * momentum + grad_master
    ranges = [(index_one * D, D) for index_one in range(8)] + [(8 * D, FF), (8 * D + FF, FF)]
    pieces = []
    for begin_row, row_count in ranges:
        ortho = orthogonalize(new_momentum[begin_row:begin_row + row_count])
        rate = MUON_RATE * max(1.0, row_count / D) ** 0.5
        pieces.append(master[begin_row:begin_row + row_count] - rate * ortho)
    new_master = jnp.concatenate(pieces, axis=0)
    count = step_count[0].astype(jnp.float32)
    new_first = 0.5 * vec_first + 0.5 * grad_vec
    new_second = 0.999 * vec_second + 0.001 * grad_vec * grad_vec
    first_fix = new_first / (1.0 - jnp.power(0.5, count))
    second_fix = new_second / (1.0 - jnp.power(0.999, count))
    new_vectors = vectors - ADAM_RATE * (first_fix / (jnp.sqrt(second_fix) + 1e-08) + ADAM_DECAY * vectors)
    return (layer_out, input_grad, memory_grad, new_momentum, new_master, new_vectors, new_first, new_second)
```

```python
import jax
import jax.numpy as jnp
from jax import lax
from jax.sharding import PartitionSpec as P

D = 512
HEADS = 8
HEAD = 64
FF = 2048


NS_A = 3.4445
NS_B = -4.775
NS_C = 2.0315
MUON_RATE = 0.8
ADAM_RATE = 0.2
ADAM_DECAY = 0.01
HIGH = lax.Precision.HIGHEST


def partner(block, axis, stride):
    count = lax.axis_size(axis)
    route = []
    for low in range(count):
        high = low | 1 << stride
        if high != low and high < count:
            route += [(low, high), (high, low)]
    return lax.ppermute(block, axis, route)


def plain_dot(left_mat, right_mat):
    return jnp.dot(left_mat, right_mat, preferred_element_type=jnp.float32)


def lead_dot(left_mat, right_mat):
    return lax.dot_general(
        left_mat, right_mat, (((0,), (0,)), ((), ())), preferred_element_type=jnp.float32
    )


def last_dot(left_mat, right_mat):
    return lax.dot_general(
        left_mat, right_mat, (((1,), (1,)), ((), ())), preferred_element_type=jnp.float32
    )


def high_dot(left_mat, right_mat):
    return jnp.dot(left_mat, right_mat, precision=lax.Precision.HIGH)


def exact_lead(left_mat, right_mat):
    return lax.dot_general(left_mat, right_mat, (((0,), (0,)), ((), ())), precision=HIGH)


def split_rows(all_rows):
    attn_w = all_rows[: 8 * D].reshape(8, D, D)
    return (attn_w, all_rows[8 * D : 8 * D + FF], all_rows[8 * D + FF :])


def norm_forward(values, gain_vec, shift_vec):
    center = values - jnp.mean(values, axis=-1, keepdims=True)
    spread = lax.rsqrt(jnp.mean(center * center, axis=-1, keepdims=True) + 1e-05)
    normed = center * spread
    return (normed * gain_vec + shift_vec, normed, spread)


def norm_backward(normed, spread, gain_vec, grad_out):
    grad_gain = jnp.sum(grad_out * normed, axis=0)
    grad_shift = jnp.sum(grad_out, axis=0)
    scaled = grad_out * gain_vec
    grad_in = spread * (
        scaled
        - jnp.mean(scaled, axis=-1, keepdims=True)
        - normed * jnp.mean(scaled * normed, axis=-1, keepdims=True)
    )
    return (grad_in, grad_gain, grad_shift)


def split_heads(matrix):
    return matrix.reshape(matrix.shape[0], HEADS, HEAD)


def block_scores(queries, keys_all, visible):
    scores = jnp.einsum(
        "qhe,khe->hqk",
        split_heads(queries),
        split_heads(keys_all),
        preferred_element_type=jnp.float32,
    )
    return jnp.where(visible[None], scores * HEAD ** (-0.5), -1e30)


def attend_forward(queries, keys_all, values_all, visible):
    scores = block_scores(queries, keys_all, visible)
    row_max = jnp.max(scores, axis=-1, keepdims=True)
    expo = jnp.exp(scores - row_max)
    row_total = jnp.sum(expo, axis=-1, keepdims=True)
    weights_low = (expo / row_total).astype(jnp.bfloat16)
    mixed = jnp.einsum(
        "hqk,khe->qhe", weights_low, split_heads(values_all), preferred_element_type=jnp.float32
    )
    return (mixed.reshape(queries.shape[0], HEADS * HEAD), row_max + jnp.log(row_total))


def attend_backward(queries, keys_all, values_all, visible, logsum, grad_out):
    probs = jnp.exp(block_scores(queries, keys_all, visible) - logsum)
    grad_heads = split_heads(grad_out)
    grad_probs = jnp.einsum(
        "qhe,khe->hqk", grad_heads, split_heads(values_all), preferred_element_type=jnp.float32
    )
    inner_sum = jnp.sum(grad_probs * probs, axis=-1, keepdims=True)
    grad_scores = (probs * (grad_probs - inner_sum) * HEAD ** (-0.5)).astype(jnp.bfloat16)
    grad_q = jnp.einsum(
        "hqk,khe->qhe", grad_scores, split_heads(keys_all), preferred_element_type=jnp.float32
    )
    grad_k = jnp.einsum(
        "hqk,qhe->khe", grad_scores, split_heads(queries), preferred_element_type=jnp.float32
    )
    grad_v = jnp.einsum(
        "hqk,qhe->khe", probs.astype(jnp.bfloat16), grad_heads, preferred_element_type=jnp.float32
    )
    key_count = keys_all.shape[0]
    return (
        grad_q.reshape(queries.shape[0], HEADS * HEAD),
        grad_k.reshape(key_count, HEADS * HEAD),
        grad_v.reshape(key_count, HEADS * HEAD),
    )


def attend_all(queries, keys_all, values_all, visible):
    mixed, logsum = attend_forward(queries, keys_all, values_all, visible)
    logsums = [logsum]
    return (mixed, logsums)


def attend_back_all(queries, keys_all, values_all, visible, logsums, grad_out):
    block_rows = min(512, queries.shape[0])
    grad_q_parts = []
    grad_keys = jnp.zeros(keys_all.shape, jnp.float32)
    grad_values = jnp.zeros(values_all.shape, jnp.float32)
    for block_index, begin_row in enumerate(range(0, queries.shape[0], block_rows)):
        grad_q, grad_k, grad_v = attend_backward(
            queries, keys_all, values_all, visible, logsums[block_index], grad_out
        )
        grad_q_parts.append(grad_q)
        grad_keys = grad_k
        grad_values = grad_v
    return (grad_q_parts[0], grad_keys, grad_values)


def per_device(
    tokens,
    memory,
    cotangent,
    segments,
    padding,
    priority,
    threshold,
    master,
    momentum,
    vectors,
    vec_first,
    vec_second,
    step_count,
):

    def vector_part(position):
        return vectors[position * D : (position + 1) * D]

    low_master = master.astype(jnp.bfloat16)
    attn_w, w_in, w_out = split_rows(
        lax.all_gather(low_master, ("dp", "stream"), axis=0, tiled=True)
    )
    tokens_f32 = tokens.astype(jnp.float32)
    ln_one, normed_one, spread_one = norm_forward(tokens_f32, vector_part(0), vector_part(1))
    h_one = ln_one.astype(jnp.bfloat16)
    queries = (plain_dot(h_one, attn_w[0]) + vector_part(6)).astype(jnp.bfloat16)
    keys_own = plain_dot(h_one, attn_w[1]).astype(jnp.bfloat16)
    values_own = (plain_dot(h_one, attn_w[2]) + vector_part(7)).astype(jnp.bfloat16)
    mem_keys = plain_dot(memory, attn_w[5]).astype(jnp.bfloat16)
    mem_values = (plain_dot(memory, attn_w[6]) + vector_part(10)).astype(jnp.bfloat16)
    keys_all, values_all, mem_keys_all, mem_values_all = (
        lax.all_gather(keys_own, "stream", axis=0, tiled=True),
        lax.all_gather(values_own, "stream", axis=0, tiled=True),
        lax.all_gather(mem_keys, "stream", axis=0, tiled=True),
        lax.all_gather(mem_values, "stream", axis=0, tiled=True),
    )
    seg_all, pad_all, prio_all = (
        lax.all_gather(segments, "stream", axis=0, tiled=True),
        lax.all_gather(padding, "stream", axis=0, tiled=True),
        lax.all_gather(priority, "stream", axis=0, tiled=True),
    )
    own_rows = queries.shape[0]
    place = jnp.arange(own_rows, dtype=jnp.int32) + lax.axis_index("stream") * own_rows
    key_place = jnp.arange(seg_all.shape[0], dtype=jnp.int32)
    diagonal = place[:, None] == key_place[None, :]
    same_seg = segments[:, None] == seg_all[None, :]
    open_key = (pad_all == 0)[None, :]
    vis_self = same_seg & ((prio_all[None, :] < threshold[:, None]) & open_key | diagonal)
    vis_cross = same_seg & (open_key | diagonal)
    attn_out, lse_one = attend_all(queries, keys_all, values_all, vis_self)
    attn_low = attn_out.astype(jnp.bfloat16)
    res_one = tokens_f32 + plain_dot(attn_low, attn_w[3]) + vector_part(8)
    ln_two, normed_two, spread_two = norm_forward(res_one, vector_part(2), vector_part(3))
    h_two = ln_two.astype(jnp.bfloat16)
    cross_q = (plain_dot(h_two, attn_w[4]) + vector_part(9)).astype(jnp.bfloat16)
    cross_out, lse_two = attend_all(cross_q, mem_keys_all, mem_values_all, vis_cross)
    cross_low = cross_out.astype(jnp.bfloat16)
    res_two = res_one + plain_dot(cross_low, attn_w[7]) + vector_part(11)
    ln_three, normed_three, spread_three = norm_forward(res_two, vector_part(4), vector_part(5))
    h_three = ln_three.astype(jnp.bfloat16)
    pre_act = last_dot(h_three, w_in) + vectors[13 * D :]
    hidden = jnp.maximum(pre_act, 0.0).astype(jnp.bfloat16)
    layer_out = (res_two + plain_dot(hidden, w_out) + vector_part(12)).astype(jnp.bfloat16)
    grad_out_w = lead_dot(hidden, cotangent)
    grad_bias_out = jnp.sum(cotangent.astype(jnp.float32), axis=0)
    grad_hidden = last_dot(cotangent, w_out)
    grad_pre = jnp.where(pre_act > 0, grad_hidden, 0.0).astype(jnp.bfloat16)
    grad_bias_hidden = jnp.sum(grad_pre.astype(jnp.float32), axis=0)
    grad_in_w = lead_dot(grad_pre, h_three)
    grad_ln_three, grad_gain_three, grad_shift_three = norm_backward(
        normed_three, spread_three, vector_part(4), plain_dot(grad_pre, w_in)
    )
    grad_res_two = cotangent.astype(jnp.float32) + grad_ln_three
    grad_res_two_low = grad_res_two.astype(jnp.bfloat16)
    grad_bias_cross_o = jnp.sum(grad_res_two, axis=0)
    grad_cross_o_w = lead_dot(cross_low, grad_res_two_low)
    grad_cross = last_dot(grad_res_two_low, attn_w[7]).astype(jnp.bfloat16)
    grad_cq, grad_mk_all, grad_mv_all = attend_back_all(
        cross_q, mem_keys_all, mem_values_all, vis_cross, lse_two, grad_cross
    )
    grad_cq_low = grad_cq.astype(jnp.bfloat16)
    grad_bias_cq = jnp.sum(grad_cq_low.astype(jnp.float32), axis=0)
    grad_cq_w = lead_dot(h_two, grad_cq_low)
    grad_ln_two, grad_gain_two, grad_shift_two = norm_backward(
        normed_two, spread_two, vector_part(2), last_dot(grad_cq_low, attn_w[4])
    )
    grad_res_one = grad_res_two + grad_ln_two
    grad_res_one_low = grad_res_one.astype(jnp.bfloat16)
    grad_bias_o = jnp.sum(grad_res_one, axis=0)
    grad_o_w = lead_dot(attn_low, grad_res_one_low)
    grad_attn = last_dot(grad_res_one_low, attn_w[3]).astype(jnp.bfloat16)
    grad_q, grad_k_all, grad_v_all = attend_back_all(
        queries, keys_all, values_all, vis_self, lse_one, grad_attn
    )
    grad_k, grad_v, grad_mk, grad_mv = (
        lax.psum_scatter(grad_k_all, "stream", scatter_dimension=0, tiled=True),
        lax.psum_scatter(grad_v_all, "stream", scatter_dimension=0, tiled=True),
        lax.psum_scatter(grad_mk_all, "stream", scatter_dimension=0, tiled=True),
        lax.psum_scatter(grad_mv_all, "stream", scatter_dimension=0, tiled=True),
    )
    grad_q_low = grad_q.astype(jnp.bfloat16)
    grad_k_low = grad_k.astype(jnp.bfloat16)
    grad_v_low = grad_v.astype(jnp.bfloat16)
    grad_mk_low = grad_mk.astype(jnp.bfloat16)
    grad_mv_low = grad_mv.astype(jnp.bfloat16)
    grad_h_one = (
        last_dot(grad_q_low, attn_w[0])
        + last_dot(grad_k_low, attn_w[1])
        + last_dot(grad_v_low, attn_w[2])
    )
    grad_ln_one, grad_gain_one, grad_shift_one = norm_backward(
        normed_one, spread_one, vector_part(0), grad_h_one
    )
    input_grad = grad_res_one + grad_ln_one
    memory_grad = last_dot(grad_mk_low, attn_w[5]) + last_dot(grad_mv_low, attn_w[6])
    stacked = jnp.concatenate(
        [
            lead_dot(h_one, grad_q_low),
            lead_dot(h_one, grad_k_low),
            lead_dot(h_one, grad_v_low),
            grad_o_w,
            grad_cq_w,
            lead_dot(memory, grad_mk_low),
            lead_dot(memory, grad_mv_low),
            grad_cross_o_w,
            grad_in_w,
            grad_out_w,
        ],
        axis=0,
    )
    vec_local = jnp.concatenate(
        [
            grad_gain_one,
            grad_shift_one,
            grad_gain_two,
            grad_shift_two,
            grad_gain_three,
            grad_shift_three,
            jnp.sum(grad_q_low.astype(jnp.float32), axis=0),
            jnp.sum(grad_v_low.astype(jnp.float32), axis=0),
            grad_bias_o,
            grad_bias_cq,
            jnp.sum(grad_mv_low.astype(jnp.float32), axis=0),
            grad_bias_cross_o,
            grad_bias_out,
            grad_bias_hidden,
        ],
        axis=0,
    )
    grad_rows = lax.psum_scatter(stacked, ("dp", "stream"), scatter_dimension=0, tiled=True)
    grad_vec = lax.psum(vec_local, ("dp", "stream"))
    opt_rows = master.shape[0]
    device_index = lax.axis_index(("dp", "stream"))
    start_row = device_index * opt_rows
    in_ffn = start_row >= 8 * D
    att_bits = (D // opt_rows).bit_length() - 1
    ffn_bits = (FF // opt_rows).bit_length() - 1
    own_bits = jnp.where(in_ffn, ffn_bits, att_bits)
    new_momentum = 0.5 * momentum + grad_rows

    def gram_total(partial_value):
        for bit_pos in range(ffn_bits):
            other = partner(partial_value, ("dp", "stream"), bit_pos)
            partial_value = partial_value + jnp.where(bit_pos < own_bits, other, 0.0)
        return partial_value

    gram_first = gram_total(exact_lead(new_momentum, new_momentum))
    divisor = jnp.sqrt(jnp.trace(gram_first)) + 1e-07
    gram = gram_first / (divisor * divisor)
    unit = jnp.eye(D, dtype=jnp.float32)
    chain = None
    for turn in range(5):
        poly = NS_A * unit + NS_B * gram + NS_C * high_dot(gram, gram)
        chain = poly if chain is None else high_dot(chain, poly)
        if turn < 4:
            gram = high_dot(high_dot(gram, poly), poly)
    current = high_dot(new_momentum / divisor, chain)
    rate = MUON_RATE * jnp.where(in_ffn, (FF / D) ** 0.5, 1.0)
    new_master = master - rate * current
    count = step_count[0].astype(jnp.float32)
    new_first = 0.5 * vec_first + 0.5 * grad_vec
    new_second = 0.999 * vec_second + 0.001 * grad_vec * grad_vec
    first_fix = new_first / (1.0 - jnp.power(0.5, count))
    second_fix = new_second / (1.0 - jnp.power(0.999, count))
    new_vectors = vectors - ADAM_RATE * (
        first_fix / (jnp.sqrt(second_fix) + 1e-08) + ADAM_DECAY * vectors
    )
    return (
        layer_out,
        input_grad,
        memory_grad,
        new_momentum,
        new_master,
        new_vectors,
        new_first,
        new_second,
    )


def solution(mesh):
    return jax.shard_map(
        per_device,
        mesh=mesh,
        in_specs=(
            P(("dp", "stream"), None),
            P(("dp", "stream"), None),
            P(("dp", "stream"), None),
            P(("dp", "stream")),
            P(("dp", "stream")),
            P(("dp", "stream")),
            P(("dp", "stream")),
            P(("dp", "stream"), None),
            P(("dp", "stream"), None),
            P(),
            P(),
            P(),
            P(),
        ),
        out_specs=(
            P(("dp", "stream"), None),
            P(("dp", "stream"), None),
            P(("dp", "stream"), None),
            P(("dp", "stream"), None),
            P(("dp", "stream"), None),
            P(),
            P(),
            P(),
        ),
        check_vma=False,
    )
```

```python
import functools

import jax
import jax.numpy as jnp
from jax import lax
from jax.experimental import pallas as pl
from jax.experimental.pallas import tpu as pltpu
from jax.sharding import PartitionSpec as P

D = 512
HEADS = 8
HEAD = 64
FF = 2048
ROWS = 512
KEYS = 1024
CHUNK = 256
BF = jnp.bfloat16
F32 = jnp.float32
SCALE = HEAD ** (-0.5)
LOG2E = 1.4426950408889634
MESH = pl.DeviceIdType.MESH

NS_A = 3.4445
NS_B = -4.775
NS_C = 2.0315
MUON_RATE = 0.8
ADAM_RATE = 0.2
ADAM_DECAY = 0.01
HIGH = lax.Precision.HIGHEST


def nn(left_mat, right_mat):
    return lax.dot_general(
        left_mat, right_mat, (((1,), (0,)), ((), ())), preferred_element_type=F32
    )


def nt(left_mat, right_mat):
    return lax.dot_general(
        left_mat, right_mat, (((1,), (1,)), ((), ())), preferred_element_type=F32
    )


def tn(left_mat, right_mat):
    return lax.dot_general(
        left_mat, right_mat, (((0,), (0,)), ((), ())), preferred_element_type=F32
    )


def norm_forward(values, gain_vec, shift_vec):
    center = values - jnp.mean(values, axis=-1, keepdims=True)
    spread = lax.rsqrt(jnp.mean(center * center, axis=-1, keepdims=True) + 1e-05)
    normed = center * spread
    return normed * gain_vec + shift_vec, normed, spread


def norm_backward(normed, spread, gain_vec, grad_out):
    grad_gain = jnp.sum(grad_out * normed, axis=0, keepdims=True)
    grad_shift = jnp.sum(grad_out, axis=0, keepdims=True)
    scaled = grad_out * gain_vec
    grad_in = spread * (
        scaled
        - jnp.mean(scaled, axis=-1, keepdims=True)
        - normed * jnp.mean(scaled * normed, axis=-1, keepdims=True)
    )
    return grad_in, grad_gain, grad_shift


def column_sum(values):
    return jnp.sum(values.astype(F32), axis=0, keepdims=True)


def half_lanes(values, sub):
    lane = lax.broadcasted_iota(jnp.int32, values.shape, 1)
    keep = lane < HEAD if sub == 0 else lane >= HEAD
    return jnp.where(keep, values, jnp.zeros_like(values))


def attend_forward(q_ref, k_ref, value_t, bias, probs, mixed_t):
    def pair_body(pair, carry):
        lanes = pl.ds(pl.multiple_of(pair * 128, 128), 128)
        keys = k_ref[:, lanes]
        for sub in range(2):
            head_rows = pl.ds(pl.multiple_of(pair * 128 + sub * HEAD, HEAD), HEAD)
            for begin in range(0, ROWS, CHUNK):
                cols = slice(begin, begin + CHUNK)
                scores = nt(keys, half_lanes(q_ref[cols, lanes], sub))
                scores = scores * (SCALE * LOG2E) + bias[:, cols]
                expo = jnp.exp2(scores - jnp.max(scores, axis=0, keepdims=True))
                total = jnp.sum(expo, axis=0, keepdims=True)
                low = (expo * (1.0 / total)).astype(BF)
                probs[pair * 2 + sub, :, cols] = low
                mixed_t[head_rows, cols] = nn(value_t[head_rows, :], low).astype(BF)
        return carry

    lax.fori_loop(0, HEADS // 2, pair_body, 0)


def attend_backward(q_ref, k_t, v_ref, grad_t, mixed_t, probs, dq_t, dk_ref, dv_ref):
    def pair_body(pair, carry):
        lanes = pl.ds(pl.multiple_of(pair * 128, 128), 128)
        values = v_ref[:, lanes]
        sum_k = None
        sum_v = None
        for sub in range(2):
            head_rows = pl.ds(pl.multiple_of(pair * 128 + sub * HEAD, HEAD), HEAD)
            for begin in range(0, ROWS, CHUNK):
                cols = slice(begin, begin + CHUNK)
                grad = grad_t[head_rows, cols]
                inner = jnp.sum(
                    grad.astype(F32) * mixed_t[head_rows, cols].astype(F32), axis=0, keepdims=True
                )
                zero = jnp.zeros_like(grad)
                grad_pair = jnp.concatenate([grad, zero] if sub == 0 else [zero, grad], axis=0)
                grad_probs = nn(values, grad_pair)
                low = probs[pair * 2 + sub, :, cols]
                grad_scores = (low.astype(F32) * (grad_probs - inner)).astype(BF)
                dq_t[head_rows, cols] = (nn(k_t[head_rows, :], grad_scores) * SCALE).astype(BF)
                part_k = nn(grad_scores, half_lanes(q_ref[cols, lanes], sub))
                part_v = nn(low, grad_pair.T)
                sum_k = part_k if sum_k is None else sum_k + part_k
                sum_v = part_v if sum_v is None else sum_v + part_v
        dk_ref[:, lanes] = (sum_k * SCALE).astype(dk_ref.dtype)
        dv_ref[:, lanes] = sum_v.astype(dv_ref.dtype)
        return carry

    lax.fori_loop(0, HEADS // 2, pair_body, 0)


def layer_kernel(
    tok, mem, cot, meta, vec, w,
    out_ref, igrad_ref, mgrad_ref, g_ref, gv_ref,
    keys, metas, bias, probs_s, probs_c, flip, q_ref, cq_ref, attn_t, cross_t, grad_t, dq_t,
    parts, arrived, res_a, res_b, res_c,
    send_sem, recv_sem, meta_sem,
):
    core = lax.axis_index("stream")
    other = 1 - core
    own = pl.ds(pl.multiple_of(core * ROWS, ROWS), ROWS)
    theirs = pl.ds(pl.multiple_of(other * ROWS, ROWS), ROWS)

    def swap(src, dst, index, sems=(send_sem, recv_sem)):
        return pltpu.make_async_remote_copy(
            src_ref=src, dst_ref=dst, send_sem=sems[0].at[index], recv_sem=sems[1].at[index],
            device_id={"stream": other}, device_id_type=MESH,
        )

    barrier = pltpu.get_barrier_semaphore()
    pl.semaphore_signal(barrier, inc=1, device_id={"stream": other}, device_id_type=MESH)
    pl.semaphore_wait(barrier, 1)

    def weight(index):
        return w[index * D : (index + 1) * D, :]

    def vector(index):
        return vec[index : index + 1, :]

    def wide(index):
        return slice(index * D, (index + 1) * D)

    meta_copy = pltpu.make_async_remote_copy(
        src_ref=meta, dst_ref=metas, send_sem=meta_sem.at[0], recv_sem=meta_sem.at[1],
        device_id={"stream": other}, device_id_type=MESH,
    )
    meta_copy.start()
    hid, _, _ = norm_forward(tok[...].astype(F32), vector(0), vector(1))
    hid = hid.astype(BF)
    keys[0, own, :] = nn(hid, weight(1)).astype(BF)
    copies = []
    for index in range(4):
        copies.append(swap(keys.at[index, own, :], keys.at[index, own, :], index))
    copies[0].start()
    keys[1, own, :] = (nn(hid, weight(2)) + vector(7)).astype(BF)
    copies[1].start()
    q_ref[...] = (nn(hid, weight(0)) + vector(6)).astype(BF)
    keys[2, own, :] = nn(mem[...], weight(5)).astype(BF)
    copies[2].start()
    keys[3, own, :] = (nn(mem[...], weight(6)) + vector(10)).astype(BF)
    copies[3].start()

    meta_copy.wait()
    row = lax.broadcasted_iota(jnp.int32, (ROWS, ROWS), 0)
    col = lax.broadcasted_iota(jnp.int32, (ROWS, ROWS), 1)

    def fill_bias(with_priority):
        for rows, source, own_half in ((own, meta, True), (theirs, metas, False)):
            turned = source[...].T
            visible = turned[:, 0:1] == meta[2:3, :]
            if with_priority:
                visible = visible & (turned[:, 1:2] < meta[3:4, :])
            if own_half:
                visible = visible | (row == col)
            bias[rows, :] = jnp.where(visible, 0.0, -1e30)

    fill_bias(True)
    copies[0].wait()
    copies[1].wait()
    flip[...] = keys[1].T
    attend_forward(q_ref, keys.at[0], flip, bias, probs_s, attn_t)
    res_one = tok[...].astype(F32) + nn(attn_t[...].T, weight(3)) + vector(8)
    res_a[...] = res_one
    hid, _, _ = norm_forward(res_one, vector(2), vector(3))
    cq_ref[...] = (nn(hid.astype(BF), weight(4)) + vector(9)).astype(BF)
    fill_bias(False)
    copies[2].wait()
    copies[3].wait()
    flip[...] = keys[3].T
    attend_forward(cq_ref, keys.at[2], flip, bias, probs_c, cross_t)
    res_two = res_a[...] + nn(cross_t[...].T, weight(7)) + vector(11)
    res_b[...] = res_two
    hid, _, _ = norm_forward(res_two, vector(4), vector(5))
    grad_t[...] = hid.astype(BF)
    res_c[...] = jnp.zeros((ROWS, D), F32)
    out_sum = res_two + vector(12)
    igrad_ref[...] = out_sum
    gv_ref[12:13, :] = column_sum(cot[...])

    def ffn_body(part, carry):
        rows_in = pl.ds(pl.multiple_of(8 * D + part * D, D), D)
        rows_out = pl.ds(pl.multiple_of(8 * D + FF + part * D, D), D)
        w_in = w[rows_in, :]
        w_out = w[rows_out, :]
        h_three = grad_t[...]
        pre = nt(h_three, w_in) + vec[pl.ds(13 + part, 1), :]
        hidden = jnp.maximum(pre, 0.0).astype(BF)
        igrad_ref[...] += nn(hidden, w_out)
        grad_pre = jnp.where(pre > 0, nt(cot[...], w_out), 0.0).astype(BF)
        res_c[...] += nn(grad_pre, w_in)
        gv_ref[pl.ds(13 + part, 1), :] = column_sum(grad_pre)
        g_ref[rows_in, :] = tn(grad_pre, h_three).astype(BF)
        g_ref[rows_out, :] = tn(hidden, cot[...]).astype(BF)
        return carry

    lax.fori_loop(0, FF // D, ffn_body, 0)
    out_ref[...] = igrad_ref[...].astype(BF)

    _, normed, spread = norm_forward(res_b[...], vector(4), vector(5))
    grad_in, gv_ref[4:5, :], gv_ref[5:6, :] = norm_backward(normed, spread, vector(4), res_c[...])
    grad_res = cot[...].astype(F32) + grad_in
    res_b[...] = grad_res
    gv_ref[11:12, :] = column_sum(grad_res)
    grad_low = grad_res.astype(BF)
    g_ref[wide(7), :] = nn(cross_t[...], grad_low).astype(BF)
    grad_t[...] = nt(weight(7), grad_low).astype(BF)
    flip[...] = keys[2].T
    attend_backward(
        cq_ref, flip, keys.at[3], grad_t, cross_t, probs_c, dq_t, parts.at[2], parts.at[3]
    )
    back = [swap(parts.at[index, theirs, :], arrived.at[index], 4 + index) for index in range(4)]
    back[2].start()
    back[3].start()
    grad_cq = dq_t[...].T
    gv_ref[9:10, :] = column_sum(grad_cq)
    hid, normed, spread = norm_forward(res_a[...], vector(2), vector(3))
    g_ref[wide(4), :] = tn(hid.astype(BF), grad_cq).astype(BF)
    grad_in, gv_ref[2:3, :], gv_ref[3:4, :] = norm_backward(
        normed, spread, vector(2), nt(grad_cq, weight(4))
    )
    grad_res = res_b[...] + grad_in
    res_b[...] = grad_res
    gv_ref[8:9, :] = column_sum(grad_res)
    grad_low = grad_res.astype(BF)
    g_ref[wide(3), :] = nn(attn_t[...], grad_low).astype(BF)
    grad_t[...] = nt(weight(3), grad_low).astype(BF)
    flip[...] = keys[0].T
    attend_backward(
        q_ref, flip, keys.at[1], grad_t, attn_t, probs_s, dq_t, parts.at[0], parts.at[1]
    )
    back[0].start()
    back[1].start()

    def summed(index):
        back[index].wait()
        return (parts[index, own, :].astype(F32) + arrived[index].astype(F32)).astype(BF)

    grad_mk = summed(2)
    grad_mv = summed(3)
    gv_ref[10:11, :] = column_sum(grad_mv)
    mgrad_ref[...] = nt(grad_mk, weight(5)) + nt(grad_mv, weight(6))
    g_ref[wide(5), :] = tn(mem[...], grad_mk).astype(BF)
    g_ref[wide(6), :] = tn(mem[...], grad_mv).astype(BF)
    hid, normed, spread = norm_forward(tok[...].astype(F32), vector(0), vector(1))
    hid = hid.astype(BF)
    grad_q = dq_t[...].T
    gv_ref[6:7, :] = column_sum(grad_q)
    g_ref[wide(0), :] = tn(hid, grad_q).astype(BF)
    grad_h = nt(grad_q, weight(0))
    grad_k = summed(0)
    g_ref[wide(1), :] = tn(hid, grad_k).astype(BF)
    grad_h = grad_h + nt(grad_k, weight(1))
    grad_v = summed(1)
    gv_ref[7:8, :] = column_sum(grad_v)
    g_ref[wide(2), :] = tn(hid, grad_v).astype(BF)
    grad_h = grad_h + nt(grad_v, weight(2))
    grad_in, gv_ref[0:1, :], gv_ref[1:2, :] = norm_backward(normed, spread, vector(0), grad_h)
    igrad_ref[...] = res_b[...] + grad_in


def layer_call(tok, mem, cot, meta, vec, w):
    shape = jax.ShapeDtypeStruct
    vmem = pl.BlockSpec(memory_space=pltpu.VMEM)
    return pl.pallas_call(
        layer_kernel,
        out_shape=[
            shape((ROWS, D), BF), shape((ROWS, D), F32), shape((ROWS, D), F32),
            shape(w.shape, BF), shape(vec.shape, F32),
        ],
        in_specs=[vmem] * 6,
        out_specs=[vmem] * 5,
        scratch_shapes=[
            pltpu.VMEM((4, KEYS, D), BF),
            pltpu.VMEM((8, ROWS), jnp.int32),
            pltpu.VMEM((KEYS, ROWS), F32),
            pltpu.VMEM((HEADS, KEYS, ROWS), BF),
            pltpu.VMEM((HEADS, KEYS, ROWS), BF),
            pltpu.VMEM((D, KEYS), BF),
            pltpu.VMEM((ROWS, D), BF),
            pltpu.VMEM((ROWS, D), BF),
            pltpu.VMEM((D, ROWS), BF),
            pltpu.VMEM((D, ROWS), BF),
            pltpu.VMEM((D, ROWS), BF),
            pltpu.VMEM((D, ROWS), BF),
            pltpu.VMEM((4, KEYS, D), BF),
            pltpu.VMEM((4, ROWS, D), BF),
            pltpu.VMEM((ROWS, D), F32),
            pltpu.VMEM((ROWS, D), F32),
            pltpu.VMEM((ROWS, D), F32),
            pltpu.SemaphoreType.DMA((8,)),
            pltpu.SemaphoreType.DMA((8,)),
            pltpu.SemaphoreType.DMA((2,)),
        ],
        compiler_params=pltpu.CompilerParams(
            collective_id=0, has_side_effects=True, vmem_limit_bytes=63 * 1024 * 1024
        ),
        cost_estimate=pl.CostEstimate(
            flops=22_000_000_000, bytes_accessed=24_000_000, transcendentals=8_000_000
        ),
    )(tok, mem, cot, meta, vec, w)


def partner(block, axis, stride):
    count = lax.axis_size(axis)
    route = []
    for low in range(count):
        high = low | 1 << stride
        if high != low and high < count:
            route += [(low, high), (high, low)]
    return lax.ppermute(block, axis, route)


def high_dot(left_mat, right_mat):
    return jnp.dot(left_mat, right_mat, precision=lax.Precision.HIGH)


def exact_lead(left_mat, right_mat):
    return lax.dot_general(left_mat, right_mat, (((0,), (0,)), ((), ())), precision=HIGH)


def per_device(
    tokens,
    memory,
    cotangent,
    segments,
    padding,
    priority,
    threshold,
    master,
    momentum,
    vectors,
    vec_first,
    vec_second,
    step_count,
):
    low_all = lax.all_gather(master.astype(BF), ("dp", "stream"), axis=0, tiled=True)
    meta = jnp.stack([jnp.where(padding == 0, segments, -1), priority, segments, threshold] * 2)
    layer_out, input_grad, memory_grad, grad_all, vec_local = layer_call(
        tokens, memory, cotangent, meta, vectors.reshape(-1, D), low_all
    )
    grad_rows = lax.psum_scatter(
        grad_all, ("dp", "stream"), scatter_dimension=0, tiled=True
    ).astype(F32)
    grad_vec = lax.psum(vec_local.reshape(-1), ("dp", "stream"))
    opt_rows = master.shape[0]
    device_index = lax.axis_index(("dp", "stream"))
    start_row = device_index * opt_rows
    in_ffn = start_row >= 8 * D
    att_bits = (D // opt_rows).bit_length() - 1
    ffn_bits = (FF // opt_rows).bit_length() - 1
    own_bits = jnp.where(in_ffn, ffn_bits, att_bits)
    new_momentum = 0.5 * momentum + grad_rows

    def gram_total(partial_value):
        for bit_pos in range(ffn_bits):
            other = partner(partial_value, ("dp", "stream"), bit_pos)
            partial_value = partial_value + jnp.where(bit_pos < own_bits, other, 0.0)
        return partial_value

    gram_first = gram_total(exact_lead(new_momentum, new_momentum))
    divisor = jnp.sqrt(jnp.trace(gram_first)) + 1e-07
    gram = gram_first / (divisor * divisor)
    unit = jnp.eye(D, dtype=jnp.float32)
    chain = None
    for turn in range(5):
        poly = NS_A * unit + NS_B * gram + NS_C * high_dot(gram, gram)
        chain = poly if chain is None else high_dot(chain, poly)
        if turn < 4:
            gram = high_dot(high_dot(gram, poly), poly)
    current = high_dot(new_momentum / divisor, chain)
    rate = MUON_RATE * jnp.where(in_ffn, (FF / D) ** 0.5, 1.0)
    new_master = master - rate * current
    count = step_count[0].astype(jnp.float32)
    new_first = 0.5 * vec_first + 0.5 * grad_vec
    new_second = 0.999 * vec_second + 0.001 * grad_vec * grad_vec
    first_fix = new_first / (1.0 - jnp.power(0.5, count))
    second_fix = new_second / (1.0 - jnp.power(0.999, count))
    new_vectors = vectors - ADAM_RATE * (
        first_fix / (jnp.sqrt(second_fix) + 1e-08) + ADAM_DECAY * vectors
    )
    return (
        layer_out,
        input_grad,
        memory_grad,
        new_momentum,
        new_master,
        new_vectors,
        new_first,
        new_second,
    )


def solution(mesh):
    return jax.shard_map(
        per_device,
        mesh=mesh,
        in_specs=(
            P(("dp", "stream"), None),
            P(("dp", "stream"), None),
            P(("dp", "stream"), None),
            P(("dp", "stream")),
            P(("dp", "stream")),
            P(("dp", "stream")),
            P(("dp", "stream")),
            P(("dp", "stream"), None),
            P(("dp", "stream"), None),
            P(),
            P(),
            P(),
            P(),
        ),
        out_specs=(
            P(("dp", "stream"), None),
            P(("dp", "stream"), None),
            P(("dp", "stream"), None),
            P(("dp", "stream"), None),
            P(("dp", "stream"), None),
            P(),
            P(),
            P(),
        ),
        check_vma=False,
    )
```

```python
import functools

import jax
import jax.numpy as jnp
from jax import lax
from jax.experimental import pallas as pl
from jax.experimental.pallas import tpu as pltpu
from jax.sharding import PartitionSpec as P

D = 512
HEADS = 8
HEAD = 64
FF = 2048
ROWS = 512
KEYS = 1024
CHUNK = 256
HALF = 256
BF = jnp.bfloat16
F32 = jnp.float32
SCALE = HEAD ** (-0.5)
LOG2E = 1.4426950408889634
MESH = pl.DeviceIdType.MESH

NS_A = 3.4445
NS_B = -4.775
NS_C = 2.0315
MUON_RATE = 0.8
ADAM_RATE = 0.2
ADAM_DECAY = 0.01
HIGH = lax.Precision.HIGHEST


def nn(left_mat, right_mat):
    return lax.dot_general(
        left_mat, right_mat, (((1,), (0,)), ((), ())), preferred_element_type=F32
    )


def nt(left_mat, right_mat):
    return lax.dot_general(
        left_mat, right_mat, (((1,), (1,)), ((), ())), preferred_element_type=F32
    )


def tn(left_mat, right_mat):
    return lax.dot_general(
        left_mat, right_mat, (((0,), (0,)), ((), ())), preferred_element_type=F32
    )


def norm_forward(values, gain_vec, shift_vec):
    center = values - jnp.mean(values, axis=-1, keepdims=True)
    spread = lax.rsqrt(jnp.mean(center * center, axis=-1, keepdims=True) + 1e-05)
    normed = center * spread
    return normed * gain_vec + shift_vec, normed, spread


def norm_backward(normed, spread, gain_vec, grad_out):
    grad_gain = jnp.sum(grad_out * normed, axis=0, keepdims=True)
    grad_shift = jnp.sum(grad_out, axis=0, keepdims=True)
    scaled = grad_out * gain_vec
    grad_in = spread * (
        scaled
        - jnp.mean(scaled, axis=-1, keepdims=True)
        - normed * jnp.mean(scaled * normed, axis=-1, keepdims=True)
    )
    return grad_in, grad_gain, grad_shift


def column_sum(values):
    return jnp.sum(values.astype(F32), axis=0, keepdims=True)


def half_lanes(values, sub):
    lane = lax.broadcasted_iota(jnp.int32, values.shape, 1)
    keep = lane < HEAD if sub == 0 else lane >= HEAD
    return jnp.where(keep, values, jnp.zeros_like(values))


def head_keys(head):
    return pl.ds(pl.multiple_of(head * KEYS, KEYS), KEYS)


def attend_forward(q_ref, k_ref, value_t, bias, probs, mixed_t, pairs):
    def pair_body(pair, carry):
        lanes = pl.ds(pl.multiple_of(pair * 128, 128), 128)
        keys = k_ref[:, lanes]
        for sub in range(2):
            head_rows = pl.ds(pl.multiple_of(pair * 128 + sub * HEAD, HEAD), HEAD)
            for begin in range(0, ROWS, CHUNK):
                cols = slice(begin, begin + CHUNK)
                scores = nt(keys, half_lanes(q_ref[cols, lanes], sub))
                scores = scores * (SCALE * LOG2E) + bias[:, cols]
                expo = jnp.exp2(scores - jnp.max(scores, axis=0, keepdims=True))
                total = jnp.sum(expo, axis=0, keepdims=True)
                low = (expo * (1.0 / total)).astype(BF)
                probs[head_keys(pair * 2 + sub), cols] = low
                mixed_t[head_rows, cols] = nn(value_t[head_rows, :], low).astype(BF)
        return carry

    lax.fori_loop(pairs[0], pairs[1], pair_body, 0)


def attend_backward(q_ref, k_t, v_ref, grad_t, mixed_t, probs, dq_t, dk_ref, dv_ref, pairs):
    def pair_body(pair, carry):
        lanes = pl.ds(pl.multiple_of(pair * 128, 128), 128)
        values = v_ref[:, lanes]
        sum_k = None
        sum_v = None
        for sub in range(2):
            head_rows = pl.ds(pl.multiple_of(pair * 128 + sub * HEAD, HEAD), HEAD)
            for begin in range(0, ROWS, CHUNK):
                cols = slice(begin, begin + CHUNK)
                grad = grad_t[head_rows, cols]
                inner = jnp.sum(
                    grad.astype(F32) * mixed_t[head_rows, cols].astype(F32), axis=0, keepdims=True
                )
                zero = jnp.zeros_like(grad)
                grad_pair = jnp.concatenate([grad, zero] if sub == 0 else [zero, grad], axis=0)
                grad_probs = nn(values, grad_pair)
                low = probs[head_keys(pair * 2 + sub), cols]
                grad_scores = (low.astype(F32) * (grad_probs - inner)).astype(BF)
                dq_t[head_rows, cols] = (nn(k_t[head_rows, :], grad_scores) * SCALE).astype(BF)
                part_k = nn(grad_scores, half_lanes(q_ref[cols, lanes], sub))
                part_v = nn(low, grad_pair.T)
                sum_k = part_k if sum_k is None else sum_k + part_k
                sum_v = part_v if sum_v is None else sum_v + part_v
        dk_ref[:, lanes] = (sum_k * SCALE).astype(dk_ref.dtype)
        dv_ref[:, lanes] = sum_v.astype(dv_ref.dtype)
        return carry

    lax.fori_loop(pairs[0], pairs[1], pair_body, 0)


class Board:
    def __init__(self):
        self.dp = lax.axis_index("dp")
        self.core = lax.axis_index("stream")
        self.z = self.dp // 4
        self.place = self.dp % 4
        x = self.place % 2
        y = self.place // 2
        side_x = self.place + 1 - 2 * x
        side_y = self.place + 2 - 4 * y
        self.places = (self.place, side_x, side_y, 3 - self.place)

    def chip(self, plane, place):
        return {"dp": plane * 4 + place, "stream": self.core}

    def across(self):
        return {"dp": self.dp, "stream": 1 - self.core}

    def half_rows(self, block, core=None, begin=0, count=HALF):
        core = self.core if core is None else core
        return pl.ds(pl.multiple_of(block * D + core * HALF + begin, 128), count)


def remote(src, dst, send, recv, device):
    return pltpu.make_async_remote_copy(
        src_ref=src, dst_ref=dst, send_sem=send, recv_sem=recv,
        device_id=device, device_id_type=MESH,
    )


class Gather:
    def __init__(self, board, w, line_s, line_r, far_s, far_r, plane_s, plane_r, core_s, core_r):
        self.board = board
        self.w = w
        self.line = (line_s, line_r)
        self.far = (far_s, far_r)
        self.plane = (plane_s, plane_r)
        self.core = (core_s, core_r)

    def copy(self, rows, sems, send, recv, device):
        view = self.w.at[rows, :]
        return remote(view, view, sems[0].at[send], sems[1].at[recv], device)

    def line_copy(self, part):
        b = self.board
        rows = b.half_rows(b.place, begin=part * 128, count=128)
        return self.copy(rows, self.line, part, part, b.chip(lax.rem(b.z + 1, 4), b.place))

    def far_copy(self, group, step):
        b = self.board
        rows = b.half_rows(group * 4 + b.place)
        return self.copy(rows, self.far, step - 1, group, b.chip((group + step) % 4, b.place))

    def plane_copy(self, group, near, of=None, begin=0, count=HALF, sem=None):
        b = self.board
        place = b.place if of is None else b.places[of]
        rows = b.half_rows(group * 4 + place, begin=begin, count=count)
        sem = group * 4 + (near if sem is None else sem)
        return self.copy(rows, self.plane, sem, sem, b.chip(b.z, b.places[near]))

    def core_copy(self, group, of):
        b = self.board
        rows = b.half_rows(group * 4 + b.places[of])
        return self.copy(rows, self.core, group * 4 + of, group * 4 + of, b.across())

    def first_line(self):
        z = self.board.z

        @pl.when(z == 0)
        def _():
            for part in range(2):
                self.line_copy(part).start()

        for part in range(2):

            @pl.when(z > 0)
            def _():
                self.line_copy(part).wait_recv()

            @pl.when((z > 0) & (z < 3))
            def _():
                self.line_copy(part).start()

    def first_plane_start(self):
        self.plane_copy(0, 1).start()
        self.plane_copy(0, 2).start()
        self.core_copy(0, 0).start()

    def first_plane_end(self):
        self.plane_copy(0, 1).wait_recv()
        self.plane_copy(0, 2, of=1, begin=128, count=128, sem=3).start()
        self.core_copy(0, 1).start()
        self.plane_copy(0, 2).wait_recv()
        self.plane_copy(0, 1, of=2, begin=0, count=128, sem=0).start()
        self.core_copy(0, 2).start()
        self.plane_copy(0, 1, of=2, begin=0, count=128, sem=0).wait_recv()
        self.plane_copy(0, 2, of=1, begin=128, count=128, sem=3).wait_recv()
        self.core_copy(0, 3).start()
        self.finish(0)

    def send_far(self, group):
        @pl.when(self.board.z == group)
        def _():
            for step in range(1, 4):
                self.far_copy(group, step).start()

    def send_plane(self, group):
        @pl.when(self.board.z != group)
        def _():
            self.far_copy(group, 1).wait_recv()

        for near in range(1, 4):
            self.plane_copy(group, near).start()
        self.core_copy(group, 0).start()

    def send_core(self, group):
        for near in range(1, 4):
            self.plane_copy(group, near).wait_recv()
            self.core_copy(group, near).start()

    def finish(self, group):
        for of in range(4):
            self.core_copy(group, of).wait_recv()

    def drain(self):
        z = self.board.z

        @pl.when(z < 3)
        def _():
            for part in range(2):
                self.line_copy(part).wait_send()

        for group in range(1, 4):

            @pl.when(z == group)
            def _():
                for step in range(1, 4):
                    self.far_copy(group, step).wait_send()

            for near in range(1, 4):
                self.plane_copy(group, near).wait_send()
        self.plane_copy(0, 1).wait_send()
        self.plane_copy(0, 2).wait_send()
        self.plane_copy(0, 1, of=2, begin=0, count=128, sem=0).wait_send()
        self.plane_copy(0, 2, of=1, begin=128, count=128, sem=3).wait_send()
        for group in range(4):
            for of in range(4):
                self.core_copy(group, of).wait_send()


class Scatter:
    def __init__(self, board, late, early, core_in, plane_in, line_in, total, sems):
        self.board = board
        self.late = late
        self.early = early
        self.core_in = core_in
        self.plane_in = plane_in
        self.line_in = line_in
        self.total = total
        self.core_s, self.core_r, self.plane_s, self.plane_r, self.line_s, self.line_r = sems

    def home(self, group):
        return (self.late, 0) if group < 2 else (self.early, 8)

    def core_copy(self, group, index):
        b = self.board
        ref, first = self.home(group)
        rows = b.half_rows(group * 4 + index - first, core=1 - b.core)
        slot = {0: 4, 1: 0, 2: 0, 3: 4}[group] + index
        sem = group * 4 + index
        return remote(
            ref.at[rows, :], self.core_in.at[slot], self.core_s.at[sem], self.core_r.at[sem],
            b.across(),
        )

    def plane_copy(self, group, near):
        b = self.board
        ref, first = self.home(group)
        rows = b.half_rows(group * 4 + b.places[near] - first)
        sem = group * 3 + near - 1
        return remote(
            ref.at[rows, :], self.plane_in.at[sem], self.plane_s.at[sem], self.plane_r.at[sem],
            b.chip(b.z, b.places[near]),
        )

    def line_copy(self, group):
        b = self.board
        ref, first = self.home(group)
        rows = b.half_rows(group * 4 + b.place - first)
        slot = lax.rem(b.z - group + 4, 4) - 1
        return remote(
            ref.at[rows, :], self.line_in.at[slot], self.line_s.at[group], self.line_r.at[slot],
            b.chip(group, b.place),
        )

    def add_core(self, group):
        b = self.board
        ref, first = self.home(group)
        for index in range(4):
            copy = self.core_copy(group, index)
            copy.wait_recv()
            rows = b.half_rows(group * 4 + index - first)
            slot = {0: 4, 1: 0, 2: 0, 3: 4}[group] + index
            ref[rows, :] = (ref[rows, :].astype(F32) + self.core_in[slot].astype(F32)).astype(BF)
        for near in (3, 1, 2):
            self.plane_copy(group, near).start()

    def add_plane(self, group):
        b = self.board
        ref, first = self.home(group)
        rows = b.half_rows(group * 4 + b.place - first)
        value = ref[rows, :].astype(F32)
        for near in range(1, 4):
            self.plane_copy(group, near).wait_recv()
            value = value + self.plane_in[group * 3 + near - 1].astype(F32)

        @pl.when(b.z == group)
        def _():
            self.total[...] = value

        @pl.when(b.z != group)
        def _():
            ref[rows, :] = value.astype(BF)
            self.line_copy(group).start()

    def finish(self):
        b = self.board
        value = self.total[...]
        for slot in range(3):
            remote(
                self.line_in.at[slot], self.line_in.at[slot], self.line_s.at[4],
                self.line_r.at[slot], b.across(),
            ).wait_recv()
            value = value + self.line_in[slot].astype(F32)
        self.total[...] = value

    def drain(self):
        for group in range(4):
            for index in range(4):
                self.core_copy(group, index).wait_send()
            for near in range(1, 4):
                self.plane_copy(group, near).wait_send()

            @pl.when(self.board.z != group)
            def _():
                self.line_copy(group).wait_send()


class VectorSum:
    def __init__(self, board, own, core_in, plane_in, line_in, total, send, recv):
        self.board = board
        self.own = own
        self.core_in = core_in
        self.plane_in = plane_in
        self.line_in = line_in
        self.total = total
        self.send = send
        self.recv = recv

    def core_copy(self):
        return remote(
            self.own, self.core_in, self.send.at[0], self.recv.at[0], self.board.across()
        )

    def plane_copy(self, near):
        b = self.board
        return remote(
            self.plane_in.at[b.place], self.plane_in.at[b.place], self.send.at[near],
            self.recv.at[near], b.chip(b.z, b.places[near]),
        )

    def line_copy(self, step):
        b = self.board
        return remote(
            self.line_in.at[b.z], self.line_in.at[b.z], self.send.at[3 + step],
            self.recv.at[3 + step], b.chip(lax.rem(b.z + step, 4), b.place),
        )

    def begin(self):
        self.core_copy().start()

    def middle(self):
        b = self.board
        self.core_copy().wait_recv()
        self.plane_in[b.place] = self.own[...] + self.core_in[...]
        for near in range(1, 4):
            self.plane_copy(near).start()

    def late(self):
        b = self.board
        for near in range(1, 4):
            self.plane_copy(near).wait_recv()
        self.line_in[b.z] = (
            (self.plane_in[0] + self.plane_in[1]) + (self.plane_in[2] + self.plane_in[3])
        )
        for step in range(1, 4):
            self.line_copy(step).start()

    def end(self):
        for step in range(1, 4):
            self.line_copy(step).wait_recv()
        value = (self.line_in[0] + self.line_in[1]) + (self.line_in[2] + self.line_in[3])
        self.total[...] = value[: self.total.shape[0], :]
        self.core_copy().wait_send()
        for near in range(1, 4):
            self.plane_copy(near).wait_send()
            self.line_copy(near).wait_send()


def layer_kernel(fused, *refs):
    tok, mem, cot, meta, vec, source, out_ref, igrad_ref, mgrad_ref, g_ref, gv_ref = refs[:11]
    (
        keys, metas, bias, probs_s, probs_c, flip, q_ref, cq_ref, attn_t, cross_t, grad_t, dq_t,
        parts, arrived, res_a, res_b, res_c, send_sem, recv_sem, meta_sem,
    ) = refs[11:31]
    core = lax.axis_index("stream")
    other = 1 - core
    own = pl.ds(pl.multiple_of(core * ROWS, ROWS), ROWS)
    theirs = pl.ds(pl.multiple_of(other * ROWS, ROWS), ROWS)
    barrier = pltpu.get_barrier_semaphore()
    gather = scatter = vectors = None
    if fused:
        w, early, core_in, plane_in, line_in, vec_own, vec_core, vec_plane, vec_line = refs[31:40]
        sems = refs[40:]
        board = Board()
        gather = Gather(board, w, *sems[:8])
        scatter = Scatter(board, probs_c, early, core_in, plane_in, line_in, g_ref, sems[8:14])
        vectors = VectorSum(
            board, vec_own, vec_core, vec_plane, vec_line, gv_ref, sems[14], sems[15]
        )
        w[board.half_rows(board.dp), :] = source[...].astype(BF)
        friends = [board.across()]
        friends += [board.chip(board.z, board.places[near]) for near in range(1, 4)]
        friends += [board.chip(lax.rem(board.z + step, 4), board.place) for step in range(1, 4)]
        sums = vec_own
        sums[...] = jnp.zeros_like(sums)
    else:
        w = source
        friends = [{"stream": other}]
        sums = gv_ref
    for friend in friends:
        pl.semaphore_signal(barrier, inc=1, device_id=friend, device_id_type=MESH)
    pl.semaphore_wait(barrier, len(friends))

    def swap(src, dst, index):
        return remote(src, dst, send_sem.at[index], recv_sem.at[index], {"stream": other})

    def weight(index):
        return w[index * D : (index + 1) * D, :]

    def vector(index):
        return vec[index : index + 1, :]

    def gradient(group, index, value):
        if fused:
            ref, first = scatter.home(group)
            rows = pl.ds(pl.multiple_of((group * 4 + index - first) * D, D), D)
            ref[rows, :] = value.astype(BF)
            scatter.core_copy(group, index).start()
        else:
            rows = pl.ds(pl.multiple_of((group * 4 + index) * D, D), D)
            g_ref[rows, :] = value.astype(BF)

    meta_copy = remote(meta, metas, meta_sem.at[0], meta_sem.at[1], {"stream": other})
    meta_copy.start()
    if fused:
        gather.first_line()
        gather.first_plane_start()
        gather.send_far(1)
    hid, _, _ = norm_forward(tok[...].astype(F32), vector(0), vector(1))
    attn_t[...] = hid.astype(BF)

    meta_copy.wait()
    row = lax.broadcasted_iota(jnp.int32, (ROWS, ROWS), 0)
    col = lax.broadcasted_iota(jnp.int32, (ROWS, ROWS), 1)

    def fill_bias(with_priority):
        for rows, held, own_half in ((own, meta, True), (theirs, metas, False)):
            turned = held[...].T
            visible = turned[:, 0:1] == meta[2:3, :]
            if with_priority:
                visible = visible & (turned[:, 1:2] < meta[3:4, :])
            if own_half:
                visible = visible | (row == col)
            bias[rows, :] = jnp.where(visible, 0.0, -1e30)

    fill_bias(True)
    if fused:
        gather.first_plane_end()
        gather.send_far(2)
        gather.send_far(3)

    copies = [swap(keys.at[index, own, :], keys.at[index, own, :], index) for index in range(4)]
    hid = attn_t[...]
    keys[0, own, :] = nn(hid, weight(1)).astype(BF)
    copies[0].start()
    keys[1, own, :] = (nn(hid, weight(2)) + vector(7)).astype(BF)
    copies[1].start()
    q_ref[...] = (nn(hid, weight(0)) + vector(6)).astype(BF)
    if fused:
        gather.send_plane(1)
    copies[0].wait()
    copies[1].wait()
    flip[...] = keys[1].T
    attend_forward(q_ref, keys.at[0], flip, bias, probs_s, attn_t, (0, 2))
    if fused:
        gather.send_plane(2)
    attend_forward(q_ref, keys.at[0], flip, bias, probs_s, attn_t, (2, 4))
    if fused:
        gather.send_core(1)
        gather.send_plane(3)
    res_one = tok[...].astype(F32) + nn(attn_t[...].T, weight(3)) + vector(8)
    res_a[...] = res_one
    hid, _, _ = norm_forward(res_one, vector(2), vector(3))
    fill_bias(False)
    if fused:
        gather.finish(1)
    keys[2, own, :] = nn(mem[...], weight(5)).astype(BF)
    copies[2].start()
    keys[3, own, :] = (nn(mem[...], weight(6)) + vector(10)).astype(BF)
    copies[3].start()
    cq_ref[...] = (nn(hid.astype(BF), weight(4)) + vector(9)).astype(BF)
    copies[2].wait()
    copies[3].wait()
    flip[...] = keys[3].T
    attend_forward(cq_ref, keys.at[2], flip, bias, probs_c, cross_t, (0, 2))
    if fused:
        gather.send_core(2)
    attend_forward(cq_ref, keys.at[2], flip, bias, probs_c, cross_t, (2, 4))
    if fused:
        gather.send_core(3)
    res_two = res_a[...] + nn(cross_t[...].T, weight(7)) + vector(11)
    res_b[...] = res_two
    hid, _, _ = norm_forward(res_two, vector(4), vector(5))
    grad_t[...] = hid.astype(BF)
    res_c[...] = jnp.zeros((ROWS, D), F32)
    igrad_ref[...] = res_two + vector(12)
    sums[12:13, :] = column_sum(cot[...])
    if fused:
        gather.finish(2)
        gather.finish(3)

    def ffn_body(part, carry):
        w_in = w[pl.ds(pl.multiple_of(8 * D + part * D, D), D), :]
        w_out = w[pl.ds(pl.multiple_of(8 * D + FF + part * D, D), D), :]
        h_three = grad_t[...]
        pre = nt(h_three, w_in) + vec[pl.ds(13 + part, 1), :]
        hidden = jnp.maximum(pre, 0.0).astype(BF)
        igrad_ref[...] += nn(hidden, w_out)
        grad_pre = jnp.where(pre > 0, nt(cot[...], w_out), 0.0).astype(BF)
        res_c[...] += nn(grad_pre, w_in)
        sums[pl.ds(13 + part, 1), :] = column_sum(grad_pre)
        gradient(2, part, tn(grad_pre, h_three))
        gradient(3, part, tn(hidden, cot[...]))
        return carry

    lax.fori_loop(0, FF // D, ffn_body, 0)
    out_ref[...] = igrad_ref[...].astype(BF)

    _, normed, spread = norm_forward(res_b[...], vector(4), vector(5))
    grad_in, sums[4:5, :], sums[5:6, :] = norm_backward(normed, spread, vector(4), res_c[...])
    grad_res = cot[...].astype(F32) + grad_in
    res_b[...] = grad_res
    sums[11:12, :] = column_sum(grad_res)
    dz_two = grad_res.astype(BF)
    grad_t[...] = nt(weight(7), dz_two).astype(BF)
    flip[...] = keys[2].T
    if fused:
        scatter.add_core(2)
        scatter.add_core(3)
    attend_backward(
        cq_ref, flip, keys.at[3], grad_t, cross_t, probs_c, dq_t, parts.at[0], parts.at[1], (0, 4)
    )
    back = [swap(parts.at[index % 2, theirs, :], arrived.at[index], 4 + index) for index in range(4)]
    back[2].start()
    back[3].start()

    def summed(index):
        back[index].wait()
        return (parts[index % 2, own, :].astype(F32) + arrived[index].astype(F32)).astype(BF)

    if fused:
        scatter.add_plane(2)
    grad_cq = dq_t[...].T
    sums[9:10, :] = column_sum(grad_cq)
    hid, normed, spread = norm_forward(res_a[...], vector(2), vector(3))
    grad_in, sums[2:3, :], sums[3:4, :] = norm_backward(
        normed, spread, vector(2), nt(grad_cq, weight(4))
    )
    grad_mk = summed(2)
    grad_mv = summed(3)
    gradient(1, 0, tn(hid.astype(BF), grad_cq))
    gradient(1, 3, nn(cross_t[...], res_b[...].astype(BF)))
    grad_res = res_b[...] + grad_in
    res_b[...] = grad_res
    sums[8:9, :] = column_sum(grad_res)
    sums[10:11, :] = column_sum(grad_mv)
    mgrad_ref[...] = nt(grad_mk, weight(5)) + nt(grad_mv, weight(6))
    gradient(1, 1, tn(mem[...], grad_mk))
    gradient(1, 2, tn(mem[...], grad_mv))
    dz_one = res_b[...].astype(BF)
    grad_t[...] = nt(weight(3), dz_one).astype(BF)
    gradient(0, 3, nn(attn_t[...], dz_one))
    flip[...] = keys[0].T
    if fused:
        scatter.add_plane(3)
        scatter.add_core(1)
    attend_backward(
        q_ref, flip, keys.at[1], grad_t, attn_t, probs_s, dq_t, parts.at[0], parts.at[1], (0, 2)
    )
    if fused:
        scatter.add_plane(1)
    attend_backward(
        q_ref, flip, keys.at[1], grad_t, attn_t, probs_s, dq_t, parts.at[0], parts.at[1], (2, 4)
    )
    back[0].start()
    back[1].start()
    hid, normed, spread = norm_forward(tok[...].astype(F32), vector(0), vector(1))
    hid = hid.astype(BF)
    grad_q = dq_t[...].T
    gradient(0, 0, tn(hid, grad_q))
    grad_k = summed(0)
    gradient(0, 1, tn(hid, grad_k))
    grad_v = summed(1)
    gradient(0, 2, tn(hid, grad_v))
    sums[6:7, :] = column_sum(grad_q)
    sums[7:8, :] = column_sum(grad_v)
    grad_h = nt(grad_q, weight(0)) + nt(grad_k, weight(1)) + nt(grad_v, weight(2))
    if fused:
        scatter.add_core(0)
    grad_in, sums[0:1, :], sums[1:2, :] = norm_backward(normed, spread, vector(0), grad_h)
    if fused:
        vectors.begin()
    igrad_ref[...] = res_b[...] + grad_in
    if fused:
        vectors.middle()
        scatter.add_plane(0)
        vectors.late()
        scatter.finish()
        vectors.end()
        gather.drain()
        scatter.drain()


def layer_call(fused, tok, mem, cot, meta, vec, source):
    shape = jax.ShapeDtypeStruct
    vmem = pl.BlockSpec(memory_space=pltpu.VMEM)
    dma = pltpu.SemaphoreType.DMA
    scratch = [
        pltpu.VMEM((4, KEYS, D), BF),
        pltpu.VMEM((8, ROWS), jnp.int32),
        pltpu.VMEM((KEYS, ROWS), F32),
        pltpu.VMEM((HEADS * KEYS, ROWS), BF),
        pltpu.VMEM((HEADS * KEYS, ROWS), BF),
        pltpu.VMEM((D, KEYS), BF),
        *[pltpu.VMEM((ROWS, D), BF) for _ in range(6)],
        pltpu.VMEM((2, KEYS, D), BF),
        pltpu.VMEM((4, ROWS, D), BF),
        *[pltpu.VMEM((ROWS, D), F32) for _ in range(3)],
        dma((8,)), dma((8,)), dma((2,)),
    ]
    if fused:
        scratch += [
            pltpu.VMEM((8 * D + 2 * FF, D), BF),
            pltpu.VMEM((2 * FF, D), BF),
            pltpu.VMEM((8, HALF, D), BF),
            pltpu.VMEM((12, HALF, D), BF),
            pltpu.VMEM((3, HALF, D), BF),
            pltpu.VMEM((24, D), F32),
            pltpu.VMEM((24, D), F32),
            pltpu.VMEM((4, 24, D), F32),
            pltpu.VMEM((4, 24, D), F32),
            dma((2,)), dma((2,)), dma((3,)), dma((4,)), dma((16,)), dma((16,)), dma((16,)), dma((16,)),
            dma((16,)), dma((16,)), dma((12,)), dma((12,)), dma((5,)), dma((3,)),
            dma((7,)), dma((7,)),
        ]
    grad_shape = shape((HALF, D), F32) if fused else shape(source.shape, BF)
    return pl.pallas_call(
        functools.partial(layer_kernel, fused),
        out_shape=[
            shape((ROWS, D), BF), shape((ROWS, D), F32), shape((ROWS, D), F32),
            grad_shape, shape(vec.shape, F32),
        ],
        in_specs=[vmem] * 6,
        out_specs=[vmem] * 5,
        scratch_shapes=scratch,
        compiler_params=pltpu.CompilerParams(
            collective_id=0, has_side_effects=True, vmem_limit_bytes=63 * 1024 * 1024
        ),
        cost_estimate=pl.CostEstimate(
            flops=22_000_000_000, bytes_accessed=24_000_000, transcendentals=8_000_000
        ),
    )(tok, mem, cot, meta, vec, source)


def partner(block, axis, stride):
    count = lax.axis_size(axis)
    route = []
    for low in range(count):
        high = low | 1 << stride
        if high != low and high < count:
            route += [(low, high), (high, low)]
    return lax.ppermute(block, axis, route)


def high_dot(left_mat, right_mat):
    return jnp.dot(left_mat, right_mat, precision=lax.Precision.HIGH)


def exact_lead(left_mat, right_mat):
    return lax.dot_general(left_mat, right_mat, (((0,), (0,)), ((), ())), precision=HIGH)


def per_device(
    tokens,
    memory,
    cotangent,
    segments,
    padding,
    priority,
    threshold,
    master,
    momentum,
    vectors,
    vec_first,
    vec_second,
    step_count,
):
    meta = jnp.stack([jnp.where(padding == 0, segments, -1), priority, segments, threshold] * 2)
    matrix = vectors.reshape(-1, D)
    fused = lax.axis_size("dp") == 16 and lax.axis_size("stream") == 2
    if fused:
        layer_out, input_grad, memory_grad, grad_rows, grad_vec = layer_call(
            True, tokens, memory, cotangent, meta, matrix, master
        )
        grad_vec = grad_vec.reshape(-1)
    else:
        low_all = lax.all_gather(master.astype(BF), ("dp", "stream"), axis=0, tiled=True)
        layer_out, input_grad, memory_grad, grad_all, vec_local = layer_call(
            False, tokens, memory, cotangent, meta, matrix, low_all
        )
        grad_rows = lax.psum_scatter(
            grad_all, ("dp", "stream"), scatter_dimension=0, tiled=True
        ).astype(F32)
        grad_vec = lax.psum(vec_local.reshape(-1), ("dp", "stream"))
    opt_rows = master.shape[0]
    device_index = lax.axis_index(("dp", "stream"))
    start_row = device_index * opt_rows
    in_ffn = start_row >= 8 * D
    att_bits = (D // opt_rows).bit_length() - 1
    ffn_bits = (FF // opt_rows).bit_length() - 1
    own_bits = jnp.where(in_ffn, ffn_bits, att_bits)
    new_momentum = 0.5 * momentum + grad_rows

    def gram_total(partial_value):
        for bit_pos in range(ffn_bits):
            other = partner(partial_value, ("dp", "stream"), bit_pos)
            partial_value = partial_value + jnp.where(bit_pos < own_bits, other, 0.0)
        return partial_value

    gram_first = gram_total(exact_lead(new_momentum, new_momentum))
    divisor = jnp.sqrt(jnp.trace(gram_first)) + 1e-07
    gram = gram_first / (divisor * divisor)
    unit = jnp.eye(D, dtype=jnp.float32)
    chain = None
    for turn in range(5):
        poly = NS_A * unit + NS_B * gram + NS_C * high_dot(gram, gram)
        chain = poly if chain is None else high_dot(chain, poly)
        if turn < 4:
            gram = high_dot(high_dot(gram, poly), poly)
    current = high_dot(new_momentum / divisor, chain)
    rate = MUON_RATE * jnp.where(in_ffn, (FF / D) ** 0.5, 1.0)
    new_master = master - rate * current
    count = step_count[0].astype(jnp.float32)
    new_first = 0.5 * vec_first + 0.5 * grad_vec
    new_second = 0.999 * vec_second + 0.001 * grad_vec * grad_vec
    first_fix = new_first / (1.0 - jnp.power(0.5, count))
    second_fix = new_second / (1.0 - jnp.power(0.999, count))
    new_vectors = vectors - ADAM_RATE * (
        first_fix / (jnp.sqrt(second_fix) + 1e-08) + ADAM_DECAY * vectors
    )
    return (
        layer_out,
        input_grad,
        memory_grad,
        new_momentum,
        new_master,
        new_vectors,
        new_first,
        new_second,
    )


def solution(mesh):
    return jax.shard_map(
        per_device,
        mesh=mesh,
        in_specs=(
            P(("dp", "stream"), None),
            P(("dp", "stream"), None),
            P(("dp", "stream"), None),
            P(("dp", "stream")),
            P(("dp", "stream")),
            P(("dp", "stream")),
            P(("dp", "stream")),
            P(("dp", "stream"), None),
            P(("dp", "stream"), None),
            P(),
            P(),
            P(),
            P(),
        ),
        out_specs=(
            P(("dp", "stream"), None),
            P(("dp", "stream"), None),
            P(("dp", "stream"), None),
            P(("dp", "stream"), None),
            P(("dp", "stream"), None),
            P(),
            P(),
            P(),
        ),
        check_vma=False,
    )
```

```python
import functools

import jax
import jax.numpy as jnp
from jax import lax
from jax.experimental import pallas as pl
from jax.experimental.pallas import tpu as pltpu
from jax.sharding import PartitionSpec as P

D = 512
HEADS = 8
HEAD = 64
FF = 2048
ROWS = 512
KEYS = 1024
CHUNK = 256
HALF = 256
BF = jnp.bfloat16
F32 = jnp.float32
SCALE = HEAD ** (-0.5)
LOG2E = 1.4426950408889634
MESH = pl.DeviceIdType.MESH

NS_A = 3.4445
NS_B = -4.775
NS_C = 2.0315
MUON_RATE = 0.8
ADAM_RATE = 0.2
ADAM_DECAY = 0.01
HIGH = lax.Precision.HIGHEST


def nn(left_mat, right_mat):
    return lax.dot_general(
        left_mat, right_mat, (((1,), (0,)), ((), ())), preferred_element_type=F32
    )


def nt(left_mat, right_mat):
    return lax.dot_general(
        left_mat, right_mat, (((1,), (1,)), ((), ())), preferred_element_type=F32
    )


def tn(left_mat, right_mat):
    return lax.dot_general(
        left_mat, right_mat, (((0,), (0,)), ((), ())), preferred_element_type=F32
    )


def norm_forward(values, gain_vec, shift_vec):
    center = values - jnp.mean(values, axis=-1, keepdims=True)
    spread = lax.rsqrt(jnp.mean(center * center, axis=-1, keepdims=True) + 1e-05)
    normed = center * spread
    return normed * gain_vec + shift_vec, normed, spread


def norm_backward(normed, spread, gain_vec, grad_out):
    grad_gain = jnp.sum(grad_out * normed, axis=0, keepdims=True)
    grad_shift = jnp.sum(grad_out, axis=0, keepdims=True)
    scaled = grad_out * gain_vec
    grad_in = spread * (
        scaled
        - jnp.mean(scaled, axis=-1, keepdims=True)
        - normed * jnp.mean(scaled * normed, axis=-1, keepdims=True)
    )
    return grad_in, grad_gain, grad_shift


def column_sum(values):
    return jnp.sum(values.astype(F32), axis=0, keepdims=True)


def half_lanes(values, sub):
    lane = lax.broadcasted_iota(jnp.int32, values.shape, 1)
    keep = lane < HEAD if sub == 0 else lane >= HEAD
    return jnp.where(keep, values, jnp.zeros_like(values))


def head_keys(head):
    return pl.ds(pl.multiple_of(head * KEYS, KEYS), KEYS)


def attend_forward(q_ref, k_ref, value_t, bias, probs, mixed_t, pairs):
    def pair_body(pair, carry):
        lanes = pl.ds(pl.multiple_of(pair * 128, 128), 128)
        keys = k_ref[:, lanes]
        for sub in range(2):
            head_rows = pl.ds(pl.multiple_of(pair * 128 + sub * HEAD, HEAD), HEAD)
            for begin in range(0, ROWS, CHUNK):
                cols = slice(begin, begin + CHUNK)
                scores = nt(keys, half_lanes(q_ref[cols, lanes], sub))
                scores = scores * (SCALE * LOG2E) + bias[:, cols]
                expo = jnp.exp2(scores - jnp.max(scores, axis=0, keepdims=True))
                total = jnp.sum(expo, axis=0, keepdims=True)
                low = (expo * (1.0 / total)).astype(BF)
                probs[head_keys(pair * 2 + sub), cols] = low
                mixed_t[head_rows, cols] = nn(value_t[head_rows, :], low).astype(BF)
        return carry

    lax.fori_loop(pairs[0], pairs[1], pair_body, 0)


def attend_backward(q_ref, k_t, v_ref, grad_t, mixed_t, probs, dq_t, dk_ref, dv_ref, pairs):
    def pair_body(pair, carry):
        lanes = pl.ds(pl.multiple_of(pair * 128, 128), 128)
        values = v_ref[:, lanes]
        sum_k = None
        sum_v = None
        for sub in range(2):
            head_rows = pl.ds(pl.multiple_of(pair * 128 + sub * HEAD, HEAD), HEAD)
            for begin in range(0, ROWS, CHUNK):
                cols = slice(begin, begin + CHUNK)
                grad = grad_t[head_rows, cols]
                inner = jnp.sum(
                    grad.astype(F32) * mixed_t[head_rows, cols].astype(F32), axis=0, keepdims=True
                )
                zero = jnp.zeros_like(grad)
                grad_pair = jnp.concatenate([grad, zero] if sub == 0 else [zero, grad], axis=0)
                grad_probs = nn(values, grad_pair)
                low = probs[head_keys(pair * 2 + sub), cols]
                grad_scores = (low.astype(F32) * (grad_probs - inner)).astype(BF)
                dq_t[head_rows, cols] = (nn(k_t[head_rows, :], grad_scores) * SCALE).astype(BF)
                part_k = nn(grad_scores, half_lanes(q_ref[cols, lanes], sub))
                part_v = nn(low, grad_pair.T)
                sum_k = part_k if sum_k is None else sum_k + part_k
                sum_v = part_v if sum_v is None else sum_v + part_v
        dk_ref[:, lanes] = (sum_k * SCALE).astype(dk_ref.dtype)
        dv_ref[:, lanes] = sum_v.astype(dv_ref.dtype)
        return carry

    lax.fori_loop(pairs[0], pairs[1], pair_body, 0)


class Board:
    def __init__(self):
        self.dp = lax.axis_index("dp")
        self.core = lax.axis_index("stream")
        self.z = self.dp // 4
        self.place = self.dp % 4
        x = self.place % 2
        y = self.place // 2
        side_x = self.place + 1 - 2 * x
        side_y = self.place + 2 - 4 * y
        self.places = (self.place, side_x, side_y, 3 - self.place)

    def chip(self, plane, place):
        return {"dp": plane * 4 + place, "stream": self.core}

    def across(self):
        return {"dp": self.dp, "stream": 1 - self.core}

    def half_rows(self, block, core=None, begin=0, count=HALF):
        core = self.core if core is None else core
        return pl.ds(pl.multiple_of(block * D + core * HALF + begin, 64), count)


def remote(src, dst, send, recv, device):
    return pltpu.make_async_remote_copy(
        src_ref=src, dst_ref=dst, send_sem=send, recv_sem=recv,
        device_id=device, device_id_type=MESH,
    )


class Gather:
    def __init__(self, board, w, line_s, line_r, far_s, far_r, plane_s, plane_r, core_s, core_r):
        self.board = board
        self.w = w
        self.line = (line_s, line_r)
        self.far = (far_s, far_r)
        self.plane = (plane_s, plane_r)
        self.core = (core_s, core_r)

    def copy(self, rows, sems, send, recv, device):
        view = self.w.at[rows, :]
        return remote(view, view, sems[0].at[send], sems[1].at[recv], device)

    def line_copy(self, part):
        b = self.board
        rows = b.half_rows(b.place, begin=part * 64, count=64)
        return self.copy(rows, self.line, part, part, b.chip(lax.rem(b.z + 1, 4), b.place))

    def far_copy(self, group, plane):
        b = self.board
        rows = b.half_rows(group * 4 + b.place)
        return self.copy(rows, self.far, plane, group, b.chip(plane, b.place))

    def near_copy(self, of, near, part, sem):
        b = self.board
        rows = b.half_rows(b.places[of], begin=part * 128, count=128)
        return self.copy(rows, self.plane, sem, sem, b.chip(b.z, b.places[near]))

    def first_copy(self, index):
        of, near, part = ((0, 1, 0), (0, 2, 0), (0, 1, 1), (0, 2, 1), (2, 1, 0), (1, 2, 1))[index]
        return self.near_copy(of, near, part, index)

    def plane_copy(self, group, near):
        b = self.board
        rows = b.half_rows(group * 4 + b.place)
        sem = 3 + group * 3 + near - 1
        return self.copy(rows, self.plane, sem, sem, b.chip(b.z, b.places[near]))

    def core_copy(self, group, of):
        b = self.board
        rows = b.half_rows(group * 4 + b.places[of])
        return self.copy(rows, self.core, group * 4 + of, group * 4 + of, b.across())

    def first_line(self):
        z = self.board.z
        for group in (3, 2, 1):
            for plane in range(group):

                @pl.when(z == group)
                def _():
                    self.far_copy(group, plane).start()

        for part in range(4):

            @pl.when(z > 0)
            def _():
                self.line_copy(part).wait_recv()

            @pl.when(z < 3)
            def _():
                self.line_copy(part).start()

            if part % 2:
                self.first_copy(part - 1).start()
                self.first_copy(part).start()
        self.core_copy(0, 0).start()
        for group in (1, 2):
            for plane in range(group + 1, 4):

                @pl.when(z == group)
                def _():
                    self.far_copy(group, plane).start()

    def first_plane(self):
        self.first_copy(1).wait_recv()
        self.first_copy(4).start()
        self.first_copy(0).wait_recv()
        self.first_copy(2).wait_recv()
        self.first_copy(5).start()
        self.core_copy(0, 1).start()
        self.first_copy(3).wait_recv()
        self.core_copy(0, 2).start()
        self.first_copy(4).wait_recv()
        self.first_copy(5).wait_recv()
        self.core_copy(0, 3).start()

    def send_plane(self, group):
        @pl.when(self.board.z != group)
        def _():
            self.far_copy(group, 0).wait_recv()

        for near in range(1, 4):
            self.plane_copy(group, near).start()
        self.core_copy(group, 0).start()

    def send_core(self, group):
        for near in range(1, 4):
            self.plane_copy(group, near).wait_recv()
            self.core_copy(group, near).start()

    def finish(self, group):
        for of in range(4):
            self.core_copy(group, of).wait_recv()

    def drain(self):
        z = self.board.z
        for part in range(4):

            @pl.when(z < 3)
            def _():
                self.line_copy(part).wait_send()

        for group in range(1, 4):
            for plane in range(4):
                if plane != group:

                    @pl.when(z == group)
                    def _():
                        self.far_copy(group, plane).wait_send()

            for near in range(1, 4):
                self.plane_copy(group, near).wait_send()
        for index in range(6):
            self.first_copy(index).wait_send()
        for group in range(4):
            for of in range(4):
                self.core_copy(group, of).wait_send()


class Scatter:
    def __init__(self, board, late, early, core_in, plane_in, line_in, total, sems):
        self.board = board
        self.late = late
        self.early = early
        self.core_in = core_in
        self.plane_in = plane_in
        self.line_in = line_in
        self.total = total
        self.core_s, self.core_r, self.plane_s, self.plane_r, self.line_s, self.line_r = sems

    def group(self, pack):
        return max(pack - 1, 0)

    def lanes(self, pack):
        return slice(0, D) if pack > 1 else slice(pack * HALF, pack * HALF + HALF)

    def home(self, group):
        return (self.late, 0) if group < 2 else (self.early, 8)

    def slot(self, group, index):
        return (4, 0, 0, 4)[group] + index

    def part(self, pack, of, begin, count=128):
        ref, first = self.home(self.group(pack))
        rows = self.board.half_rows(self.group(pack) * 4 + self.board.places[of] - first, None, begin, count)
        return ref.at[rows, self.lanes(pack)]

    def core_copy(self, pack, index):
        b = self.board
        group = self.group(pack)
        ref, first = self.home(group)
        rows = b.half_rows(group * 4 + index - first, core=1 - b.core)
        return remote(
            ref.at[rows, self.lanes(pack)],
            self.core_in.at[self.slot(group, index), :, self.lanes(pack)],
            self.core_s.at[pack * 4 + index], self.core_r.at[pack * 4 + index], b.across(),
        )

    def landed(self, pack, slot):
        return self.plane_in.at[self.group(pack) * 6 + slot, :, self.lanes(pack)]

    def plane_copy(self, pack, slot):
        of, near, begin = ((1, 1, 0), (3, 1, 0), (2, 2, 128), (3, 2, 128), (2, 2, 0), (1, 1, 128))[slot]
        b = self.board
        sem = pack * 6 + slot
        return remote(
            self.part(pack, of, begin), self.landed(pack, slot), self.plane_s.at[sem],
            self.plane_r.at[sem], b.chip(b.z, b.places[near]),
        )

    def line_copy(self, pack):
        b = self.board
        group = self.group(pack)
        slot = lax.rem(b.z - group + 4, 4) - 1
        half = 1 if pack == 1 else 0
        return remote(
            self.part(pack, 0, 0, HALF), self.line_in.at[slot, :, self.lanes(pack)],
            self.line_s.at[pack], self.line_r.at[half * 3 + slot], b.chip(group, b.place),
        )

    def add_core(self, pack):
        b = self.board
        group = self.group(pack)
        ref, first = self.home(group)
        lanes = self.lanes(pack)
        for index in range(4):
            self.core_copy(pack, index).wait_recv()
        for index in range(4):
            rows = b.half_rows(group * 4 + index - first)
            came = self.core_in[self.slot(group, index), :, lanes]
            ref[rows, lanes] = (ref[rows, lanes].astype(F32) + came.astype(F32)).astype(BF)
        for slot in (1, 3, 0, 2):
            self.plane_copy(pack, slot).start()

    def pass_plane(self, pack):
        for slot, of, begin, onward in ((1, 2, 0, 4), (3, 1, 128, 5)):
            self.plane_copy(pack, slot).wait_recv()
            mine = self.part(pack, of, begin)
            mine[...] = (mine[...].astype(F32) + self.landed(pack, slot)[...].astype(F32)).astype(BF)
            self.plane_copy(pack, onward).start()

    def end_plane(self, pack):
        b = self.board
        for begin, first, second in ((0, 0, 4), (128, 2, 5)):
            self.plane_copy(pack, first).wait_recv()
            self.plane_copy(pack, second).wait_recv()
            mine = self.part(pack, 0, begin)
            value = mine[...].astype(F32) + self.landed(pack, first)[...].astype(F32)
            value = value + self.landed(pack, second)[...].astype(F32)

            @pl.when(b.z == self.group(pack))
            def _():
                self.total[begin : begin + 128, self.lanes(pack)] = value

            @pl.when(b.z != self.group(pack))
            def _():
                mine[...] = value.astype(BF)

        @pl.when(b.z != self.group(pack))
        def _():
            self.line_copy(pack).start()

    def arrive(self, half, lanes):
        b = self.board
        value = self.total[:, lanes]
        for slot in range(3):
            view = self.line_in.at[slot, :, lanes]
            remote(
                view, view, self.line_s.at[5], self.line_r.at[half * 3 + slot], b.across()
            ).wait_recv()
            value = value + view[...].astype(F32)
        self.total[:, lanes] = value

    def drain(self):
        for pack in range(5):
            for index in range(4):
                self.core_copy(pack, index).wait_send()
            for slot in range(6):
                self.plane_copy(pack, slot).wait_send()

            @pl.when(self.board.z != self.group(pack))
            def _():
                self.line_copy(pack).wait_send()


def split(value):
    high = value.astype(BF)
    return high, (value - high.astype(F32)).astype(BF)


def product(left, right):
    return nn(left[0], right[0]) + (nn(left[0], right[1]) + nn(left[1], right[0]))


class Muon:
    def __init__(self, board, momentum, master, new_momentum, new_master, gram, work, mine,
                 theirs, sems):
        self.board = board
        self.momentum = momentum
        self.master = master
        self.new_momentum = new_momentum
        self.new_master = new_master
        self.gram = gram
        self.work = work
        self.mine = mine
        self.theirs = theirs
        self.core_in = work.at[0:HALF, :]
        self.plane_in = [work.at[HALF + 64 * near : HALF + 64 * near + 64, :] for near in range(3)]
        self.half_s, self.half_r, self.sum_s, self.sum_r, self.all_s, self.all_r, self.back_s, self.back_r = sems

    def part_rows(self, place, core=None):
        core = self.board.core if core is None else core
        return pl.ds(pl.multiple_of(core * HALF + place * 64, 64), 64)

    def half_copy(self):
        b = self.board
        rows = pl.ds(pl.multiple_of((1 - b.core) * HALF, HALF), HALF)
        return remote(
            self.gram.at[rows, :], self.core_in, self.half_s.at[0], self.half_r.at[0], b.across()
        )

    def sum_copy(self, near):
        b = self.board
        return remote(
            self.gram.at[self.part_rows(b.places[near]), :], self.plane_in[near - 1],
            self.sum_s.at[near - 1], self.sum_r.at[near - 1], b.chip(b.z, b.places[near]),
        )

    def all_copy(self, near):
        b = self.board
        view = self.mine.at[pl.ds(pl.multiple_of(b.place * 64, 64), 64), :]
        return remote(
            view, view, self.all_s.at[near - 1], self.all_r.at[near - 1],
            b.chip(b.z, b.places[near]),
        )

    def back_copy(self):
        return remote(
            self.mine, self.theirs, self.back_s.at[0], self.back_r.at[0], self.board.across()
        )

    def begin(self):
        value = 0.5 * self.momentum[...] + self.new_momentum[...]
        self.new_momentum[...] = value
        high, low = split(value)
        self.gram[...] = tn(high, high) + (tn(high, low) + tn(low, high))
        self.half_copy().start()

    def add_core(self):
        b = self.board
        self.half_copy().wait_recv()
        rows = pl.ds(pl.multiple_of(b.core * HALF, HALF), HALF)
        self.gram[rows, :] = self.gram[rows, :] + self.core_in[...]

    def send_sum(self):
        for near in range(1, 4):
            self.sum_copy(near).start()

    def send_all(self):
        b = self.board
        value = self.gram[self.part_rows(b.place), :]
        for near in range(1, 4):
            self.sum_copy(near).wait_recv()
            value = value + self.plane_in[near - 1][...]
        self.mine[pl.ds(pl.multiple_of(b.place * 64, 64), 64), :] = value
        for near in range(1, 4):
            self.all_copy(near).start()

    def wait_all(self):
        for near in range(1, 4):
            self.all_copy(near).wait_recv()

    def keep_half(self):
        rows = pl.ds(pl.multiple_of(self.board.core * HALF, HALF), HALF)
        self.mine[...] = self.gram[rows, :]

    def send_back(self):
        self.back_copy().start()

    def gather(self):
        b = self.board
        self.half_copy().wait_send()

        @pl.when(b.z > 1)
        def _():
            for near in range(1, 4):
                self.sum_copy(near).wait_send()
                self.all_copy(near).wait_send()

        self.back_copy().wait()
        for core, held in ((b.core, self.mine), (1 - b.core, self.theirs)):
            self.gram[pl.ds(pl.multiple_of(core * HALF, HALF), HALF), :] = held[...]

    def iterate(self):
        gram = self.gram
        work = self.work
        current = self.new_master
        row = lax.broadcasted_iota(jnp.int32, (D, D), 0)
        col = lax.broadcasted_iota(jnp.int32, (D, D), 1)
        first = gram[...]
        square = jnp.sum(jnp.where(row == col, first, 0.0), axis=0, keepdims=True)
        divisor = jnp.sqrt(jnp.sum(square, axis=1, keepdims=True)) + 1e-07
        gram[...] = first / (divisor * divisor)
        current[...] = self.new_momentum[...] / divisor

        def polynomial():
            here = split(gram[...])
            diagonal = jnp.where(row == col, NS_A, 0.0)
            work[...] = diagonal + NS_B * gram[...] + NS_C * product(here, here)
            poly = split(work[...])
            current[...] = product(split(current[...]), poly)
            return here, poly

        def turn(step, carry):
            here, poly = polynomial()
            gram[...] = product(split(product(here, poly)), poly)
            return carry

        lax.fori_loop(0, 4, turn, 0)
        polynomial()
        stretch = jnp.where(self.board.z > 1, MUON_RATE * (FF / D) ** 0.5, MUON_RATE)
        current[...] = self.master[...] - stretch * current[...]


class VectorSum:
    def __init__(self, board, own, core_in, plane_in, line_in, total, send, recv):
        self.board = board
        self.own = own
        self.core_in = core_in
        self.plane_in = plane_in
        self.line_in = line_in
        self.total = total
        self.send = send
        self.recv = recv

    def core_copy(self):
        return remote(
            self.own, self.core_in, self.send.at[0], self.recv.at[0], self.board.across()
        )

    def plane_copy(self, near):
        b = self.board
        return remote(
            self.plane_in.at[b.place], self.plane_in.at[b.place], self.send.at[near],
            self.recv.at[near], b.chip(b.z, b.places[near]),
        )

    def line_copy(self, step):
        b = self.board
        return remote(
            self.line_in.at[b.z], self.line_in.at[b.z], self.send.at[3 + step],
            self.recv.at[3 + step], b.chip(lax.rem(b.z + step, 4), b.place),
        )

    def begin(self):
        self.core_copy().start()

    def middle(self):
        b = self.board
        self.core_copy().wait_recv()
        self.plane_in[b.place] = self.own[...] + self.core_in[...]
        for near in range(1, 4):
            self.plane_copy(near).start()

    def late(self):
        b = self.board
        for near in range(1, 4):
            self.plane_copy(near).wait_recv()
        self.line_in[b.z] = (
            (self.plane_in[0] + self.plane_in[1]) + (self.plane_in[2] + self.plane_in[3])
        )
        for step in range(1, 4):
            self.line_copy(step).start()

    def end(self):
        for step in range(1, 4):
            self.line_copy(step).wait_recv()
        value = (self.line_in[0] + self.line_in[1]) + (self.line_in[2] + self.line_in[3])
        self.total[...] = value[: self.total.shape[0], :]
        self.core_copy().wait_send()
        for near in range(1, 4):
            self.plane_copy(near).wait_send()
            self.line_copy(near).wait_send()


def layer_kernel(fused, *refs):
    tok, mem, cot, meta, vec, source, *refs = refs
    if fused:
        old_momentum, *refs = refs
    out_ref, igrad_ref, mgrad_ref, g_ref, gv_ref, *refs = refs
    if fused:
        new_master, *refs = refs
    (
        keys, metas, bias, probs_s, probs_c, flip, q_ref, cq_ref, attn_t, cross_t, grad_t, dq_t,
        parts, arrived, res_a, res_b, send_sem, recv_sem, meta_sem,
    ) = refs[:19]
    core = lax.axis_index("stream")
    other = 1 - core
    own = pl.ds(pl.multiple_of(core * ROWS, ROWS), ROWS)
    theirs = pl.ds(pl.multiple_of(other * ROWS, ROWS), ROWS)
    barrier = pltpu.get_barrier_semaphore()
    gather = scatter = vectors = None
    if fused:
        w, early, core_in, plane_in, line_in, vec_own, vec_core, vec_plane, vec_line = refs[19:28]
        sems = refs[28:]
        board = Board()
        gather = Gather(board, w, *sems[:8])
        scatter = Scatter(board, probs_c, early, core_in, plane_in, line_in, g_ref, sems[8:14])
        vectors = VectorSum(
            board, vec_own, vec_core, vec_plane, vec_line, gv_ref, sems[14], sems[15]
        )
        muon = Muon(
            board, old_momentum, source, g_ref, new_master, bias.at[0:D, :], bias.at[D : 2 * D, :],
            igrad_ref.at[0:HALF, :], igrad_ref.at[HALF:D, :], sems[16:24],
        )
        w[board.half_rows(board.dp), :] = source[...].astype(BF)
        friends = [board.across()]
        friends += [board.chip(board.z, board.places[near]) for near in range(1, 4)]
        friends += [board.chip(lax.rem(board.z + step, 4), board.place) for step in range(1, 4)]
        sums = vec_own
        sums[...] = jnp.zeros_like(sums)
    else:
        w = source
        friends = [{"stream": other}]
        sums = gv_ref
    for friend in friends:
        pl.semaphore_signal(barrier, inc=1, device_id=friend, device_id_type=MESH)
    pl.semaphore_wait(barrier, len(friends))

    def swap(src, dst, index):
        return remote(src, dst, send_sem.at[index], recv_sem.at[index], {"stream": other})

    def weight(index):
        return w[index * D : (index + 1) * D, :]

    def vector(index):
        return vec[index : index + 1, :]

    def gradient(group, index, value):
        if fused:
            ref, first = scatter.home(group)
            rows = pl.ds(pl.multiple_of((group * 4 + index - first) * D, D), D)
            ref[rows, :] = value.astype(BF)
            if group > 0:
                scatter.core_copy(group + 1, index).start()
        else:
            rows = pl.ds(pl.multiple_of((group * 4 + index) * D, D), D)
            g_ref[rows, :] = value.astype(BF)

    meta_copy = remote(meta, metas, meta_sem.at[0], meta_sem.at[1], {"stream": other})
    meta_copy.start()
    if fused:
        gather.first_line()
    hid, _, _ = norm_forward(tok[...].astype(F32), vector(0), vector(1))
    attn_t[...] = hid.astype(BF)

    meta_copy.wait()
    row = lax.broadcasted_iota(jnp.int32, (ROWS, ROWS), 0)
    col = lax.broadcasted_iota(jnp.int32, (ROWS, ROWS), 1)

    def fill_bias(with_priority):
        for rows, held, own_half in ((own, meta, True), (theirs, metas, False)):
            turned = held[...].T
            visible = turned[:, 0:1] == meta[2:3, :]
            if with_priority:
                visible = visible & (turned[:, 1:2] < meta[3:4, :])
            if own_half:
                visible = visible | (row == col)
            bias[rows, :] = jnp.where(visible, 0.0, -1e30)

    fill_bias(True)
    if fused:
        gather.first_plane()
        gather.send_plane(1)
        gather.finish(0)

    copies = [swap(keys.at[index, own, :], keys.at[index, own, :], index) for index in range(4)]
    hid = attn_t[...]
    keys[0, own, :] = nn(hid, weight(1)).astype(BF)
    copies[0].start()
    keys[1, own, :] = (nn(hid, weight(2)) + vector(7)).astype(BF)
    copies[1].start()
    q_ref[...] = (nn(hid, weight(0)) + vector(6)).astype(BF)
    copies[0].wait()
    copies[1].wait()
    flip[...] = keys[1].T
    attend_forward(q_ref, keys.at[0], flip, bias, probs_s, attn_t, (0, 2))
    if fused:
        gather.send_plane(2)
    attend_forward(q_ref, keys.at[0], flip, bias, probs_s, attn_t, (2, 4))
    if fused:
        gather.send_core(1)
        gather.send_plane(3)
    res_one = tok[...].astype(F32) + nn(attn_t[...].T, weight(3)) + vector(8)
    res_a[...] = res_one
    hid, _, _ = norm_forward(res_one, vector(2), vector(3))
    fill_bias(False)
    if fused:
        gather.finish(1)
    keys[2, own, :] = nn(mem[...], weight(5)).astype(BF)
    copies[2].start()
    keys[3, own, :] = (nn(mem[...], weight(6)) + vector(10)).astype(BF)
    copies[3].start()
    cq_ref[...] = (nn(hid.astype(BF), weight(4)) + vector(9)).astype(BF)
    copies[2].wait()
    copies[3].wait()
    flip[...] = keys[3].T
    attend_forward(cq_ref, keys.at[2], flip, bias, probs_c, cross_t, (0, 2))
    if fused:
        gather.send_core(2)
    attend_forward(cq_ref, keys.at[2], flip, bias, probs_c, cross_t, (2, 4))
    if fused:
        gather.send_core(3)
    res_two = res_a[...] + nn(cross_t[...].T, weight(7)) + vector(11)
    res_b[...] = res_two
    hid, _, _ = norm_forward(res_two, vector(4), vector(5))
    grad_t[...] = hid.astype(BF)
    mgrad_ref[...] = jnp.zeros((ROWS, D), F32)
    igrad_ref[...] = res_two + vector(12)
    sums[12:13, :] = column_sum(cot[...])
    if fused:
        gather.finish(2)
        gather.finish(3)

    def ffn_body(part, carry):
        w_in = w[pl.ds(pl.multiple_of(8 * D + part * D, D), D), :]
        w_out = w[pl.ds(pl.multiple_of(8 * D + FF + part * D, D), D), :]
        h_three = grad_t[...]
        pre = nt(h_three, w_in) + vec[pl.ds(13 + part, 1), :]
        hidden = jnp.maximum(pre, 0.0).astype(BF)
        igrad_ref[...] += nn(hidden, w_out)
        grad_pre = jnp.where(pre > 0, nt(cot[...], w_out), 0.0).astype(BF)
        mgrad_ref[...] += nn(grad_pre, w_in)
        sums[pl.ds(13 + part, 1), :] = column_sum(grad_pre)
        gradient(2, part, tn(grad_pre, h_three))
        gradient(3, part, tn(hidden, cot[...]))
        return carry

    lax.fori_loop(0, FF // D, ffn_body, 0)
    out_ref[...] = igrad_ref[...].astype(BF)

    _, normed, spread = norm_forward(res_b[...], vector(4), vector(5))
    grad_in, sums[4:5, :], sums[5:6, :] = norm_backward(normed, spread, vector(4), mgrad_ref[...])
    grad_res = cot[...].astype(F32) + grad_in
    res_b[...] = grad_res
    sums[11:12, :] = column_sum(grad_res)
    dz_two = grad_res.astype(BF)
    grad_t[...] = nt(weight(7), dz_two).astype(BF)
    flip[...] = keys[2].T
    if fused:
        scatter.add_core(3)
        scatter.add_core(4)

    def cross_back(pairs):
        attend_backward(
            cq_ref, flip, keys.at[3], grad_t, cross_t, probs_c, dq_t, parts.at[0], parts.at[1], pairs
        )

    cross_back((0, 2))
    if fused:
        scatter.pass_plane(3)
    cross_back((2, 4))

    def back_copy(index, lanes, sem):
        rows = parts.at[index % 2, theirs, lanes]
        return swap(rows, arrived.at[index % arrived.shape[0], :, lanes], sem)

    whole = slice(0, D)
    back = [back_copy(2, whole, 4), back_copy(3, whole, 5)]
    back[0].start()
    back[1].start()

    def summed(index, lanes):
        mine = parts[index % 2, own, lanes].astype(F32)
        return (mine + arrived[index % arrived.shape[0], :, lanes].astype(F32)).astype(BF)

    if fused:
        scatter.pass_plane(4)
        scatter.end_plane(3)
    grad_cq = dq_t[...].T
    sums[9:10, :] = column_sum(grad_cq)
    hid, normed, spread = norm_forward(res_a[...], vector(2), vector(3))
    grad_in, sums[2:3, :], sums[3:4, :] = norm_backward(
        normed, spread, vector(2), nt(grad_cq, weight(4))
    )
    back[0].wait()
    back[1].wait()
    grad_mk = summed(2, whole)
    grad_mv = summed(3, whole)
    gradient(1, 0, tn(hid.astype(BF), grad_cq))
    gradient(1, 3, nn(cross_t[...], res_b[...].astype(BF)))
    grad_res = res_b[...] + grad_in
    res_b[...] = grad_res
    sums[8:9, :] = column_sum(grad_res)
    sums[10:11, :] = column_sum(grad_mv)
    gradient(1, 1, tn(mem[...], grad_mk))
    gradient(1, 2, tn(mem[...], grad_mv))
    mgrad_ref[...] = nt(grad_mk, weight(5)) + nt(grad_mv, weight(6))
    dz_one = res_b[...].astype(BF)
    grad_t[...] = nt(weight(3), dz_one).astype(BF)
    gradient(0, 3, nn(attn_t[...], dz_one))
    flip[...] = keys[0].T
    if fused:
        scatter.end_plane(4)
        scatter.add_core(2)

    def self_back(pairs):
        attend_backward(
            q_ref, flip, keys.at[1], grad_t, attn_t, probs_s, dq_t, parts.at[0], parts.at[1], pairs
        )

    def send_back(half):
        lanes = slice(half * HALF, half * HALF + HALF)
        both = [back_copy(index, lanes, half * 2 + index) for index in (0, 1)]
        for copy in both:
            copy.start()
        return both

    def first_weights(half, copies):
        lanes = slice(half * HALF, half * HALF + HALF)
        low = norm_forward(tok[...].astype(F32), vector(0), vector(1))[0].astype(BF)
        grad_q = dq_t[lanes, :].T
        sums[6:7, lanes] = column_sum(grad_q)
        values = [grad_q]
        late = scatter.late if fused else g_ref
        late[0:D, lanes] = tn(low, grad_q).astype(BF)
        if fused:
            scatter.core_copy(half, 3).start()
            scatter.core_copy(half, 0).start()
        for index in (0, 1):
            copies[index].wait()
            value = summed(index, lanes)
            values.append(value)
            late[(index + 1) * D : (index + 2) * D, lanes] = tn(low, value).astype(BF)
            if fused:
                scatter.core_copy(half, index + 1).start()
        sums[7:8, lanes] = column_sum(values[2])
        total = None
        for index, value in enumerate(values):
            term = nt(value, w[index * D : (index + 1) * D, lanes])
            total = term if total is None else total + term
        if half == 0:
            res_a[...] = total
        else:
            res_a[...] += total

    if fused:
        wide_plane = board.z > 1
    self_back((0, 1))
    if fused:
        scatter.pass_plane(2)
    self_back((1, 2))
    copies = send_back(0)
    if fused:
        scatter.end_plane(2)

        @pl.when(wide_plane)
        def _():
            scatter.arrive(0, whole)
            muon.begin()

    self_back((2, 3))
    first_weights(0, copies)
    if fused:

        @pl.when(wide_plane)
        def _():
            muon.add_core()
            muon.send_sum()

    self_back((3, 4))
    copies = send_back(1)
    if fused:
        scatter.add_core(0)

        @pl.when(wide_plane)
        def _():
            muon.send_all()

    first_weights(1, copies)
    if fused:
        scatter.pass_plane(0)
        scatter.add_core(1)

        @pl.when(wide_plane)
        def _():
            muon.wait_all()
            muon.send_back()

    _, normed, spread = norm_forward(tok[...].astype(F32), vector(0), vector(1))
    grad_in, sums[0:1, :], sums[1:2, :] = norm_backward(normed, spread, vector(0), res_a[...])
    if fused:
        vectors.begin()
        scatter.end_plane(0)
    res_b[...] += grad_in
    if fused:
        vectors.middle()
        scatter.pass_plane(1)
        scatter.end_plane(1)
        vectors.late()
        narrow = board.z < 2

        @pl.when(board.z == 1)
        def _():
            scatter.arrive(0, whole)

        @pl.when(board.z == 0)
        def _():
            scatter.arrive(0, slice(0, HALF))
            scatter.arrive(1, slice(HALF, D))

        @pl.when(narrow)
        def _():
            muon.begin()
            muon.add_core()
            muon.keep_half()
            muon.send_back()

        muon.gather()
    igrad_ref[...] = res_b[...]
    if fused:
        muon.iterate()
        vectors.end()
        gather.drain()
        scatter.drain()


def layer_call(fused, tok, mem, cot, meta, vec, source, *rest):
    shape = jax.ShapeDtypeStruct
    vmem = pl.BlockSpec(memory_space=pltpu.VMEM)
    dma = pltpu.SemaphoreType.DMA
    scratch = [
        pltpu.VMEM((4, KEYS, D), BF),
        pltpu.VMEM((8, ROWS), jnp.int32),
        pltpu.VMEM((KEYS, ROWS), F32),
        pltpu.VMEM((HEADS * KEYS, ROWS), BF),
        pltpu.VMEM((HEADS * KEYS, ROWS), BF),
        pltpu.VMEM((D, KEYS), BF),
        *[pltpu.VMEM((ROWS, D), BF) for _ in range(6)],
        pltpu.VMEM((2, KEYS, D), BF),
        pltpu.VMEM((2 if fused else 4, ROWS, D), BF),
        *[pltpu.VMEM((ROWS, D), F32) for _ in range(2)],
        dma((8,)), dma((8,)), dma((2,)),
    ]
    if fused:
        scratch += [
            pltpu.VMEM((8 * D + 2 * FF, D), BF),
            pltpu.VMEM((2 * FF, D), BF),
            pltpu.VMEM((8, HALF, D), BF),
            pltpu.VMEM((24, 128, D), BF),
            pltpu.VMEM((3, HALF, D), BF),
            pltpu.VMEM((24, D), F32),
            pltpu.VMEM((24, D), F32),
            pltpu.VMEM((4, 24, D), F32),
            pltpu.VMEM((4, 24, D), F32),
            *[dma((count,)) for count in (4, 4, 4, 4, 15, 15, 16, 16)],
            *[dma((count,)) for count in (20, 20, 30, 30, 6, 6)],
            *[dma((count,)) for count in (7, 7, 1, 1, 3, 3, 3, 3, 1, 1)],
        ]
    grad_shape = shape((HALF, D), F32) if fused else shape(source.shape, BF)
    return pl.pallas_call(
        functools.partial(layer_kernel, fused),
        out_shape=[
            shape((ROWS, D), BF), shape((ROWS, D), F32), shape((ROWS, D), F32),
            grad_shape, shape(vec.shape, F32), *[shape((HALF, D), F32) for _ in rest],
        ],
        in_specs=[vmem] * (6 + len(rest)),
        out_specs=[vmem] * (5 + len(rest)),
        scratch_shapes=scratch,
        compiler_params=pltpu.CompilerParams(
            collective_id=0, has_side_effects=True, vmem_limit_bytes=63 * 1024 * 1024
        ),
        cost_estimate=pl.CostEstimate(
            flops=22_000_000_000, bytes_accessed=24_000_000, transcendentals=8_000_000
        ),
    )(tok, mem, cot, meta, vec, source, *rest)


def partner(block, axis, stride):
    count = lax.axis_size(axis)
    route = []
    for low in range(count):
        high = low | 1 << stride
        if high != low and high < count:
            route += [(low, high), (high, low)]
    return lax.ppermute(block, axis, route)


def high_dot(left_mat, right_mat):
    return jnp.dot(left_mat, right_mat, precision=lax.Precision.HIGH)


def exact_lead(left_mat, right_mat):
    return lax.dot_general(left_mat, right_mat, (((0,), (0,)), ((), ())), precision=HIGH)


def per_device(
    tokens,
    memory,
    cotangent,
    segments,
    padding,
    priority,
    threshold,
    master,
    momentum,
    vectors,
    vec_first,
    vec_second,
    step_count,
):
    meta = jnp.stack([jnp.where(padding == 0, segments, -1), priority, segments, threshold] * 2)
    matrix = vectors.reshape(-1, D)
    if lax.axis_size("dp") == 16 and lax.axis_size("stream") == 2:
        layer_out, input_grad, memory_grad, new_momentum, grad_vec, new_master = layer_call(
            True, tokens, memory, cotangent, meta, matrix, master, momentum
        )
        grad_vec = grad_vec.reshape(-1)
    else:
        low_all = lax.all_gather(master.astype(BF), ("dp", "stream"), axis=0, tiled=True)
        layer_out, input_grad, memory_grad, grad_all, vec_local = layer_call(
            False, tokens, memory, cotangent, meta, matrix, low_all
        )
        grad_rows = lax.psum_scatter(
            grad_all, ("dp", "stream"), scatter_dimension=0, tiled=True
        ).astype(F32)
        grad_vec = lax.psum(vec_local.reshape(-1), ("dp", "stream"))
        opt_rows = master.shape[0]
        device_index = lax.axis_index(("dp", "stream"))
        start_row = device_index * opt_rows
        in_ffn = start_row >= 8 * D
        att_bits = (D // opt_rows).bit_length() - 1
        ffn_bits = (FF // opt_rows).bit_length() - 1
        own_bits = jnp.where(in_ffn, ffn_bits, att_bits)
        new_momentum = 0.5 * momentum + grad_rows

        def gram_total(partial_value):
            for bit_pos in range(ffn_bits):
                other = partner(partial_value, ("dp", "stream"), bit_pos)
                partial_value = partial_value + jnp.where(bit_pos < own_bits, other, 0.0)
            return partial_value

        gram_first = gram_total(exact_lead(new_momentum, new_momentum))
        divisor = jnp.sqrt(jnp.trace(gram_first)) + 1e-07
        gram = gram_first / (divisor * divisor)
        unit = jnp.eye(D, dtype=jnp.float32)
        chain = None
        for turn in range(5):
            poly = NS_A * unit + NS_B * gram + NS_C * high_dot(gram, gram)
            chain = poly if chain is None else high_dot(chain, poly)
            if turn < 4:
                gram = high_dot(high_dot(gram, poly), poly)
        current = high_dot(new_momentum / divisor, chain)
        rate = MUON_RATE * jnp.where(in_ffn, (FF / D) ** 0.5, 1.0)
        new_master = master - rate * current
    count = step_count[0].astype(jnp.float32)
    new_first = 0.5 * vec_first + 0.5 * grad_vec
    new_second = 0.999 * vec_second + 0.001 * grad_vec * grad_vec
    first_fix = new_first / (1.0 - jnp.power(0.5, count))
    second_fix = new_second / (1.0 - jnp.power(0.999, count))
    new_vectors = vectors - ADAM_RATE * (
        first_fix / (jnp.sqrt(second_fix) + 1e-08) + ADAM_DECAY * vectors
    )
    return (
        layer_out,
        input_grad,
        memory_grad,
        new_momentum,
        new_master,
        new_vectors,
        new_first,
        new_second,
    )


def solution(mesh):
    return jax.shard_map(
        per_device,
        mesh=mesh,
        in_specs=(
            P(("dp", "stream"), None),
            P(("dp", "stream"), None),
            P(("dp", "stream"), None),
            P(("dp", "stream")),
            P(("dp", "stream")),
            P(("dp", "stream")),
            P(("dp", "stream")),
            P(("dp", "stream"), None),
            P(("dp", "stream"), None),
            P(),
            P(),
            P(),
            P(),
        ),
        out_specs=(
            P(("dp", "stream"), None),
            P(("dp", "stream"), None),
            P(("dp", "stream"), None),
            P(("dp", "stream"), None),
            P(("dp", "stream"), None),
            P(),
            P(),
            P(),
        ),
        check_vma=False,
    )
```

```python
import functools

import jax
import jax.numpy as jnp
from jax import lax
from jax.experimental import pallas as pl
from jax.experimental.pallas import tpu as pltpu
from jax.sharding import PartitionSpec as P

D = 512
HEADS = 8
HEAD = 64
FF = 2048
ROWS = 512
KEYS = 1024
HALF = 256
BF = jnp.bfloat16
F32 = jnp.float32
SCALE = HEAD ** (-0.5)
LOG2E = 1.4426950408889634
MESH = pl.DeviceIdType.MESH

NS_A = 3.4445
NS_B = -4.775
NS_C = 2.0315
MUON_RATE = 0.8
ADAM_RATE = 0.2
ADAM_DECAY = 0.01
HIGH = lax.Precision.HIGHEST


def nn(left_mat, right_mat):
    return lax.dot_general(
        left_mat, right_mat, (((1,), (0,)), ((), ())), preferred_element_type=F32
    )


def nt(left_mat, right_mat):
    return lax.dot_general(
        left_mat, right_mat, (((1,), (1,)), ((), ())), preferred_element_type=F32
    )


def tn(left_mat, right_mat):
    return lax.dot_general(
        left_mat, right_mat, (((0,), (0,)), ((), ())), preferred_element_type=F32
    )


def norm_forward(values, gain_vec, shift_vec):
    center = values - jnp.mean(values, axis=-1, keepdims=True)
    spread = lax.rsqrt(jnp.mean(center * center, axis=-1, keepdims=True) + 1e-05)
    normed = center * spread
    return normed * gain_vec + shift_vec, normed, spread


def norm_backward(normed, spread, gain_vec, grad_out):
    grad_gain = jnp.sum(grad_out * normed, axis=0, keepdims=True)
    grad_shift = jnp.sum(grad_out, axis=0, keepdims=True)
    scaled = grad_out * gain_vec
    grad_in = spread * (
        scaled
        - jnp.mean(scaled, axis=-1, keepdims=True)
        - normed * jnp.mean(scaled * normed, axis=-1, keepdims=True)
    )
    return grad_in, grad_gain, grad_shift


def column_sum(values):
    return jnp.sum(values.astype(F32), axis=0, keepdims=True)


def half_lanes(values, sub):
    lane = lax.broadcasted_iota(jnp.int32, values.shape, 1)
    keep = lane < HEAD if sub == 0 else lane >= HEAD
    return jnp.where(keep, values, jnp.zeros_like(values))


def head_keys(head):
    return pl.ds(pl.multiple_of(head * KEYS, KEYS), KEYS)


def attend_forward(q_ref, k_ref, value_t, bias, probs, mixed_t, pairs):
    def pair_body(pair, carry):
        lanes = pl.ds(pl.multiple_of(pair * 128, 128), 128)
        keys = k_ref[:, lanes]
        units = [(sub, slice(b, b + ROWS)) for sub in range(2) for b in range(0, ROWS, ROWS)]

        def score(unit):
            sub, cols = unit
            return nt(keys, half_lanes(q_ref[cols, lanes], sub))

        def finish(unit, low):
            sub, cols = unit
            head_rows = pl.ds(pl.multiple_of(pair * 128 + sub * HEAD, HEAD), HEAD)
            mixed_t[head_rows, cols] = nn(value_t[head_rows, :], low).astype(BF)

        def soft(unit, scores):
            sub, cols = unit
            scores = scores * (SCALE * LOG2E) + bias[:, cols]
            expo = jnp.exp2(scores - jnp.max(scores, axis=0, keepdims=True))
            total = jnp.sum(expo, axis=0, keepdims=True)
            low = (expo * (1.0 / total)).astype(BF)
            probs[head_keys(pair * 2 + sub), cols] = low
            return low
        scores = score(units[0])
        for index, unit in enumerate(units):
            after = score(units[index + 1]) if index + 1 < len(units) else None
            finish(unit, soft(unit, scores))
            scores = after
        return carry

    lax.fori_loop(pairs[0], pairs[1], pair_body, 0)


def attend_backward(q_ref, k_t, v_ref, grad_t, mixed_t, probs, dq_t, dk_ref, dv_ref, pairs):
    def pair_body(pair, carry):
        lanes = pl.ds(pl.multiple_of(pair * 128, 128), 128)
        values = v_ref[:, lanes]
        units = [(sub, slice(b, b + ROWS)) for sub in range(2) for b in range(0, ROWS, ROWS)]
        sums = []

        def head_rows(sub):
            return pl.ds(pl.multiple_of(pair * 128 + sub * HEAD, HEAD), HEAD)

        def score(unit):
            sub, cols = unit
            grad = grad_t[head_rows(sub), cols]
            zero = jnp.zeros_like(grad)
            grad_pair = jnp.concatenate([grad, zero] if sub == 0 else [zero, grad], axis=0)
            return grad_pair, nn(values, grad_pair)

        def soft(unit, grad_pair, grad_probs):
            sub, cols = unit
            rows = head_rows(sub)
            inner = jnp.sum(
                grad_t[rows, cols].astype(F32) * mixed_t[rows, cols].astype(F32), axis=0, keepdims=True
            )
            low = probs[head_keys(pair * 2 + sub), cols]
            return low, (low.astype(F32) * (grad_probs - inner)).astype(BF), grad_pair

        def finish(unit, low, grad_scores, grad_pair):
            sub, cols = unit
            rows = head_rows(sub)
            dq_t[rows, cols] = (nn(k_t[rows, :], grad_scores) * SCALE).astype(BF)
            part_k = nn(grad_scores, half_lanes(q_ref[cols, lanes], sub))
            part_v = nn(low, grad_pair.T)
            sums.append((part_k, part_v))
            if len(sums) == 2:
                (k_one, v_one), (k_two, v_two) = sums
                sums[:] = [(k_one + k_two, v_one + v_two)]
        for unit in units:
            finish(unit, *soft(unit, *score(unit)))
        dk_ref[:, lanes] = (sums[0][0] * SCALE).astype(dk_ref.dtype)
        dv_ref[:, lanes] = sums[0][1].astype(dv_ref.dtype)
        return carry

    lax.fori_loop(pairs[0], pairs[1], pair_body, 0)


class Board:
    def __init__(self):
        self.dp = lax.axis_index("dp")
        self.core = lax.axis_index("stream")
        self.z = self.dp // 4
        self.place = self.dp % 4
        x = self.place % 2
        y = self.place // 2
        side_x = self.place + 1 - 2 * x
        side_y = self.place + 2 - 4 * y
        self.places = (self.place, side_x, side_y, 3 - self.place)

    def chip(self, plane, place):
        return {"dp": plane * 4 + place, "stream": self.core}

    def across(self):
        return {"dp": self.dp, "stream": 1 - self.core}

    def half_rows(self, block, core=None, begin=0, count=HALF):
        core = self.core if core is None else core
        return pl.ds(pl.multiple_of(block * D + core * HALF + begin, 64), count)


def remote(src, dst, send, recv, device):
    return pltpu.make_async_remote_copy(
        src_ref=src, dst_ref=dst, send_sem=send, recv_sem=recv,
        device_id=device, device_id_type=MESH,
    )


class Gather:
    def __init__(self, board, w, line_s, line_r, far_s, far_r, first_s, first_r, plane_s,
                 plane_r, core_s, core_r):
        self.board = board
        self.w = w
        self.line = (line_s, line_r)
        self.far = (far_s, far_r)
        self.first = (first_s, first_r)
        self.plane = (plane_s, plane_r)
        self.core = (core_s, core_r)

    def copy(self, rows, sems, send, recv, device):
        view = self.w.at[rows, :]
        return remote(view, view, sems[0].at[send], sems[1].at[recv], device)

    def line_copy(self, part):
        b = self.board
        rows = b.half_rows(b.place, begin=part * 64, count=64)
        return self.copy(rows, self.line, part, part, b.chip(lax.rem(b.z + 1, 4), b.place))

    def far_copy(self, group, plane):
        b = self.board
        rows = b.half_rows(group * 4 + b.place)
        return self.copy(rows, self.far, plane, group, b.chip(plane, b.place))

    def first_copy(self, index):
        b = self.board
        of, near = ((0, 1), (0, 2), (2, 1) if index < 10 else (1, 2))[index // 4]
        rows = b.half_rows(b.places[of], begin=index % 4 * 64, count=64)
        return self.copy(rows, self.first, index, index, b.chip(b.z, b.places[near]))

    def first_core(self, of, part):
        b = self.board
        rows = b.half_rows(b.places[of], begin=part * 128, count=128)
        return self.copy(rows, self.core, of * 2 + part, of * 2 + part, b.across())

    def plane_copy(self, group, index):
        b = self.board
        of, near, begin, count = (
            (0, 1, 0, HALF), (0, 2, 0, HALF), (2, 1, 0, 128), (1, 2, 128, 128)
        )[index]
        rows = b.half_rows(group * 4 + b.places[of], begin=begin, count=count)
        sem = group * 4 - 4 + index
        return self.copy(rows, self.plane, sem, sem, b.chip(b.z, b.places[near]))

    def core_copy(self, group, of):
        b = self.board
        rows = b.half_rows(group * 4 + b.places[of])
        return self.copy(rows, self.core, 4 + group * 4 + of, 4 + group * 4 + of, b.across())

    def first_line(self):
        z = self.board.z

        @pl.when(z == 0)
        def _():
            for part in range(4):
                self.line_copy(part).start()

        for group in (3, 2, 1):
            for plane in range(group):

                @pl.when(z == group)
                def _():
                    self.far_copy(group, plane).start()

        for part in range(4):

            @pl.when(z > 0)
            def _():
                self.line_copy(part).wait_recv()

            @pl.when((z > 0) & (z < 3))
            def _():
                self.line_copy(part).start()

            self.first_copy(part).start()
            self.first_copy(4 + part).start()
            if part in (1, 2):
                self.first_copy(3 + part).wait_recv()
                self.first_copy(7 + part).start()
            if part % 2:
                self.first_core(0, part // 2).start()
        for group in (1, 2):
            for plane in range(group + 1, 4):

                @pl.when(z == group)
                def _():
                    self.far_copy(group, plane).start()

    def first_plane(self):
        for part in range(3):
            self.first_copy(part).wait_recv()
        self.first_copy(10).start()
        self.first_core(1, 0).start()
        self.first_copy(3).wait_recv()
        self.first_copy(11).start()
        self.first_core(1, 1).start()
        self.first_core(2, 0).start()
        self.first_copy(6).wait_recv()
        self.first_copy(7).wait_recv()
        self.first_core(2, 1).start()
        for part in range(2):
            self.first_copy(8 + part * 2).wait_recv()
            self.first_copy(9 + part * 2).wait_recv()
            self.first_core(3, part).start()

    def send_plane(self, group):
        @pl.when(self.board.z != group)
        def _():
            self.far_copy(group, 0).wait_recv()

        for index in range(2):
            self.plane_copy(group, index).start()
        self.core_copy(group, 0).start()

    def pass_plane(self, group):
        for index in range(2):
            self.plane_copy(group, index).wait_recv()
        for index in range(2):
            self.plane_copy(group, 2 + index).start()
            self.core_copy(group, 1 + index).start()

    def send_core(self, group):
        for index in range(2):
            self.plane_copy(group, 2 + index).wait_recv()
        self.core_copy(group, 3).start()

    def finish(self, group):
        if group == 0:
            for of in range(4):
                for part in range(2):
                    self.first_core(of, part).wait_recv()
        else:
            for of in range(4):
                self.core_copy(group, of).wait_recv()

    def drain(self, groups):
        z = self.board.z
        if 0 in groups:
            for part in range(4):

                @pl.when(z < 3)
                def _():
                    self.line_copy(part).wait_send()

            for index in range(12):
                self.first_copy(index).wait_send()
            for of in range(4):
                for part in range(2):
                    self.first_core(of, part).wait_send()
        for group in groups:
            if group > 0:
                for plane in range(4):
                    if plane != group:

                        @pl.when(z == group)
                        def _():
                            self.far_copy(group, plane).wait_send()

                for index in range(4):
                    self.plane_copy(group, index).wait_send()
                    self.core_copy(group, index).wait_send()


class Scatter:
    def __init__(self, board, late, early, core_in, plane_in, line_in, total, sems):
        self.board = board
        self.late = late
        self.early = early
        self.core_in = core_in
        self.plane_in = plane_in
        self.line_in = line_in
        self.total = total
        self.core_s, self.core_r, self.plane_s, self.plane_r, self.line_s, self.line_r = sems

    def group(self, pack):
        return max(pack - 1, 0)

    def lanes(self, pack):
        return slice(0, D) if pack > 1 else slice(pack * HALF, pack * HALF + HALF)

    def home(self, group):
        return (self.late if group < 2 else self.early), 0

    def slot(self, group, index):
        return (4, 0, 0, 4)[group] + index

    def part(self, pack, of, begin, count=128):
        ref, first = self.home(self.group(pack))
        rows = self.board.half_rows(self.group(pack) * 4 + self.board.places[of] - first, None, begin, count)
        return ref.at[rows, self.lanes(pack)]

    def core_copy(self, pack, index):
        b = self.board
        group = self.group(pack)
        ref, first = self.home(group)
        rows = b.half_rows(group * 4 + index - first, core=1 - b.core)
        return remote(
            ref.at[rows, self.lanes(pack)],
            self.core_in.at[self.slot(group, index), :, self.lanes(pack)],
            self.core_s.at[pack * 4 + index], self.core_r.at[pack * 4 + index], b.across(),
        )

    def landed(self, pack, slot):
        return self.plane_in.at[self.group(pack) * 6 + slot, :, self.lanes(pack)]

    def plane_copy(self, pack, slot):
        of, near, begin = ((1, 1, 0), (3, 1, 0), (2, 2, 128), (3, 2, 128), (2, 2, 0), (1, 1, 128))[slot]
        b = self.board
        sem = pack * 6 + slot
        return remote(
            self.part(pack, of, begin), self.landed(pack, slot), self.plane_s.at[sem],
            self.plane_r.at[sem], b.chip(b.z, b.places[near]),
        )

    def line_copy(self, pack):
        b = self.board
        group = self.group(pack)
        slot = lax.rem(b.z - group + 4, 4) - 1
        half = 1 if pack == 1 else 0
        return remote(
            self.part(pack, 0, 0, HALF), self.line_in.at[slot, :, self.lanes(pack)],
            self.line_s.at[pack], self.line_r.at[half * 3 + slot], b.chip(group, b.place),
        )

    def add_core(self, pack):
        b = self.board
        group = self.group(pack)
        ref, first = self.home(group)
        lanes = self.lanes(pack)
        for index in range(4):
            self.core_copy(pack, index).wait_recv()
        for index in range(4):
            rows = b.half_rows(group * 4 + index - first)
            came = self.core_in[self.slot(group, index), :, lanes]
            ref[rows, lanes] = (ref[rows, lanes].astype(F32) + came.astype(F32)).astype(BF)
        for slot in (1, 3, 0, 2):
            self.plane_copy(pack, slot).start()

    def pass_plane(self, pack):
        for slot, of, begin, onward in ((1, 2, 0, 4), (3, 1, 128, 5)):
            self.plane_copy(pack, slot).wait_recv()
            mine = self.part(pack, of, begin)
            mine[...] = (mine[...].astype(F32) + self.landed(pack, slot)[...].astype(F32)).astype(BF)
            self.plane_copy(pack, onward).start()

    def end_plane(self, pack):
        b = self.board
        for begin, first, second in ((0, 0, 4), (128, 2, 5)):
            self.plane_copy(pack, first).wait_recv()
            self.plane_copy(pack, second).wait_recv()
            mine = self.part(pack, 0, begin)
            value = mine[...].astype(F32) + self.landed(pack, first)[...].astype(F32)
            value = value + self.landed(pack, second)[...].astype(F32)

            @pl.when(b.z == self.group(pack))
            def _():
                self.total[begin : begin + 128, self.lanes(pack)] = value

            @pl.when(b.z != self.group(pack))
            def _():
                mine[...] = value.astype(BF)

        @pl.when(b.z != self.group(pack))
        def _():
            self.line_copy(pack).start()

    def arrive(self, half, lanes):
        b = self.board
        value = self.total[:, lanes]
        for slot in range(3):
            view = self.line_in.at[slot, :, lanes]
            remote(
                view, view, self.line_s.at[5], self.line_r.at[half * 3 + slot], b.across()
            ).wait_recv()
            value = value + view[...].astype(F32)
        self.total[:, lanes] = value

    def drain(self):
        for pack in range(5):
            for index in range(4):
                self.core_copy(pack, index).wait_send()
            for slot in range(6):
                self.plane_copy(pack, slot).wait_send()

            @pl.when(self.board.z != self.group(pack))
            def _():
                self.line_copy(pack).wait_send()


def split(value):
    high = value.astype(BF)
    return high, (value - high.astype(F32)).astype(BF)


def product(left, right):
    return nn(left[0], right[0]) + (nn(left[0], right[1]) + nn(left[1], right[0]))


class Muon:
    def __init__(self, board, momentum, master, new_momentum, new_master, gram, work, mine,
                 theirs, sems):
        self.board = board
        self.momentum = momentum
        self.master = master
        self.new_momentum = new_momentum
        self.new_master = new_master
        self.gram = gram
        self.work = work
        self.mine = mine
        self.theirs = theirs
        self.core_in = work.at[0:HALF, :]
        self.plane_in = [work.at[HALF + 64 * near : HALF + 64 * near + 64, :] for near in range(3)]
        self.half_s, self.half_r, self.sum_s, self.sum_r, self.all_s, self.all_r, self.back_s, self.back_r = sems

    def part_rows(self, place, core=None):
        core = self.board.core if core is None else core
        return pl.ds(pl.multiple_of(core * HALF + place * 64, 64), 64)

    def half_copy(self):
        b = self.board
        rows = pl.ds(pl.multiple_of((1 - b.core) * HALF, HALF), HALF)
        return remote(
            self.gram.at[rows, :], self.core_in, self.half_s.at[0], self.half_r.at[0], b.across()
        )

    def sum_copy(self, near):
        b = self.board
        return remote(
            self.gram.at[self.part_rows(b.places[near]), :], self.plane_in[near - 1],
            self.sum_s.at[near - 1], self.sum_r.at[near - 1], b.chip(b.z, b.places[near]),
        )

    def all_copy(self, near):
        b = self.board
        view = self.mine.at[pl.ds(pl.multiple_of(b.place * 64, 64), 64), :]
        return remote(
            view, view, self.all_s.at[near - 1], self.all_r.at[near - 1],
            b.chip(b.z, b.places[near]),
        )

    def back_copy(self):
        return remote(
            self.mine, self.theirs, self.back_s.at[0], self.back_r.at[0], self.board.across()
        )

    def momentum_row(self):
        return 0.5 * self.momentum[...] + self.new_momentum[...]

    def begin(self):
        value = self.momentum_row()
        self.new_momentum[...] = value
        high, low = split(value)
        self.gram[...] = tn(high, high) + (tn(high, low) + tn(low, high))
        self.half_copy().start()

    def add_core(self):
        b = self.board
        self.half_copy().wait_recv()
        rows = pl.ds(pl.multiple_of(b.core * HALF, HALF), HALF)
        self.gram[rows, :] = self.gram[rows, :] + self.core_in[...]

    def send_sum(self):
        for near in range(1, 4):
            self.sum_copy(near).start()

    def send_all(self):
        b = self.board
        value = self.gram[self.part_rows(b.place), :]
        for near in range(1, 4):
            self.sum_copy(near).wait_recv()
            value = value + self.plane_in[near - 1][...]
        self.mine[pl.ds(pl.multiple_of(b.place * 64, 64), 64), :] = value
        for near in range(1, 4):
            self.all_copy(near).start()

    def wait_all(self):
        for near in range(1, 4):
            self.all_copy(near).wait_recv()

    def row_copy(self):
        return remote(
            self.mine, self.theirs, self.half_s.at[0], self.half_r.at[0], self.board.across()
        )

    def pair(self):
        self.mine[...] = self.momentum_row()
        self.row_copy().start()
        self.new_momentum[...] = self.mine[...]
        high, low = split(self.mine[...])
        first = tn(high, high) + (tn(high, low) + tn(low, high))
        self.row_copy().wait_recv()
        high, low = split(self.theirs[...])
        second = tn(high, high) + (tn(high, low) + tn(low, high))
        lower = self.board.core == 0
        self.gram[...] = jnp.where(lower, first, second) + jnp.where(lower, second, first)
        self.row_copy().wait_send()

    def send_back(self):
        self.back_copy().start()

    def gather(self):
        b = self.board
        self.half_copy().wait_send()
        for near in range(1, 4):
            self.sum_copy(near).wait_send()
            self.all_copy(near).wait_send()
        self.back_copy().wait()
        for core, held in ((b.core, self.mine), (1 - b.core, self.theirs)):
            self.gram[pl.ds(pl.multiple_of(core * HALF, HALF), HALF), :] = held[...]

    def iterate(self):
        gram = self.gram
        work = self.work
        current = self.new_master
        row = lax.broadcasted_iota(jnp.int32, (D, D), 0)
        col = lax.broadcasted_iota(jnp.int32, (D, D), 1)
        first = gram[...]
        square = jnp.sum(jnp.where(row == col, first, 0.0), axis=0, keepdims=True)
        divisor = jnp.sqrt(jnp.sum(square, axis=1, keepdims=True)) + 1e-07
        gram[...] = first / (divisor * divisor)
        current[...] = self.new_momentum[...] / divisor

        def polynomial():
            here = split(gram[...])
            diagonal = jnp.where(row == col, NS_A, 0.0)
            work[...] = diagonal + NS_B * gram[...] + NS_C * product(here, here)
            poly = split(work[...])
            current[...] = product(split(current[...]), poly)
            return here, poly

        def turn(step, carry):
            here, poly = polynomial()
            gram[...] = product(split(product(here, poly)), poly)
            return carry

        lax.fori_loop(0, 4, turn, 0)
        polynomial()
        stretch = jnp.where(self.board.z > 1, MUON_RATE * (FF / D) ** 0.5, MUON_RATE)
        current[...] = self.master[...] - stretch * current[...]


class VectorSum:
    def __init__(self, board, own, core_in, plane_in, line_in, total, send, recv):
        self.board = board
        self.own = own
        self.core_in = core_in
        self.plane_in = plane_in
        self.line_in = line_in
        self.total = total
        self.send = send
        self.recv = recv

    def core_copy(self):
        return remote(
            self.own, self.core_in, self.send.at[0], self.recv.at[0], self.board.across()
        )

    def plane_copy(self, near):
        b = self.board
        return remote(
            self.plane_in.at[b.place], self.plane_in.at[b.place], self.send.at[near],
            self.recv.at[near], b.chip(b.z, b.places[near]),
        )

    def line_copy(self, step):
        b = self.board
        return remote(
            self.line_in.at[b.z], self.line_in.at[b.z], self.send.at[3 + step],
            self.recv.at[3 + step], b.chip(lax.rem(b.z + step, 4), b.place),
        )

    def begin(self):
        self.core_copy().start()

    def middle(self):
        b = self.board
        self.core_copy().wait_recv()
        self.plane_in[b.place] = self.own[...] + self.core_in[...]
        for near in range(1, 4):
            self.plane_copy(near).start()

    def late(self):
        b = self.board
        for near in range(1, 4):
            self.plane_copy(near).wait_recv()
        self.line_in[b.z] = (
            (self.plane_in[0] + self.plane_in[1]) + (self.plane_in[2] + self.plane_in[3])
        )
        for step in range(1, 4):
            self.line_copy(step).start()

    def end(self):
        for step in range(1, 4):
            self.line_copy(step).wait_recv()
        value = (self.line_in[0] + self.line_in[1]) + (self.line_in[2] + self.line_in[3])
        self.total[...] = value[: self.total.shape[0], :]
        self.core_copy().wait_send()
        for near in range(1, 4):
            self.plane_copy(near).wait_send()
            self.line_copy(near).wait_send()


def layer_kernel(fused, *refs):
    tok, mem, cot, meta, vec, source, *refs = refs
    if fused:
        old_momentum, *refs = refs
    out_ref, igrad_ref, mgrad_ref, g_ref, gv_ref, *refs = refs
    if fused:
        new_master, *refs = refs
    (
        keys, metas, bias, probs_s, probs_c, flip, q_ref, cq_ref, attn_t, cross_t, grad_t, dq_t,
        parts, arrived, res_a, res_b, send_sem, recv_sem, meta_sem,
    ) = refs[:19]
    core = lax.axis_index("stream")
    other = 1 - core
    own = pl.ds(pl.multiple_of(core * ROWS, ROWS), ROWS)
    theirs = pl.ds(pl.multiple_of(other * ROWS, ROWS), ROWS)
    barrier = pltpu.get_barrier_semaphore()
    gather = scatter = vectors = None
    if fused:
        w, core_in, plane_in, line_in, vec_own, vec_core, vec_plane, vec_line = refs[19:27]
        sems = refs[27:]
        board = Board()
        gather = Gather(board, w, *sems[:10])
        sems = sems[10:]
        scatter = Scatter(board, probs_c, w, core_in, plane_in, line_in, g_ref, sems[:6])
        vectors = VectorSum(
            board, vec_own, vec_core, vec_plane, vec_line, gv_ref, sems[6], sems[7]
        )
        muon = Muon(
            board, old_momentum, source, g_ref, new_master, bias.at[0:D, :], bias.at[D : 2 * D, :],
            igrad_ref.at[0:HALF, :], igrad_ref.at[HALF:D, :], sems[8:],
        )
        w[board.half_rows(board.dp), :] = source[...].astype(BF)
        friends = [board.across()]
        friends += [board.chip(board.z, board.places[near]) for near in range(1, 4)]
        friends += [board.chip(lax.rem(board.z + step, 4), board.place) for step in range(1, 4)]
        sums = vec_own
        sums[...] = jnp.zeros_like(sums)
    else:
        w = source
        friends = [{"stream": other}]
        sums = gv_ref
    for friend in friends:
        pl.semaphore_signal(barrier, inc=1, device_id=friend, device_id_type=MESH)
    pl.semaphore_wait(barrier, len(friends))

    def swap(src, dst, index):
        return remote(src, dst, send_sem.at[index], recv_sem.at[index], {"stream": other})

    def weight(index):
        return w[index * D : (index + 1) * D, :]

    def vector(index):
        return vec[index : index + 1, :]

    def gradient(group, index, value):
        if fused:
            ref, first = scatter.home(group)
            rows = pl.ds(pl.multiple_of((group * 4 + index - first) * D, D), D)
            ref[rows, :] = value.astype(BF)
            if group > 0:
                scatter.core_copy(group + 1, index).start()
        else:
            rows = pl.ds(pl.multiple_of((group * 4 + index) * D, D), D)
            g_ref[rows, :] = value.astype(BF)

    meta_copy = remote(meta, metas, meta_sem.at[0], meta_sem.at[1], {"stream": other})
    meta_copy.start()
    if fused:
        gather.first_line()
    hid, _, _ = norm_forward(tok[...].astype(F32), vector(0), vector(1))
    attn_t[...] = hid.astype(BF)

    meta_copy.wait()
    row = lax.broadcasted_iota(jnp.int32, (ROWS, ROWS), 0)
    col = lax.broadcasted_iota(jnp.int32, (ROWS, ROWS), 1)

    def fill_bias(with_priority):
        for rows, held, own_half in ((own, meta, True), (theirs, metas, False)):
            turned = held[...].T
            visible = turned[:, 0:1] == meta[2:3, :]
            if with_priority:
                visible = visible & (turned[:, 1:2] < meta[3:4, :])
            if own_half:
                visible = visible | (row == col)
            bias[rows, :] = jnp.where(visible, 0.0, -1e30)

    fill_bias(True)
    if fused:
        gather.first_plane()
        gather.send_plane(1)
        gather.finish(0)

    copies = [swap(keys.at[index, own, :], keys.at[index, own, :], index) for index in range(4)]
    hid = attn_t[...]
    keys[0, own, :] = nn(hid, weight(1)).astype(BF)
    copies[0].start()
    keys[1, own, :] = (nn(hid, weight(2)) + vector(7)).astype(BF)
    copies[1].start()
    q_ref[...] = (nn(hid, weight(0)) + vector(6)).astype(BF)
    copies[0].wait()
    copies[1].wait()
    flip[...] = keys[1].T

    def self_forward(pair):
        attend_forward(q_ref, keys.at[0], flip, bias, probs_s, attn_t, (pair, pair + 1))

    self_forward(0)
    if fused:
        gather.pass_plane(1)
    self_forward(1)
    if fused:
        gather.send_plane(2)
    self_forward(2)
    if fused:
        gather.send_core(1)
    self_forward(3)
    res_one = tok[...].astype(F32) + nn(attn_t[...].T, weight(3)) + vector(8)
    res_a[...] = res_one
    hid, _, _ = norm_forward(res_one, vector(2), vector(3))
    fill_bias(False)
    if fused:
        gather.finish(1)
    keys[2, own, :] = nn(mem[...], weight(5)).astype(BF)
    copies[2].start()
    keys[3, own, :] = (nn(mem[...], weight(6)) + vector(10)).astype(BF)
    copies[3].start()
    cq_ref[...] = (nn(hid.astype(BF), weight(4)) + vector(9)).astype(BF)
    copies[2].wait()
    copies[3].wait()
    flip[...] = keys[3].T
    if fused:
        gather.pass_plane(2)
        gather.send_plane(3)

    def cross_forward(pair):
        attend_forward(cq_ref, keys.at[2], flip, bias, probs_c, cross_t, (pair, pair + 1))

    cross_forward(0)
    cross_forward(1)
    if fused:
        gather.send_core(2)
    cross_forward(2)
    cross_forward(3)
    if fused:
        gather.pass_plane(3)
    res_two = res_a[...] + nn(cross_t[...].T, weight(7)) + vector(11)
    res_b[...] = res_two
    hid, _, _ = norm_forward(res_two, vector(4), vector(5))
    grad_t[...] = hid.astype(BF)
    mgrad_ref[...] = jnp.zeros((ROWS, D), F32)
    igrad_ref[...] = res_two + vector(12)
    sums[12:13, :] = column_sum(cot[...])
    if fused:
        gather.send_core(3)
        gather.finish(2)
        gather.finish(3)
        gather.drain((2, 3))

    def ffn_body(part, carry):
        w_in = w[pl.ds(pl.multiple_of(8 * D + part * D, D), D), :]
        w_out = w[pl.ds(pl.multiple_of(8 * D + FF + part * D, D), D), :]
        h_three = grad_t[...]
        pre = nt(h_three, w_in) + vec[pl.ds(13 + part, 1), :]
        hidden = jnp.maximum(pre, 0.0).astype(BF)
        igrad_ref[...] += nn(hidden, w_out)
        grad_pre = jnp.where(pre > 0, nt(cot[...], w_out), 0.0).astype(BF)
        mgrad_ref[...] += nn(grad_pre, w_in)
        sums[pl.ds(13 + part, 1), :] = column_sum(grad_pre)
        gradient(2, part, tn(grad_pre, h_three))
        gradient(3, part, tn(hidden, cot[...]))
        return carry

    lax.fori_loop(0, FF // D, ffn_body, 0)
    out_ref[...] = igrad_ref[...].astype(BF)

    _, normed, spread = norm_forward(res_b[...], vector(4), vector(5))
    grad_in, sums[4:5, :], sums[5:6, :] = norm_backward(normed, spread, vector(4), mgrad_ref[...])
    grad_res = cot[...].astype(F32) + grad_in
    res_b[...] = grad_res
    sums[11:12, :] = column_sum(grad_res)
    dz_two = grad_res.astype(BF)
    grad_t[...] = nt(weight(7), dz_two).astype(BF)
    flip[...] = keys[2].T
    if fused:
        scatter.add_core(3)
        scatter.add_core(4)

    def cross_back(pairs):
        attend_backward(
            cq_ref, flip, keys.at[3], grad_t, cross_t, probs_c, dq_t, parts.at[0], parts.at[1], pairs
        )

    cross_back((0, 2))
    if fused:
        scatter.pass_plane(3)
    cross_back((2, 4))

    def back_copy(index, lanes, sem):
        rows = parts.at[index % 2, theirs, lanes]
        return swap(rows, arrived.at[index % arrived.shape[0], :, lanes], sem)

    whole = slice(0, D)
    back = [back_copy(2, whole, 4), back_copy(3, whole, 5)]
    back[0].start()
    back[1].start()

    def summed(index, lanes):
        mine = parts[index % 2, own, lanes].astype(F32)
        return (mine + arrived[index % arrived.shape[0], :, lanes].astype(F32)).astype(BF)

    if fused:
        scatter.pass_plane(4)
        scatter.end_plane(3)
    grad_cq = dq_t[...].T
    sums[9:10, :] = column_sum(grad_cq)
    hid, normed, spread = norm_forward(res_a[...], vector(2), vector(3))
    grad_in, sums[2:3, :], sums[3:4, :] = norm_backward(
        normed, spread, vector(2), nt(grad_cq, weight(4))
    )
    back[0].wait()
    back[1].wait()
    grad_mk = summed(2, whole)
    grad_mv = summed(3, whole)
    gradient(1, 0, tn(hid.astype(BF), grad_cq))
    gradient(1, 3, nn(cross_t[...], res_b[...].astype(BF)))
    grad_res = res_b[...] + grad_in
    res_b[...] = grad_res
    sums[8:9, :] = column_sum(grad_res)
    sums[10:11, :] = column_sum(grad_mv)
    gradient(1, 1, tn(mem[...], grad_mk))
    gradient(1, 2, tn(mem[...], grad_mv))
    mgrad_ref[...] = nt(grad_mk, weight(5)) + nt(grad_mv, weight(6))
    dz_one = res_b[...].astype(BF)
    grad_t[...] = nt(weight(3), dz_one).astype(BF)
    gradient(0, 3, nn(attn_t[...], dz_one))
    flip[...] = keys[0].T
    if fused:
        scatter.end_plane(4)
        scatter.add_core(2)

    def self_back(pairs):
        attend_backward(
            q_ref, flip, keys.at[1], grad_t, attn_t, probs_s, dq_t, parts.at[0], parts.at[1], pairs
        )

    def send_back(half):
        lanes = slice(half * HALF, half * HALF + HALF)
        both = [back_copy(index, lanes, half * 2 + index) for index in (0, 1)]
        for copy in both:
            copy.start()
        return both

    def first_weights(half, copies):
        lanes = slice(half * HALF, half * HALF + HALF)
        low = norm_forward(tok[...].astype(F32), vector(0), vector(1))[0].astype(BF)
        grad_q = dq_t[lanes, :].T
        sums[6:7, lanes] = column_sum(grad_q)
        values = [grad_q]
        late = scatter.late if fused else g_ref
        late[0:D, lanes] = tn(low, grad_q).astype(BF)
        if fused:
            scatter.core_copy(half, 3).start()
            scatter.core_copy(half, 0).start()
        for index in (0, 1):
            copies[index].wait()
            value = summed(index, lanes)
            values.append(value)
            late[(index + 1) * D : (index + 2) * D, lanes] = tn(low, value).astype(BF)
            if fused:
                scatter.core_copy(half, index + 1).start()
        sums[7:8, lanes] = column_sum(values[2])
        total = None
        for index, value in enumerate(values):
            term = nt(value, w[index * D : (index + 1) * D, lanes])
            total = term if total is None else total + term
        if half == 0:
            res_a[...] = total
        else:
            res_a[...] += total

    if fused:
        wide_plane = board.z > 1
    self_back((0, 1))
    if fused:
        scatter.pass_plane(2)
    self_back((1, 2))
    copies = send_back(0)
    if fused:
        scatter.end_plane(2)

        @pl.when(wide_plane)
        def _():
            scatter.arrive(0, whole)
            muon.begin()

    self_back((2, 3))
    first_weights(0, copies)
    if fused:

        @pl.when(wide_plane)
        def _():
            muon.add_core()
            muon.send_sum()

    self_back((3, 4))
    copies = send_back(1)
    if fused:
        scatter.add_core(0)

        @pl.when(wide_plane)
        def _():
            muon.send_all()

    first_weights(1, copies)
    if fused:
        scatter.pass_plane(0)
        scatter.add_core(1)

        @pl.when(wide_plane)
        def _():
            muon.wait_all()
            muon.send_back()

    _, normed, spread = norm_forward(tok[...].astype(F32), vector(0), vector(1))
    grad_in, sums[0:1, :], sums[1:2, :] = norm_backward(normed, spread, vector(0), res_a[...])
    if fused:
        vectors.begin()
        scatter.end_plane(0)
    res_b[...] += grad_in
    if fused:
        vectors.middle()
        scatter.pass_plane(1)
        scatter.end_plane(1)
        vectors.late()
        narrow = board.z < 2

        @pl.when(board.z == 1)
        def _():
            scatter.arrive(0, whole)

        @pl.when(board.z == 0)
        def _():
            scatter.arrive(0, slice(0, HALF))
            scatter.arrive(1, slice(HALF, D))

        @pl.when(narrow)
        def _():
            muon.pair()

        @pl.when(wide_plane)
        def _():
            muon.gather()

    igrad_ref[...] = res_b[...]
    if fused:
        muon.iterate()
        vectors.end()
        gather.drain((0, 1))
        scatter.drain()


def layer_call(fused, tok, mem, cot, meta, vec, source, *rest):
    shape = jax.ShapeDtypeStruct
    vmem = pl.BlockSpec(memory_space=pltpu.VMEM)
    dma = pltpu.SemaphoreType.DMA
    scratch = [
        pltpu.VMEM((4, KEYS, D), BF),
        pltpu.VMEM((8, ROWS), jnp.int32),
        pltpu.VMEM((KEYS, ROWS), F32),
        pltpu.VMEM((HEADS * KEYS, ROWS), BF),
        pltpu.VMEM((HEADS * KEYS, ROWS), BF),
        pltpu.VMEM((D, KEYS), BF),
        *[pltpu.VMEM((ROWS, D), BF) for _ in range(6)],
        pltpu.VMEM((2, KEYS, D), BF),
        pltpu.VMEM((2 if fused else 4, ROWS, D), BF),
        *[pltpu.VMEM((ROWS, D), F32) for _ in range(2)],
        dma((8,)), dma((8,)), dma((2,)),
    ]
    if fused:
        scratch += [
            pltpu.VMEM((8 * D + 2 * FF, D), BF),
            pltpu.VMEM((8, HALF, D), BF),
            pltpu.VMEM((24, 128, D), BF),
            pltpu.VMEM((3, HALF, D), BF),
            pltpu.VMEM((24, D), F32),
            pltpu.VMEM((24, D), F32),
            pltpu.VMEM((4, 24, D), F32),
            pltpu.VMEM((4, 24, D), F32),
            *[dma((count,)) for count in (4, 4, 4, 4, 12, 12, 12, 12, 20, 20)],
            *[dma((count,)) for count in (20, 20, 30, 30, 6, 6)],
            *[dma((count,)) for count in (7, 7, 1, 1, 3, 3, 3, 3, 1, 1)],
        ]
    grad_shape = shape((HALF, D), F32) if fused else shape(source.shape, BF)
    return pl.pallas_call(
        functools.partial(layer_kernel, fused),
        out_shape=[
            shape((ROWS, D), BF), shape((ROWS, D), F32), shape((ROWS, D), F32),
            grad_shape, shape(vec.shape, F32), *[shape((HALF, D), F32) for _ in rest],
        ],
        in_specs=[vmem] * (6 + len(rest)),
        out_specs=[vmem] * (5 + len(rest)),
        scratch_shapes=scratch,
        compiler_params=pltpu.CompilerParams(
            collective_id=0, has_side_effects=True, vmem_limit_bytes=63 * 1024 * 1024
        ),
        cost_estimate=pl.CostEstimate(
            flops=22_000_000_000, bytes_accessed=24_000_000, transcendentals=8_000_000
        ),
    )(tok, mem, cot, meta, vec, source, *rest)


def copy_kernel(*refs):
    count = len(refs) // 2
    for index in range(count):
        refs[count + index][...] = refs[index][...]


def copy_out(*arrays):
    vmem = pl.BlockSpec(memory_space=pltpu.VMEM)
    return pl.pallas_call(
        copy_kernel,
        out_shape=[jax.ShapeDtypeStruct(array.shape, array.dtype) for array in arrays],
        in_specs=[vmem] * len(arrays),
        out_specs=[vmem] * len(arrays),
        compiler_params=pltpu.CompilerParams(vmem_limit_bytes=62 * 1024 * 1024),
    )(*arrays)


def partner(block, axis, stride):
    count = lax.axis_size(axis)
    route = []
    for low in range(count):
        high = low | 1 << stride
        if high != low and high < count:
            route += [(low, high), (high, low)]
    return lax.ppermute(block, axis, route)


def high_dot(left_mat, right_mat):
    return jnp.dot(left_mat, right_mat, precision=lax.Precision.HIGH)


def exact_lead(left_mat, right_mat):
    return lax.dot_general(left_mat, right_mat, (((0,), (0,)), ((), ())), precision=HIGH)


def per_device(
    tokens,
    memory,
    cotangent,
    segments,
    padding,
    priority,
    threshold,
    master,
    momentum,
    vectors,
    vec_first,
    vec_second,
    step_count,
):
    meta = jnp.stack([jnp.where(padding == 0, segments, -1), priority, segments, threshold] * 2)
    matrix = vectors.reshape(-1, D)
    if lax.axis_size("dp") == 16 and lax.axis_size("stream") == 2:
        layer_out, input_grad, memory_grad, new_momentum, grad_vec, new_master = layer_call(
            True, tokens, memory, cotangent, meta, matrix, master, momentum
        )
        grad_vec = grad_vec.reshape(-1)
        layer_out, input_grad, memory_grad, new_momentum, new_master = copy_out(
            layer_out, input_grad, memory_grad, new_momentum, new_master
        )
    else:
        low_all = lax.all_gather(master.astype(BF), ("dp", "stream"), axis=0, tiled=True)
        layer_out, input_grad, memory_grad, grad_all, vec_local = layer_call(
            False, tokens, memory, cotangent, meta, matrix, low_all
        )
        grad_rows = lax.psum_scatter(
            grad_all, ("dp", "stream"), scatter_dimension=0, tiled=True
        ).astype(F32)
        grad_vec = lax.psum(vec_local.reshape(-1), ("dp", "stream"))
        opt_rows = master.shape[0]
        device_index = lax.axis_index(("dp", "stream"))
        start_row = device_index * opt_rows
        in_ffn = start_row >= 8 * D
        att_bits = (D // opt_rows).bit_length() - 1
        ffn_bits = (FF // opt_rows).bit_length() - 1
        own_bits = jnp.where(in_ffn, ffn_bits, att_bits)
        new_momentum = 0.5 * momentum + grad_rows

        def gram_total(partial_value):
            for bit_pos in range(ffn_bits):
                other = partner(partial_value, ("dp", "stream"), bit_pos)
                partial_value = partial_value + jnp.where(bit_pos < own_bits, other, 0.0)
            return partial_value

        gram_first = gram_total(exact_lead(new_momentum, new_momentum))
        divisor = jnp.sqrt(jnp.trace(gram_first)) + 1e-07
        gram = gram_first / (divisor * divisor)
        unit = jnp.eye(D, dtype=jnp.float32)
        chain = None
        for turn in range(5):
            poly = NS_A * unit + NS_B * gram + NS_C * high_dot(gram, gram)
            chain = poly if chain is None else high_dot(chain, poly)
            if turn < 4:
                gram = high_dot(high_dot(gram, poly), poly)
        current = high_dot(new_momentum / divisor, chain)
        rate = MUON_RATE * jnp.where(in_ffn, (FF / D) ** 0.5, 1.0)
        new_master = master - rate * current
    count = step_count[0].astype(jnp.float32)
    new_first = 0.5 * vec_first + 0.5 * grad_vec
    new_second = 0.999 * vec_second + 0.001 * grad_vec * grad_vec
    first_fix = new_first / (1.0 - jnp.power(0.5, count))
    second_fix = new_second / (1.0 - jnp.power(0.999, count))
    new_vectors = vectors - ADAM_RATE * (
        first_fix / (jnp.sqrt(second_fix) + 1e-08) + ADAM_DECAY * vectors
    )
    return (
        layer_out,
        input_grad,
        memory_grad,
        new_momentum,
        new_master,
        new_vectors,
        new_first,
        new_second,
    )


def solution(mesh):
    return jax.shard_map(
        per_device,
        mesh=mesh,
        in_specs=(
            P(("dp", "stream"), None),
            P(("dp", "stream"), None),
            P(("dp", "stream"), None),
            P(("dp", "stream")),
            P(("dp", "stream")),
            P(("dp", "stream")),
            P(("dp", "stream")),
            P(("dp", "stream"), None),
            P(("dp", "stream"), None),
            P(),
            P(),
            P(),
            P(),
        ),
        out_specs=(
            P(("dp", "stream"), None),
            P(("dp", "stream"), None),
            P(("dp", "stream"), None),
            P(("dp", "stream"), None),
            P(("dp", "stream"), None),
            P(),
            P(),
            P(),
        ),
        check_vma=False,
    )
```

```python
import functools

import jax
import jax.numpy as jnp
from jax import lax
from jax.experimental import pallas as pl
from jax.experimental.pallas import tpu as pltpu
from jax.sharding import PartitionSpec as P

D = 512
HEADS = 8
HEAD = 64
FF = 2048
ROWS = 512
KEYS = 1024
HALF = 256
BF = jnp.bfloat16
F32 = jnp.float32
SCALE = HEAD ** (-0.5)
LOG2E = 1.4426950408889634
MESH = pl.DeviceIdType.MESH

NS_A = 3.4445
NS_B = -4.775
NS_C = 2.0315
MUON_RATE = 0.8
ADAM_RATE = 0.2
ADAM_DECAY = 0.01
HIGH = lax.Precision.HIGHEST


def nn(left_mat, right_mat):
    return lax.dot_general(
        left_mat, right_mat, (((1,), (0,)), ((), ())), preferred_element_type=F32
    )


def nt(left_mat, right_mat):
    return lax.dot_general(
        left_mat, right_mat, (((1,), (1,)), ((), ())), preferred_element_type=F32
    )


def tn(left_mat, right_mat):
    return lax.dot_general(
        left_mat, right_mat, (((0,), (0,)), ((), ())), preferred_element_type=F32
    )


def norm_forward(values, gain_vec, shift_vec):
    center = values - jnp.mean(values, axis=-1, keepdims=True)
    spread = lax.rsqrt(jnp.mean(center * center, axis=-1, keepdims=True) + 1e-05)
    normed = center * spread
    return normed * gain_vec + shift_vec, normed, spread


def norm_backward(normed, spread, gain_vec, grad_out):
    grad_gain = jnp.sum(grad_out * normed, axis=0, keepdims=True)
    grad_shift = jnp.sum(grad_out, axis=0, keepdims=True)
    scaled = grad_out * gain_vec
    grad_in = spread * (
        scaled
        - jnp.mean(scaled, axis=-1, keepdims=True)
        - normed * jnp.mean(scaled * normed, axis=-1, keepdims=True)
    )
    return grad_in, grad_gain, grad_shift


def column_sum(values):
    return jnp.sum(values.astype(F32), axis=0, keepdims=True)


def half_lanes(values, sub):
    lane = lax.broadcasted_iota(jnp.int32, values.shape, 1)
    keep = lane < HEAD if sub == 0 else lane >= HEAD
    return jnp.where(keep, values, jnp.zeros_like(values))


def head_keys(head):
    return pl.ds(pl.multiple_of(head * KEYS, KEYS), KEYS)


def attend_forward(q_ref, k_ref, value_t, bias, probs, mixed_t, pairs):
    def pair_body(pair, carry):
        lanes = pl.ds(pl.multiple_of(pair * 128, 128), 128)
        keys = k_ref[:, lanes]
        units = [(sub, slice(b, b + ROWS)) for sub in range(2) for b in range(0, ROWS, ROWS)]

        def score(unit):
            sub, cols = unit
            return nt(keys, half_lanes(q_ref[cols, lanes], sub))

        def finish(unit, low):
            sub, cols = unit
            head_rows = pl.ds(pl.multiple_of(pair * 128 + sub * HEAD, HEAD), HEAD)
            mixed_t[head_rows, cols] = nn(value_t[head_rows, :], low).astype(BF)

        def soft(unit, scores):
            sub, cols = unit
            scores = scores * (SCALE * LOG2E) + bias[:, cols]
            expo = jnp.exp2(scores - jnp.max(scores, axis=0, keepdims=True))
            total = jnp.sum(expo, axis=0, keepdims=True)
            low = (expo * (1.0 / total)).astype(BF)
            probs[head_keys(pair * 2 + sub), cols] = low
            return low
        scores = score(units[0])
        for index, unit in enumerate(units):
            after = score(units[index + 1]) if index + 1 < len(units) else None
            finish(unit, soft(unit, scores))
            scores = after
        return carry

    lax.fori_loop(pairs[0], pairs[1], pair_body, 0)


def attend_backward(q_ref, k_t, v_ref, grad_t, mixed_t, probs, dq_t, dk_ref, dv_ref, pairs):
    def pair_body(pair, carry):
        lanes = pl.ds(pl.multiple_of(pair * 128, 128), 128)
        values = v_ref[:, lanes]
        units = [(sub, slice(b, b + ROWS)) for sub in range(2) for b in range(0, ROWS, ROWS)]
        sums = []

        def head_rows(sub):
            return pl.ds(pl.multiple_of(pair * 128 + sub * HEAD, HEAD), HEAD)

        def score(unit):
            sub, cols = unit
            grad = grad_t[head_rows(sub), cols]
            zero = jnp.zeros_like(grad)
            grad_pair = jnp.concatenate([grad, zero] if sub == 0 else [zero, grad], axis=0)
            return grad_pair, nn(values, grad_pair)

        def soft(unit, grad_pair, grad_probs):
            sub, cols = unit
            rows = head_rows(sub)
            inner = jnp.sum(
                grad_t[rows, cols].astype(F32) * mixed_t[rows, cols].astype(F32), axis=0, keepdims=True
            )
            low = probs[head_keys(pair * 2 + sub), cols]
            return low, (low.astype(F32) * (grad_probs - inner)).astype(BF), grad_pair

        def finish(unit, low, grad_scores, grad_pair):
            sub, cols = unit
            rows = head_rows(sub)
            dq_t[rows, cols] = (nn(k_t[rows, :], grad_scores) * SCALE).astype(BF)
            part_k = nn(grad_scores, half_lanes(q_ref[cols, lanes], sub))
            part_v = nn(low, grad_pair.T)
            sums.append((part_k, part_v))
            if len(sums) == 2:
                (k_one, v_one), (k_two, v_two) = sums
                sums[:] = [(k_one + k_two, v_one + v_two)]
        for unit in units:
            finish(unit, *soft(unit, *score(unit)))
        dk_ref[:, lanes] = (sums[0][0] * SCALE).astype(dk_ref.dtype)
        dv_ref[:, lanes] = sums[0][1].astype(dv_ref.dtype)
        return carry

    lax.fori_loop(pairs[0], pairs[1], pair_body, 0)


class Board:
    def __init__(self):
        self.dp = lax.axis_index("dp")
        self.core = lax.axis_index("stream")
        self.z = self.dp // 4
        self.place = self.dp % 4
        x = self.place % 2
        y = self.place // 2
        side_x = self.place + 1 - 2 * x
        side_y = self.place + 2 - 4 * y
        self.places = (self.place, side_x, side_y, 3 - self.place)

    def chip(self, plane, place):
        return {"dp": plane * 4 + place, "stream": self.core}

    def across(self):
        return {"dp": self.dp, "stream": 1 - self.core}

    def half_rows(self, block, core=None, begin=0, count=HALF):
        core = self.core if core is None else core
        return pl.ds(pl.multiple_of(block * D + core * HALF + begin, 64), count)


def remote(src, dst, send, recv, device):
    return pltpu.make_async_remote_copy(
        src_ref=src, dst_ref=dst, send_sem=send, recv_sem=recv,
        device_id=device, device_id_type=MESH,
    )


class Gather:
    def __init__(self, board, w, line_s, line_r, far_s, far_r, first_s, first_r, plane_s,
                 plane_r, core_s, core_r):
        self.board = board
        self.w = w
        self.line = (line_s, line_r)
        self.far = (far_s, far_r)
        self.first = (first_s, first_r)
        self.plane = (plane_s, plane_r)
        self.core = (core_s, core_r)

    def copy(self, rows, sems, send, recv, device):
        view = self.w.at[rows, :]
        return remote(view, view, sems[0].at[send], sems[1].at[recv], device)

    def line_copy(self, part):
        b = self.board
        rows = b.half_rows(b.place, begin=part * 64, count=64)
        return self.copy(rows, self.line, part, part, b.chip(lax.rem(b.z + 1, 4), b.place))

    def far_copy(self, group, plane):
        b = self.board
        rows = b.half_rows(group * 4 + b.place)
        return self.copy(rows, self.far, plane, group, b.chip(plane, b.place))

    def first_copy(self, index):
        b = self.board
        of, near = ((0, 1), (0, 2), (2, 1) if index < 10 else (1, 2))[index // 4]
        rows = b.half_rows(b.places[of], begin=index % 4 * 64, count=64)
        return self.copy(rows, self.first, index, index, b.chip(b.z, b.places[near]))

    def first_core(self, of, part):
        b = self.board
        rows = b.half_rows(b.places[of], begin=part * 128, count=128)
        return self.copy(rows, self.core, of * 2 + part, of * 2 + part, b.across())

    def plane_copy(self, group, index):
        b = self.board
        of, near, begin, count = (
            (0, 1, 0, HALF), (0, 2, 0, HALF), (2, 1, 0, 128), (1, 2, 128, 128)
        )[index]
        rows = b.half_rows(group * 4 + b.places[of], begin=begin, count=count)
        sem = group * 4 - 4 + index
        return self.copy(rows, self.plane, sem, sem, b.chip(b.z, b.places[near]))

    def core_copy(self, group, of):
        b = self.board
        rows = b.half_rows(group * 4 + b.places[of])
        return self.copy(rows, self.core, 4 + group * 4 + of, 4 + group * 4 + of, b.across())

    def first_line(self):
        z = self.board.z

        @pl.when(z == 0)
        def _():
            for part in range(4):
                self.line_copy(part).start()

        for group in (3, 2, 1):
            for plane in range(group):

                @pl.when(z == group)
                def _():
                    self.far_copy(group, plane).start()

        for part in range(4):

            @pl.when(z > 0)
            def _():
                self.line_copy(part).wait_recv()

            @pl.when((z > 0) & (z < 3))
            def _():
                self.line_copy(part).start()

            self.first_copy(part).start()
            self.first_copy(4 + part).start()
            if part in (1, 2):
                self.first_copy(3 + part).wait_recv()
                self.first_copy(7 + part).start()
            if part % 2:
                self.first_core(0, part // 2).start()
        for group in (1, 2):
            for plane in range(group + 1, 4):

                @pl.when(z == group)
                def _():
                    self.far_copy(group, plane).start()

    def first_plane(self):
        for part in range(3):
            self.first_copy(part).wait_recv()
        self.first_copy(10).start()
        self.first_core(1, 0).start()
        self.first_copy(3).wait_recv()
        self.first_copy(11).start()
        self.first_core(1, 1).start()
        self.first_core(2, 0).start()
        self.first_copy(6).wait_recv()
        self.first_copy(7).wait_recv()
        self.first_core(2, 1).start()
        for part in range(2):
            self.first_copy(8 + part * 2).wait_recv()
            self.first_copy(9 + part * 2).wait_recv()
            self.first_core(3, part).start()

    def send_plane(self, group):
        @pl.when(self.board.z != group)
        def _():
            self.far_copy(group, 0).wait_recv()

        for index in range(2):
            self.plane_copy(group, index).start()
        self.core_copy(group, 0).start()

    def pass_plane(self, group):
        for index in range(2):
            self.plane_copy(group, index).wait_recv()
        for index in range(2):
            self.plane_copy(group, 2 + index).start()
            self.core_copy(group, 1 + index).start()

    def send_core(self, group):
        for index in range(2):
            self.plane_copy(group, 2 + index).wait_recv()
        self.core_copy(group, 3).start()

    def finish(self, group):
        if group == 0:
            for of in range(4):
                for part in range(2):
                    self.first_core(of, part).wait_recv()
        else:
            for of in range(4):
                self.core_copy(group, of).wait_recv()

    def drain(self, groups):
        z = self.board.z
        if 0 in groups:
            for part in range(4):

                @pl.when(z < 3)
                def _():
                    self.line_copy(part).wait_send()

            for index in range(12):
                self.first_copy(index).wait_send()
            for of in range(4):
                for part in range(2):
                    self.first_core(of, part).wait_send()
        for group in groups:
            if group > 0:
                for plane in range(4):
                    if plane != group:

                        @pl.when(z == group)
                        def _():
                            self.far_copy(group, plane).wait_send()

                for index in range(4):
                    self.plane_copy(group, index).wait_send()
                    self.core_copy(group, index).wait_send()


class Scatter:
    def __init__(self, board, late, early, core_in, plane_in, line_in, total, sems):
        self.board = board
        self.late = late
        self.early = early
        self.core_in = core_in
        self.plane_in = plane_in
        self.line_in = line_in
        self.total = total
        self.core_s, self.core_r, self.plane_s, self.plane_r, self.line_s, self.line_r = sems

    def group(self, pack):
        return max(pack - 1, 0)

    def lanes(self, pack):
        return slice(0, D) if pack > 1 else slice(pack * HALF, pack * HALF + HALF)

    def home(self, group):
        return (self.late if group < 2 else self.early), 0

    def slot(self, group, index):
        return (4, 0, 0, 4)[group] + index

    def part(self, pack, of, begin, count=128):
        ref, first = self.home(self.group(pack))
        rows = self.board.half_rows(self.group(pack) * 4 + self.board.places[of] - first, None, begin, count)
        return ref.at[rows, self.lanes(pack)]

    def core_copy(self, pack, index):
        b = self.board
        group = self.group(pack)
        ref, first = self.home(group)
        rows = b.half_rows(group * 4 + index - first, core=1 - b.core)
        return remote(
            ref.at[rows, self.lanes(pack)],
            self.core_in.at[self.slot(group, index), :, self.lanes(pack)],
            self.core_s.at[pack * 4 + index], self.core_r.at[pack * 4 + index], b.across(),
        )

    def landed(self, pack, slot):
        return self.plane_in.at[self.group(pack) * 6 + slot, :, self.lanes(pack)]

    def plane_copy(self, pack, slot):
        of, near, begin = ((1, 1, 0), (3, 1, 0), (2, 2, 128), (3, 2, 128), (2, 2, 0), (1, 1, 128))[slot]
        b = self.board
        sem = pack * 6 + slot
        return remote(
            self.part(pack, of, begin), self.landed(pack, slot), self.plane_s.at[sem],
            self.plane_r.at[sem], b.chip(b.z, b.places[near]),
        )

    def line_copy(self, pack):
        b = self.board
        group = self.group(pack)
        slot = lax.rem(b.z - group + 4, 4) - 1
        half = 1 if pack == 1 else 0
        return remote(
            self.part(pack, 0, 0, HALF), self.line_in.at[slot, :, self.lanes(pack)],
            self.line_s.at[pack], self.line_r.at[half * 3 + slot], b.chip(group, b.place),
        )

    def add_core(self, pack):
        b = self.board
        group = self.group(pack)
        ref, first = self.home(group)
        lanes = self.lanes(pack)
        for index in range(4):
            self.core_copy(pack, index).wait_recv()
        for index in range(4):
            rows = b.half_rows(group * 4 + index - first)
            came = self.core_in[self.slot(group, index), :, lanes]
            ref[rows, lanes] = (ref[rows, lanes].astype(F32) + came.astype(F32)).astype(BF)
        for slot in (1, 3, 0, 2):
            self.plane_copy(pack, slot).start()

    def pass_plane(self, pack):
        for slot, of, begin, onward in ((1, 2, 0, 4), (3, 1, 128, 5)):
            self.plane_copy(pack, slot).wait_recv()
            mine = self.part(pack, of, begin)
            mine[...] = (mine[...].astype(F32) + self.landed(pack, slot)[...].astype(F32)).astype(BF)
            self.plane_copy(pack, onward).start()

    def end_plane(self, pack):
        b = self.board
        for begin, first, second in ((0, 0, 4), (128, 2, 5)):
            self.plane_copy(pack, first).wait_recv()
            self.plane_copy(pack, second).wait_recv()
            mine = self.part(pack, 0, begin)
            value = mine[...].astype(F32) + self.landed(pack, first)[...].astype(F32)
            value = value + self.landed(pack, second)[...].astype(F32)

            @pl.when(b.z == self.group(pack))
            def _():
                self.total[begin : begin + 128, self.lanes(pack)] = value

            @pl.when(b.z != self.group(pack))
            def _():
                mine[...] = value.astype(BF)

        @pl.when(b.z != self.group(pack))
        def _():
            self.line_copy(pack).start()

    def arrive(self, half, lanes):
        b = self.board
        value = self.total[:, lanes]
        for slot in range(3):
            view = self.line_in.at[slot, :, lanes]
            remote(
                view, view, self.line_s.at[5], self.line_r.at[half * 3 + slot], b.across()
            ).wait_recv()
            value = value + view[...].astype(F32)
        self.total[:, lanes] = value

    def drain(self):
        for pack in range(5):
            for index in range(4):
                self.core_copy(pack, index).wait_send()
            for slot in range(6):
                self.plane_copy(pack, slot).wait_send()

            @pl.when(self.board.z != self.group(pack))
            def _():
                self.line_copy(pack).wait_send()


def split(value):
    high = value.astype(BF)
    return high, (value - high.astype(F32)).astype(BF)


def product(left, right):
    return nn(left[0], right[0]) + (nn(left[0], right[1]) + nn(left[1], right[0]))


class Muon:
    def __init__(self, board, momentum, master, new_momentum, new_master, gram, work, mine,
                 theirs, sems):
        self.board = board
        self.momentum = momentum
        self.master = master
        self.new_momentum = new_momentum
        self.new_master = new_master
        self.gram = gram
        self.work = work
        self.mine = mine
        self.theirs = theirs
        self.core_in = work.at[0:HALF, :]
        self.plane_in = [work.at[HALF + 64 * near : HALF + 64 * near + 64, :] for near in range(3)]
        self.half_s, self.half_r, self.sum_s, self.sum_r, self.all_s, self.all_r, self.back_s, self.back_r = sems

    def part_rows(self, place, core=None):
        core = self.board.core if core is None else core
        return pl.ds(pl.multiple_of(core * HALF + place * 64, 64), 64)

    def half_copy(self):
        b = self.board
        rows = pl.ds(pl.multiple_of((1 - b.core) * HALF, HALF), HALF)
        return remote(
            self.gram.at[rows, :], self.core_in, self.half_s.at[0], self.half_r.at[0], b.across()
        )

    def sum_copy(self, near):
        b = self.board
        return remote(
            self.gram.at[self.part_rows(b.places[near]), :], self.plane_in[near - 1],
            self.sum_s.at[near - 1], self.sum_r.at[near - 1], b.chip(b.z, b.places[near]),
        )

    def all_copy(self, near):
        b = self.board
        view = self.mine.at[pl.ds(pl.multiple_of(b.place * 64, 64), 64), :]
        return remote(
            view, view, self.all_s.at[near - 1], self.all_r.at[near - 1],
            b.chip(b.z, b.places[near]),
        )

    def back_copy(self):
        return remote(
            self.mine, self.theirs, self.back_s.at[0], self.back_r.at[0], self.board.across()
        )

    def momentum_row(self):
        return 0.5 * self.momentum[...] + self.new_momentum[...]

    def begin(self):
        value = self.momentum_row()
        self.new_momentum[...] = value
        high, low = split(value)
        self.gram[...] = tn(high, high) + (tn(high, low) + tn(low, high))
        self.half_copy().start()

    def add_core(self):
        b = self.board
        self.half_copy().wait_recv()
        rows = pl.ds(pl.multiple_of(b.core * HALF, HALF), HALF)
        self.gram[rows, :] = self.gram[rows, :] + self.core_in[...]

    def send_sum(self):
        for near in range(1, 4):
            self.sum_copy(near).start()

    def send_all(self):
        b = self.board
        value = self.gram[self.part_rows(b.place), :]
        for near in range(1, 4):
            self.sum_copy(near).wait_recv()
            value = value + self.plane_in[near - 1][...]
        self.mine[pl.ds(pl.multiple_of(b.place * 64, 64), 64), :] = value
        for near in range(1, 4):
            self.all_copy(near).start()

    def wait_all(self):
        for near in range(1, 4):
            self.all_copy(near).wait_recv()

    def row_copy(self):
        return remote(
            self.mine, self.theirs, self.half_s.at[0], self.half_r.at[0], self.board.across()
        )

    def pair(self):
        self.mine[...] = self.momentum_row()
        self.row_copy().start()
        self.new_momentum[...] = self.mine[...]
        high, low = split(self.mine[...])
        first = tn(high, high) + (tn(high, low) + tn(low, high))
        self.row_copy().wait_recv()
        high, low = split(self.theirs[...])
        second = tn(high, high) + (tn(high, low) + tn(low, high))
        lower = self.board.core == 0
        self.gram[...] = jnp.where(lower, first, second) + jnp.where(lower, second, first)
        self.row_copy().wait_send()

    def send_back(self):
        self.back_copy().start()

    def gather(self):
        b = self.board
        self.half_copy().wait_send()
        for near in range(1, 4):
            self.sum_copy(near).wait_send()
            self.all_copy(near).wait_send()
        self.back_copy().wait()
        for core, held in ((b.core, self.mine), (1 - b.core, self.theirs)):
            self.gram[pl.ds(pl.multiple_of(core * HALF, HALF), HALF), :] = held[...]

    def iterate(self):
        gram = self.gram
        work = self.work
        current = self.new_master
        row = lax.broadcasted_iota(jnp.int32, (D, D), 0)
        col = lax.broadcasted_iota(jnp.int32, (D, D), 1)
        first = gram[...]
        square = jnp.sum(jnp.where(row == col, first, 0.0), axis=0, keepdims=True)
        divisor = jnp.sqrt(jnp.sum(square, axis=1, keepdims=True)) + 1e-07
        gram[...] = first / (divisor * divisor)
        current[...] = self.new_momentum[...] / divisor

        def polynomial():
            here = split(gram[...])
            diagonal = jnp.where(row == col, NS_A, 0.0)
            work[...] = diagonal + NS_B * gram[...] + NS_C * product(here, here)
            poly = split(work[...])
            current[...] = product(split(current[...]), poly)
            return here, poly

        def turn(step, carry):
            here, poly = polynomial()
            gram[...] = product(split(product(here, poly)), poly)
            return carry

        lax.fori_loop(0, 4, turn, 0)
        polynomial()
        stretch = jnp.where(self.board.z > 1, MUON_RATE * (FF / D) ** 0.5, MUON_RATE)
        current[...] = self.master[...] - stretch * current[...]


class VectorSum:
    def __init__(self, board, own, core_in, plane_in, line_in, total, send, recv):
        self.board = board
        self.own = own
        self.core_in = core_in
        self.plane_in = plane_in
        self.line_in = line_in
        self.total = total
        self.send = send
        self.recv = recv

    def core_copy(self):
        return remote(
            self.own, self.core_in, self.send.at[0], self.recv.at[0], self.board.across()
        )

    def plane_copy(self, near):
        b = self.board
        return remote(
            self.plane_in.at[b.place], self.plane_in.at[b.place], self.send.at[near],
            self.recv.at[near], b.chip(b.z, b.places[near]),
        )

    def line_copy(self, step):
        b = self.board
        return remote(
            self.line_in.at[b.z], self.line_in.at[b.z], self.send.at[3 + step],
            self.recv.at[3 + step], b.chip(lax.rem(b.z + step, 4), b.place),
        )

    def begin(self):
        self.core_copy().start()

    def middle(self):
        b = self.board
        self.core_copy().wait_recv()
        self.plane_in[b.place] = self.own[...] + self.core_in[...]
        for near in range(1, 4):
            self.plane_copy(near).start()

    def late(self):
        b = self.board
        for near in range(1, 4):
            self.plane_copy(near).wait_recv()
        self.line_in[b.z] = (
            (self.plane_in[0] + self.plane_in[1]) + (self.plane_in[2] + self.plane_in[3])
        )
        for step in range(1, 4):
            self.line_copy(step).start()

    def end(self):
        for step in range(1, 4):
            self.line_copy(step).wait_recv()
        value = (self.line_in[0] + self.line_in[1]) + (self.line_in[2] + self.line_in[3])
        self.total[...] = value[: self.total.shape[0], :]
        self.core_copy().wait_send()
        for near in range(1, 4):
            self.plane_copy(near).wait_send()
            self.line_copy(near).wait_send()


def layer_kernel(fused, *refs):
    tok, mem, cot, meta, vec, source, *refs = refs
    if fused:
        old_momentum, *refs = refs
    out_ref, igrad_ref, mgrad_ref, g_ref, gv_ref, *refs = refs
    if fused:
        new_master, *refs = refs
    (
        keys, metas, bias, probs_s, probs_c, flip, q_ref, cq_ref, attn_t, cross_t, grad_t, dq_t,
        parts, arrived, res_a, res_b, send_sem, recv_sem, meta_sem,
    ) = refs[:19]
    core = lax.axis_index("stream")
    other = 1 - core
    own = pl.ds(pl.multiple_of(core * ROWS, ROWS), ROWS)
    theirs = pl.ds(pl.multiple_of(other * ROWS, ROWS), ROWS)
    barrier = pltpu.get_barrier_semaphore()
    gather = scatter = vectors = None
    if fused:
        w, core_in, plane_in, line_in, vec_own, vec_core, vec_plane, vec_line = refs[19:27]
        sems = refs[27:]
        board = Board()
        gather = Gather(board, w, *sems[:10])
        sems = sems[10:]
        scatter = Scatter(board, probs_c, w, core_in, plane_in, line_in, g_ref, sems[:6])
        vectors = VectorSum(
            board, vec_own, vec_core, vec_plane, vec_line, gv_ref, sems[6], sems[7]
        )
        muon = Muon(
            board, old_momentum, source, g_ref, new_master, bias.at[0:D, :], bias.at[D : 2 * D, :],
            igrad_ref.at[0:HALF, :], igrad_ref.at[HALF:D, :], sems[8:],
        )
        w[board.half_rows(board.dp), :] = source[...].astype(BF)
        friends = [board.across()]
        friends += [board.chip(board.z, board.places[near]) for near in range(1, 4)]
        friends += [board.chip(lax.rem(board.z + step, 4), board.place) for step in range(1, 4)]
        sums = vec_own
        sums[...] = jnp.zeros_like(sums)
    else:
        w = source
        friends = [{"stream": other}]
        sums = gv_ref
    for friend in friends:
        pl.semaphore_signal(barrier, inc=1, device_id=friend, device_id_type=MESH)
    pl.semaphore_wait(barrier, len(friends))

    def swap(src, dst, index):
        return remote(src, dst, send_sem.at[index], recv_sem.at[index], {"stream": other})

    def weight(index):
        return w[index * D : (index + 1) * D, :]

    def vector(index):
        return vec[index : index + 1, :]

    def gradient(group, index, value):
        if fused:
            ref, first = scatter.home(group)
            rows = pl.ds(pl.multiple_of((group * 4 + index - first) * D, D), D)
            ref[rows, :] = value.astype(BF)
            if group > 0:
                scatter.core_copy(group + 1, index).start()
        else:
            rows = pl.ds(pl.multiple_of((group * 4 + index) * D, D), D)
            g_ref[rows, :] = value.astype(BF)

    meta_copy = remote(meta, metas, meta_sem.at[0], meta_sem.at[1], {"stream": other})
    meta_copy.start()
    if fused:
        gather.first_line()
    hid, _, _ = norm_forward(tok[...].astype(F32), vector(0), vector(1))
    attn_t[...] = hid.astype(BF)

    meta_copy.wait()
    row = lax.broadcasted_iota(jnp.int32, (ROWS, ROWS), 0)
    col = lax.broadcasted_iota(jnp.int32, (ROWS, ROWS), 1)

    def fill_bias(with_priority):
        for rows, held, own_half in ((own, meta, True), (theirs, metas, False)):
            turned = held[...].T
            visible = turned[:, 0:1] == meta[2:3, :]
            if with_priority:
                visible = visible & (turned[:, 1:2] < meta[3:4, :])
            if own_half:
                visible = visible | (row == col)
            bias[rows, :] = jnp.where(visible, 0.0, -1e30)

    fill_bias(True)
    if fused:
        gather.first_plane()
        gather.send_plane(1)
        gather.finish(0)

    copies = [swap(keys.at[index, own, :], keys.at[index, own, :], index) for index in range(4)]
    hid = attn_t[...]
    keys[0, own, :] = nn(hid, weight(1)).astype(BF)
    copies[0].start()
    keys[1, own, :] = (nn(hid, weight(2)) + vector(7)).astype(BF)
    copies[1].start()
    q_ref[...] = (nn(hid, weight(0)) + vector(6)).astype(BF)
    copies[0].wait()
    copies[1].wait()
    flip[...] = keys[1].T

    def self_forward(pair):
        attend_forward(q_ref, keys.at[0], flip, bias, probs_s, attn_t, (pair, pair + 1))

    self_forward(0)
    if fused:
        gather.pass_plane(1)
        gather.send_plane(2)
    self_forward(1)
    self_forward(2)
    if fused:
        gather.send_core(1)
    self_forward(3)
    if fused:
        gather.pass_plane(2)
        gather.send_plane(3)
    res_one = tok[...].astype(F32) + nn(attn_t[...].T, weight(3)) + vector(8)
    res_a[...] = res_one
    hid, _, _ = norm_forward(res_one, vector(2), vector(3))
    fill_bias(False)
    if fused:
        gather.finish(1)
    keys[2, own, :] = nn(mem[...], weight(5)).astype(BF)
    copies[2].start()
    keys[3, own, :] = (nn(mem[...], weight(6)) + vector(10)).astype(BF)
    copies[3].start()
    cq_ref[...] = (nn(hid.astype(BF), weight(4)) + vector(9)).astype(BF)
    copies[2].wait()
    copies[3].wait()
    flip[...] = keys[3].T
    def cross_forward(pair):
        attend_forward(cq_ref, keys.at[2], flip, bias, probs_c, cross_t, (pair, pair + 1))

    cross_forward(0)
    if fused:
        gather.send_core(2)
    cross_forward(1)
    cross_forward(2)
    if fused:
        gather.pass_plane(3)
    cross_forward(3)
    res_two = res_a[...] + nn(cross_t[...].T, weight(7)) + vector(11)
    res_b[...] = res_two
    hid, _, _ = norm_forward(res_two, vector(4), vector(5))
    grad_t[...] = hid.astype(BF)
    mgrad_ref[...] = jnp.zeros((ROWS, D), F32)
    igrad_ref[...] = res_two + vector(12)
    sums[12:13, :] = column_sum(cot[...])
    if fused:
        gather.send_core(3)
        gather.finish(2)
        gather.finish(3)
        gather.drain((2, 3))

    def ffn_body(part, carry):
        w_in = w[pl.ds(pl.multiple_of(8 * D + part * D, D), D), :]
        w_out = w[pl.ds(pl.multiple_of(8 * D + FF + part * D, D), D), :]
        h_three = grad_t[...]
        pre = nt(h_three, w_in) + vec[pl.ds(13 + part, 1), :]
        hidden = jnp.maximum(pre, 0.0).astype(BF)
        igrad_ref[...] += nn(hidden, w_out)
        grad_pre = jnp.where(pre > 0, nt(cot[...], w_out), 0.0).astype(BF)
        mgrad_ref[...] += nn(grad_pre, w_in)
        sums[pl.ds(13 + part, 1), :] = column_sum(grad_pre)
        gradient(2, part, tn(grad_pre, h_three))
        gradient(3, part, tn(hidden, cot[...]))
        return carry

    lax.fori_loop(0, FF // D, ffn_body, 0)
    out_ref[...] = igrad_ref[...].astype(BF)

    _, normed, spread = norm_forward(res_b[...], vector(4), vector(5))
    grad_in, sums[4:5, :], sums[5:6, :] = norm_backward(normed, spread, vector(4), mgrad_ref[...])
    grad_res = cot[...].astype(F32) + grad_in
    res_b[...] = grad_res
    sums[11:12, :] = column_sum(grad_res)
    dz_two = grad_res.astype(BF)
    grad_t[...] = nt(weight(7), dz_two).astype(BF)
    flip[...] = keys[2].T
    if fused:
        scatter.add_core(3)
        scatter.add_core(4)

    def cross_back(pairs):
        attend_backward(
            cq_ref, flip, keys.at[3], grad_t, cross_t, probs_c, dq_t, parts.at[0], parts.at[1], pairs
        )

    cross_back((0, 4))

    def back_copy(index, lanes, sem):
        rows = parts.at[index % 2, theirs, lanes]
        return swap(rows, arrived.at[index % arrived.shape[0], :, lanes], sem)

    whole = slice(0, D)
    back = [back_copy(2, whole, 4), back_copy(3, whole, 5)]
    back[0].start()
    back[1].start()

    def summed(index, lanes):
        mine = parts[index % 2, own, lanes].astype(F32)
        return (mine + arrived[index % arrived.shape[0], :, lanes].astype(F32)).astype(BF)

    if fused:
        scatter.pass_plane(3)
    grad_cq = dq_t[...].T
    sums[9:10, :] = column_sum(grad_cq)
    hid, normed, spread = norm_forward(res_a[...], vector(2), vector(3))
    grad_in, sums[2:3, :], sums[3:4, :] = norm_backward(
        normed, spread, vector(2), nt(grad_cq, weight(4))
    )
    back[0].wait()
    back[1].wait()
    grad_mk = summed(2, whole)
    grad_mv = summed(3, whole)
    gradient(1, 0, tn(hid.astype(BF), grad_cq))
    gradient(1, 3, nn(cross_t[...], res_b[...].astype(BF)))
    grad_res = res_b[...] + grad_in
    res_b[...] = grad_res
    sums[8:9, :] = column_sum(grad_res)
    sums[10:11, :] = column_sum(grad_mv)
    gradient(1, 1, tn(mem[...], grad_mk))
    gradient(1, 2, tn(mem[...], grad_mv))
    mgrad_ref[...] = nt(grad_mk, weight(5)) + nt(grad_mv, weight(6))
    dz_one = res_b[...].astype(BF)
    grad_t[...] = nt(weight(3), dz_one).astype(BF)
    gradient(0, 3, nn(attn_t[...], dz_one))
    flip[...] = keys[0].T
    if fused:
        scatter.pass_plane(4)
        scatter.end_plane(3)
        scatter.add_core(2)

    def self_back(pairs):
        attend_backward(
            q_ref, flip, keys.at[1], grad_t, attn_t, probs_s, dq_t, parts.at[0], parts.at[1], pairs
        )

    def send_back(half):
        lanes = slice(half * HALF, half * HALF + HALF)
        both = [back_copy(index, lanes, half * 2 + index) for index in (0, 1)]
        for copy in both:
            copy.start()
        return both

    def first_weights(half, copies):
        lanes = slice(half * HALF, half * HALF + HALF)
        low = norm_forward(tok[...].astype(F32), vector(0), vector(1))[0].astype(BF)
        grad_q = dq_t[lanes, :].T
        sums[6:7, lanes] = column_sum(grad_q)
        values = [grad_q]
        late = scatter.late if fused else g_ref
        late[0:D, lanes] = tn(low, grad_q).astype(BF)
        if fused:
            scatter.core_copy(half, 3).start()
            scatter.core_copy(half, 0).start()
        for index in (0, 1):
            copies[index].wait()
            value = summed(index, lanes)
            values.append(value)
            late[(index + 1) * D : (index + 2) * D, lanes] = tn(low, value).astype(BF)
            if fused:
                scatter.core_copy(half, index + 1).start()
        sums[7:8, lanes] = column_sum(values[2])
        total = None
        for index, value in enumerate(values):
            term = nt(value, w[index * D : (index + 1) * D, lanes])
            total = term if total is None else total + term
        if half == 0:
            res_a[...] = total
        else:
            res_a[...] += total

    self_back((0, 2))
    copies = send_back(0)
    if fused:
        scatter.end_plane(4)
    self_back((2, 3))
    first_weights(0, copies)
    if fused:
        scatter.pass_plane(2)
    self_back((3, 4))
    copies = send_back(1)
    if fused:
        scatter.add_core(0)
    first_weights(1, copies)
    if fused:
        scatter.add_core(1)
        scatter.pass_plane(0)
        scatter.end_plane(2)
    _, normed, spread = norm_forward(tok[...].astype(F32), vector(0), vector(1))
    grad_in, sums[0:1, :], sums[1:2, :] = norm_backward(normed, spread, vector(0), res_a[...])
    res_b[...] += grad_in
    if fused:
        vectors.begin()
        wide_plane = board.z > 1
        scatter.end_plane(0)

        @pl.when(wide_plane)
        def _():
            scatter.arrive(0, whole)
            muon.begin()

        scatter.pass_plane(1)
        vectors.middle()

        @pl.when(wide_plane)
        def _():
            muon.add_core()
            muon.send_sum()

        scatter.end_plane(1)
        vectors.late()

        @pl.when(board.z == 1)
        def _():
            scatter.arrive(0, whole)

        @pl.when(board.z == 0)
        def _():
            scatter.arrive(0, slice(0, HALF))
            scatter.arrive(1, slice(HALF, D))

        @pl.when(board.z < 2)
        def _():
            muon.pair()

        @pl.when(wide_plane)
        def _():
            muon.send_all()
            muon.wait_all()
            muon.send_back()
            muon.gather()

    igrad_ref[...] = res_b[...]
    if fused:
        muon.iterate()
        vectors.end()
        gather.drain((0, 1))
        scatter.drain()


def layer_call(fused, tok, mem, cot, meta, vec, source, *rest):
    shape = jax.ShapeDtypeStruct
    vmem = pl.BlockSpec(memory_space=pltpu.VMEM)
    dma = pltpu.SemaphoreType.DMA
    scratch = [
        pltpu.VMEM((4, KEYS, D), BF),
        pltpu.VMEM((8, ROWS), jnp.int32),
        pltpu.VMEM((KEYS, ROWS), F32),
        pltpu.VMEM((HEADS * KEYS, ROWS), BF),
        pltpu.VMEM((HEADS * KEYS, ROWS), BF),
        pltpu.VMEM((D, KEYS), BF),
        *[pltpu.VMEM((ROWS, D), BF) for _ in range(6)],
        pltpu.VMEM((2, KEYS, D), BF),
        pltpu.VMEM((2 if fused else 4, ROWS, D), BF),
        *[pltpu.VMEM((ROWS, D), F32) for _ in range(2)],
        dma((8,)), dma((8,)), dma((2,)),
    ]
    if fused:
        scratch += [
            pltpu.VMEM((8 * D + 2 * FF, D), BF),
            pltpu.VMEM((8, HALF, D), BF),
            pltpu.VMEM((24, 128, D), BF),
            pltpu.VMEM((3, HALF, D), BF),
            pltpu.VMEM((24, D), F32),
            pltpu.VMEM((24, D), F32),
            pltpu.VMEM((4, 24, D), F32),
            pltpu.VMEM((4, 24, D), F32),
            *[dma((count,)) for count in (4, 4, 4, 4, 12, 12, 12, 12, 20, 20)],
            *[dma((count,)) for count in (20, 20, 30, 30, 6, 6)],
            *[dma((count,)) for count in (7, 7, 1, 1, 3, 3, 3, 3, 1, 1)],
        ]
    grad_shape = shape((HALF, D), F32) if fused else shape(source.shape, BF)
    return pl.pallas_call(
        functools.partial(layer_kernel, fused),
        out_shape=[
            shape((ROWS, D), BF), shape((ROWS, D), F32), shape((ROWS, D), F32),
            grad_shape, shape(vec.shape, F32), *[shape((HALF, D), F32) for _ in rest],
        ],
        in_specs=[vmem] * (6 + len(rest)),
        out_specs=[vmem] * (5 + len(rest)),
        scratch_shapes=scratch,
        compiler_params=pltpu.CompilerParams(
            collective_id=0, has_side_effects=True, vmem_limit_bytes=63 * 1024 * 1024
        ),
        cost_estimate=pl.CostEstimate(
            flops=22_000_000_000, bytes_accessed=24_000_000, transcendentals=8_000_000
        ),
    )(tok, mem, cot, meta, vec, source, *rest)


def copy_kernel(*refs):
    count = len(refs) // 2
    for index in range(count):
        refs[count + index][...] = refs[index][...]


def copy_out(*arrays):
    vmem = pl.BlockSpec(memory_space=pltpu.VMEM)
    return pl.pallas_call(
        copy_kernel,
        out_shape=[jax.ShapeDtypeStruct(array.shape, array.dtype) for array in arrays],
        in_specs=[vmem] * len(arrays),
        out_specs=[vmem] * len(arrays),
        compiler_params=pltpu.CompilerParams(vmem_limit_bytes=62 * 1024 * 1024),
    )(*arrays)


def partner(block, axis, stride):
    count = lax.axis_size(axis)
    route = []
    for low in range(count):
        high = low | 1 << stride
        if high != low and high < count:
            route += [(low, high), (high, low)]
    return lax.ppermute(block, axis, route)


def high_dot(left_mat, right_mat):
    return jnp.dot(left_mat, right_mat, precision=lax.Precision.HIGH)


def exact_lead(left_mat, right_mat):
    return lax.dot_general(left_mat, right_mat, (((0,), (0,)), ((), ())), precision=HIGH)


def per_device(
    tokens,
    memory,
    cotangent,
    segments,
    padding,
    priority,
    threshold,
    master,
    momentum,
    vectors,
    vec_first,
    vec_second,
    step_count,
):
    meta = jnp.stack([jnp.where(padding == 0, segments, -1), priority, segments, threshold] * 2)
    matrix = vectors.reshape(-1, D)
    if lax.axis_size("dp") == 16 and lax.axis_size("stream") == 2:
        layer_out, input_grad, memory_grad, new_momentum, grad_vec, new_master = layer_call(
            True, tokens, memory, cotangent, meta, matrix, master, momentum
        )
        grad_vec = grad_vec.reshape(-1)
        layer_out, input_grad, memory_grad, new_momentum, new_master = copy_out(
            layer_out, input_grad, memory_grad, new_momentum, new_master
        )
    else:
        low_all = lax.all_gather(master.astype(BF), ("dp", "stream"), axis=0, tiled=True)
        layer_out, input_grad, memory_grad, grad_all, vec_local = layer_call(
            False, tokens, memory, cotangent, meta, matrix, low_all
        )
        grad_rows = lax.psum_scatter(
            grad_all, ("dp", "stream"), scatter_dimension=0, tiled=True
        ).astype(F32)
        grad_vec = lax.psum(vec_local.reshape(-1), ("dp", "stream"))
        opt_rows = master.shape[0]
        device_index = lax.axis_index(("dp", "stream"))
        start_row = device_index * opt_rows
        in_ffn = start_row >= 8 * D
        att_bits = (D // opt_rows).bit_length() - 1
        ffn_bits = (FF // opt_rows).bit_length() - 1
        own_bits = jnp.where(in_ffn, ffn_bits, att_bits)
        new_momentum = 0.5 * momentum + grad_rows

        def gram_total(partial_value):
            for bit_pos in range(ffn_bits):
                other = partner(partial_value, ("dp", "stream"), bit_pos)
                partial_value = partial_value + jnp.where(bit_pos < own_bits, other, 0.0)
            return partial_value

        gram_first = gram_total(exact_lead(new_momentum, new_momentum))
        divisor = jnp.sqrt(jnp.trace(gram_first)) + 1e-07
        gram = gram_first / (divisor * divisor)
        unit = jnp.eye(D, dtype=jnp.float32)
        chain = None
        for turn in range(5):
            poly = NS_A * unit + NS_B * gram + NS_C * high_dot(gram, gram)
            chain = poly if chain is None else high_dot(chain, poly)
            if turn < 4:
                gram = high_dot(high_dot(gram, poly), poly)
        current = high_dot(new_momentum / divisor, chain)
        rate = MUON_RATE * jnp.where(in_ffn, (FF / D) ** 0.5, 1.0)
        new_master = master - rate * current
    count = step_count[0].astype(jnp.float32)
    new_first = 0.5 * vec_first + 0.5 * grad_vec
    new_second = 0.999 * vec_second + 0.001 * grad_vec * grad_vec
    first_fix = new_first / (1.0 - jnp.power(0.5, count))
    second_fix = new_second / (1.0 - jnp.power(0.999, count))
    new_vectors = vectors - ADAM_RATE * (
        first_fix / (jnp.sqrt(second_fix) + 1e-08) + ADAM_DECAY * vectors
    )
    return (
        layer_out,
        input_grad,
        memory_grad,
        new_momentum,
        new_master,
        new_vectors,
        new_first,
        new_second,
    )


def solution(mesh):
    return jax.shard_map(
        per_device,
        mesh=mesh,
        in_specs=(
            P(("dp", "stream"), None),
            P(("dp", "stream"), None),
            P(("dp", "stream"), None),
            P(("dp", "stream")),
            P(("dp", "stream")),
            P(("dp", "stream")),
            P(("dp", "stream")),
            P(("dp", "stream"), None),
            P(("dp", "stream"), None),
            P(),
            P(),
            P(),
            P(),
        ),
        out_specs=(
            P(("dp", "stream"), None),
            P(("dp", "stream"), None),
            P(("dp", "stream"), None),
            P(("dp", "stream"), None),
            P(("dp", "stream"), None),
            P(),
            P(),
            P(),
        ),
        check_vma=False,
    )
```

```python
import functools

import jax
import jax.numpy as jnp
from jax import lax
from jax.experimental import pallas as pl
from jax.experimental.pallas import tpu as pltpu
from jax.sharding import PartitionSpec as P

D = 512
HEADS = 8
HEAD = 64
FF = 2048
ROWS = 512
KEYS = 1024
HALF = 256
BF = jnp.bfloat16
F32 = jnp.float32
SCALE = HEAD ** (-0.5)
LOG2E = 1.4426950408889634
MESH = pl.DeviceIdType.MESH

NS_A = 3.4445
NS_B = -4.775
NS_C = 2.0315
MUON_RATE = 0.8
ADAM_RATE = 0.2
ADAM_DECAY = 0.01
HIGH = lax.Precision.HIGHEST


def nn(left_mat, right_mat):
    return lax.dot_general(
        left_mat, right_mat, (((1,), (0,)), ((), ())), preferred_element_type=F32
    )


def nt(left_mat, right_mat):
    return lax.dot_general(
        left_mat, right_mat, (((1,), (1,)), ((), ())), preferred_element_type=F32
    )


def tn(left_mat, right_mat):
    return lax.dot_general(
        left_mat, right_mat, (((0,), (0,)), ((), ())), preferred_element_type=F32
    )


def norm_forward(values, gain_vec, shift_vec):
    center = values - jnp.mean(values, axis=-1, keepdims=True)
    spread = lax.rsqrt(jnp.mean(center * center, axis=-1, keepdims=True) + 1e-05)
    normed = center * spread
    return normed * gain_vec + shift_vec, normed, spread


def norm_backward(normed, spread, gain_vec, grad_out):
    grad_gain = jnp.sum(grad_out * normed, axis=0, keepdims=True)
    grad_shift = jnp.sum(grad_out, axis=0, keepdims=True)
    scaled = grad_out * gain_vec
    grad_in = spread * (
        scaled
        - jnp.mean(scaled, axis=-1, keepdims=True)
        - normed * jnp.mean(scaled * normed, axis=-1, keepdims=True)
    )
    return grad_in, grad_gain, grad_shift


def column_sum(values):
    return jnp.sum(values.astype(F32), axis=0, keepdims=True)


def half_lanes(values, sub):
    lane = lax.broadcasted_iota(jnp.int32, values.shape, 1)
    keep = lane < HEAD if sub == 0 else lane >= HEAD
    return jnp.where(keep, values, jnp.zeros_like(values))


def head_keys(head):
    return pl.ds(pl.multiple_of(head * KEYS, KEYS), KEYS)


def attend_forward(q_ref, k_ref, value_t, bias, probs, mixed_t, pairs):
    def pair_body(pair, carry):
        lanes = pl.ds(pl.multiple_of(pair * 128, 128), 128)
        keys = k_ref[:, lanes]
        units = [(sub, slice(b, b + ROWS)) for sub in range(2) for b in range(0, ROWS, ROWS)]

        def score(unit):
            sub, cols = unit
            return nt(keys, half_lanes(q_ref[cols, lanes], sub))

        def finish(unit, low):
            sub, cols = unit
            head_rows = pl.ds(pl.multiple_of(pair * 128 + sub * HEAD, HEAD), HEAD)
            mixed_t[head_rows, cols] = nn(value_t[head_rows, :], low).astype(BF)

        def soft(unit, scores):
            sub, cols = unit
            scores = scores * (SCALE * LOG2E) + bias[:, cols]
            expo = jnp.exp2(scores - jnp.max(scores, axis=0, keepdims=True))
            total = jnp.sum(expo, axis=0, keepdims=True)
            low = (expo * (1.0 / total)).astype(BF)
            probs[head_keys(pair * 2 + sub), cols] = low
            return low
        scores = score(units[0])
        for index, unit in enumerate(units):
            after = score(units[index + 1]) if index + 1 < len(units) else None
            finish(unit, soft(unit, scores))
            scores = after
        return carry

    lax.fori_loop(pairs[0], pairs[1], pair_body, 0)


def attend_backward(q_ref, k_t, v_ref, grad_t, mixed_t, probs, dq_t, dk_ref, dv_ref, pairs):
    def pair_body(pair, carry):
        lanes = pl.ds(pl.multiple_of(pair * 128, 128), 128)
        values = v_ref[:, lanes]
        units = [(sub, slice(b, b + ROWS)) for sub in range(2) for b in range(0, ROWS, ROWS)]
        sums = []

        def head_rows(sub):
            return pl.ds(pl.multiple_of(pair * 128 + sub * HEAD, HEAD), HEAD)

        def score(unit):
            sub, cols = unit
            grad = grad_t[head_rows(sub), cols]
            zero = jnp.zeros_like(grad)
            grad_pair = jnp.concatenate([grad, zero] if sub == 0 else [zero, grad], axis=0)
            return grad_pair, nn(values, grad_pair)

        def soft(unit, grad_pair, grad_probs):
            sub, cols = unit
            rows = head_rows(sub)
            inner = jnp.sum(
                grad_t[rows, cols].astype(F32) * mixed_t[rows, cols].astype(F32), axis=0, keepdims=True
            )
            low = probs[head_keys(pair * 2 + sub), cols]
            return low, (low.astype(F32) * (grad_probs - inner)).astype(BF), grad_pair

        def finish(unit, low, grad_scores, grad_pair):
            sub, cols = unit
            rows = head_rows(sub)
            dq_t[rows, cols] = (nn(k_t[rows, :], grad_scores) * SCALE).astype(BF)
            part_k = nn(grad_scores, half_lanes(q_ref[cols, lanes], sub))
            part_v = nn(low, grad_pair.T)
            sums.append((part_k, part_v))
            if len(sums) == 2:
                (k_one, v_one), (k_two, v_two) = sums
                sums[:] = [(k_one + k_two, v_one + v_two)]
        for unit in units:
            finish(unit, *soft(unit, *score(unit)))
        dk_ref[:, lanes] = (sums[0][0] * SCALE).astype(dk_ref.dtype)
        dv_ref[:, lanes] = sums[0][1].astype(dv_ref.dtype)
        return carry

    lax.fori_loop(pairs[0], pairs[1], pair_body, 0)


class Board:
    def __init__(self):
        self.dp = lax.axis_index("dp")
        self.core = lax.axis_index("stream")
        self.z = self.dp // 4
        self.place = self.dp % 4
        x = self.place % 2
        y = self.place // 2
        side_x = self.place + 1 - 2 * x
        side_y = self.place + 2 - 4 * y
        self.places = (self.place, side_x, side_y, 3 - self.place)

    def chip(self, plane, place):
        return {"dp": plane * 4 + place, "stream": self.core}

    def across(self):
        return {"dp": self.dp, "stream": 1 - self.core}

    def half_rows(self, block, core=None, begin=0, count=HALF):
        core = self.core if core is None else core
        return pl.ds(pl.multiple_of(block * D + core * HALF + begin, 64), count)


def remote(src, dst, send, recv, device):
    return pltpu.make_async_remote_copy(
        src_ref=src, dst_ref=dst, send_sem=send, recv_sem=recv,
        device_id=device, device_id_type=MESH,
    )


class Gather:
    def __init__(self, board, w, line_s, line_r, far_s, far_r, first_s, first_r, plane_s,
                 plane_r, core_s, core_r):
        self.board = board
        self.w = w
        self.line = (line_s, line_r)
        self.far = (far_s, far_r)
        self.first = (first_s, first_r)
        self.plane = (plane_s, plane_r)
        self.core = (core_s, core_r)

    def copy(self, rows, sems, send, recv, device):
        view = self.w.at[rows, :]
        return remote(view, view, sems[0].at[send], sems[1].at[recv], device)

    def line_copy(self, part):
        b = self.board
        rows = b.half_rows(b.place, begin=part * 64, count=64)
        return self.copy(rows, self.line, part, part, b.chip(lax.rem(b.z + 1, 4), b.place))

    def far_copy(self, group, plane):
        b = self.board
        rows = b.half_rows(group * 4 + b.place)
        return self.copy(rows, self.far, plane, group, b.chip(plane, b.place))

    def first_copy(self, index):
        b = self.board
        of, near = ((0, 1), (0, 2), (2, 1) if index < 10 else (1, 2))[index // 4]
        rows = b.half_rows(b.places[of], begin=index % 4 * 64, count=64)
        return self.copy(rows, self.first, index, index, b.chip(b.z, b.places[near]))

    def first_core(self, of, part):
        b = self.board
        rows = b.half_rows(b.places[of], begin=part * 128, count=128)
        return self.copy(rows, self.core, of * 2 + part, of * 2 + part, b.across())

    def plane_copy(self, group, index):
        b = self.board
        of, near, begin, count = (
            (0, 1, 0, HALF), (0, 2, 0, HALF), (2, 1, 0, 128), (1, 2, 128, 128)
        )[index]
        rows = b.half_rows(group * 4 + b.places[of], begin=begin, count=count)
        sem = group * 4 - 4 + index
        return self.copy(rows, self.plane, sem, sem, b.chip(b.z, b.places[near]))

    def core_copy(self, group, of):
        b = self.board
        rows = b.half_rows(group * 4 + b.places[of])
        return self.copy(rows, self.core, 4 + group * 4 + of, 4 + group * 4 + of, b.across())

    def first_line(self):
        z = self.board.z

        @pl.when(z == 0)
        def _():
            for part in range(4):
                self.line_copy(part).start()

        for group in (3, 2, 1):
            for plane in range(group):

                @pl.when(z == group)
                def _():
                    self.far_copy(group, plane).start()

        for part in range(4):

            @pl.when(z > 0)
            def _():
                self.line_copy(part).wait_recv()

            @pl.when((z > 0) & (z < 3))
            def _():
                self.line_copy(part).start()

            self.first_copy(part).start()
            self.first_copy(4 + part).start()
            if part in (1, 2):
                self.first_copy(3 + part).wait_recv()
                self.first_copy(7 + part).start()
            if part % 2:
                self.first_core(0, part // 2).start()
        for group in (1, 2):
            for plane in range(group + 1, 4):

                @pl.when(z == group)
                def _():
                    self.far_copy(group, plane).start()

    def first_plane(self):
        for part in range(3):
            self.first_copy(part).wait_recv()
        self.first_copy(10).start()
        self.first_core(1, 0).start()
        self.first_copy(3).wait_recv()
        self.first_copy(11).start()
        self.first_core(1, 1).start()
        self.first_core(2, 0).start()
        self.first_copy(6).wait_recv()
        self.first_copy(7).wait_recv()
        self.first_core(2, 1).start()
        for part in range(2):
            self.first_copy(8 + part * 2).wait_recv()
            self.first_copy(9 + part * 2).wait_recv()
            self.first_core(3, part).start()

    def send_plane(self, group):
        @pl.when(self.board.z != group)
        def _():
            self.far_copy(group, 0).wait_recv()

        for index in range(2):
            self.plane_copy(group, index).start()
        self.core_copy(group, 0).start()

    def pass_plane(self, group):
        for index in range(2):
            self.plane_copy(group, index).wait_recv()
        for index in range(2):
            self.plane_copy(group, 2 + index).start()
            self.core_copy(group, 1 + index).start()

    def send_core(self, group):
        for index in range(2):
            self.plane_copy(group, 2 + index).wait_recv()
        self.core_copy(group, 3).start()

    def finish(self, group):
        if group == 0:
            for of in range(4):
                for part in range(2):
                    self.first_core(of, part).wait_recv()
        else:
            for of in range(4):
                self.core_copy(group, of).wait_recv()

    def drain(self, groups):
        z = self.board.z
        if 0 in groups:
            for part in range(4):

                @pl.when(z < 3)
                def _():
                    self.line_copy(part).wait_send()

            for index in range(12):
                self.first_copy(index).wait_send()
            for of in range(4):
                for part in range(2):
                    self.first_core(of, part).wait_send()
        for group in groups:
            if group > 0:
                for plane in range(4):
                    if plane != group:

                        @pl.when(z == group)
                        def _():
                            self.far_copy(group, plane).wait_send()

                for index in range(4):
                    self.plane_copy(group, index).wait_send()
                    self.core_copy(group, index).wait_send()


class Scatter:
    def __init__(self, board, late, early, core_in, plane_in, line_in, total, sems):
        self.board = board
        self.late = late
        self.early = early
        self.core_in = core_in
        self.plane_in = plane_in
        self.line_in = line_in
        self.total = total
        self.core_s, self.core_r, self.plane_s, self.plane_r, self.line_s, self.line_r = sems

    def group(self, pack):
        return max(pack - 1, 0)

    def lanes(self, pack):
        return slice(0, D) if pack > 1 else slice(pack * HALF, pack * HALF + HALF)

    def home(self, group):
        return (self.late if group < 2 else self.early), 0

    def slot(self, group, index):
        return (4, 0, 0, 4)[group] + index

    def part(self, pack, of, begin, count=128):
        ref, first = self.home(self.group(pack))
        rows = self.board.half_rows(self.group(pack) * 4 + self.board.places[of] - first, None, begin, count)
        return ref.at[rows, self.lanes(pack)]

    def core_copy(self, pack, index):
        b = self.board
        group = self.group(pack)
        ref, first = self.home(group)
        rows = b.half_rows(group * 4 + index - first, core=1 - b.core)
        return remote(
            ref.at[rows, self.lanes(pack)],
            self.core_in.at[self.slot(group, index), :, self.lanes(pack)],
            self.core_s.at[pack * 4 + index], self.core_r.at[pack * 4 + index], b.across(),
        )

    def landed(self, pack, slot):
        return self.plane_in.at[self.group(pack) * 6 + slot, :, self.lanes(pack)]

    def plane_copy(self, pack, slot):
        of, near, begin = ((1, 1, 0), (3, 1, 0), (2, 2, 128), (3, 2, 128), (2, 2, 0), (1, 1, 128))[slot]
        b = self.board
        sem = pack * 6 + slot
        return remote(
            self.part(pack, of, begin), self.landed(pack, slot), self.plane_s.at[sem],
            self.plane_r.at[sem], b.chip(b.z, b.places[near]),
        )

    def line_copy(self, pack):
        b = self.board
        group = self.group(pack)
        slot = lax.rem(b.z - group + 4, 4) - 1
        half = 1 if pack == 1 else 0
        return remote(
            self.part(pack, 0, 0, HALF), self.line_in.at[slot, :, self.lanes(pack)],
            self.line_s.at[pack], self.line_r.at[half * 3 + slot], b.chip(group, b.place),
        )

    def add_core(self, pack):
        b = self.board
        group = self.group(pack)
        ref, first = self.home(group)
        lanes = self.lanes(pack)
        for index in range(4):
            self.core_copy(pack, index).wait_recv()
        for index in range(4):
            rows = b.half_rows(group * 4 + index - first)
            came = self.core_in[self.slot(group, index), :, lanes]
            ref[rows, lanes] = (ref[rows, lanes].astype(F32) + came.astype(F32)).astype(BF)
        for slot in (1, 3, 0, 2):
            self.plane_copy(pack, slot).start()

    def pass_plane(self, pack):
        for slot, of, begin, onward in ((1, 2, 0, 4), (3, 1, 128, 5)):
            self.plane_copy(pack, slot).wait_recv()
            mine = self.part(pack, of, begin)
            mine[...] = (mine[...].astype(F32) + self.landed(pack, slot)[...].astype(F32)).astype(BF)
            self.plane_copy(pack, onward).start()

    def end_plane(self, pack):
        b = self.board
        for begin, first, second in ((0, 0, 4), (128, 2, 5)):
            self.plane_copy(pack, first).wait_recv()
            self.plane_copy(pack, second).wait_recv()
            mine = self.part(pack, 0, begin)
            value = mine[...].astype(F32) + self.landed(pack, first)[...].astype(F32)
            value = value + self.landed(pack, second)[...].astype(F32)

            @pl.when(b.z == self.group(pack))
            def _():
                self.total[begin : begin + 128, self.lanes(pack)] = value

            @pl.when(b.z != self.group(pack))
            def _():
                mine[...] = value.astype(BF)

        @pl.when(b.z != self.group(pack))
        def _():
            self.line_copy(pack).start()

    def arrive(self, half, lanes):
        b = self.board
        value = self.total[:, lanes]
        for slot in range(3):
            view = self.line_in.at[slot, :, lanes]
            remote(
                view, view, self.line_s.at[5], self.line_r.at[half * 3 + slot], b.across()
            ).wait_recv()
            value = value + view[...].astype(F32)
        self.total[:, lanes] = value

    def drain(self):
        for pack in range(5):
            for index in range(4):
                self.core_copy(pack, index).wait_send()
            for slot in range(6):
                self.plane_copy(pack, slot).wait_send()

            @pl.when(self.board.z != self.group(pack))
            def _():
                self.line_copy(pack).wait_send()


def split(value):
    high = value.astype(BF)
    return high, (value - high.astype(F32)).astype(BF)


def product(left, right):
    return nn(left[0], right[0]) + (nn(left[0], right[1]) + nn(left[1], right[0]))


class Muon:
    def __init__(self, board, momentum, master, new_momentum, new_master, gram, work, mine,
                 theirs, sems):
        self.board = board
        self.momentum = momentum
        self.master = master
        self.new_momentum = new_momentum
        self.new_master = new_master
        self.gram = gram
        self.work = work
        self.mine = mine
        self.theirs = theirs
        self.core_in = work.at[0:HALF, :]
        self.plane_in = [work.at[HALF + 64 * near : HALF + 64 * near + 64, :] for near in range(3)]
        self.half_s, self.half_r, self.sum_s, self.sum_r, self.all_s, self.all_r, self.back_s, self.back_r = sems

    def part_rows(self, place, core=None):
        core = self.board.core if core is None else core
        return pl.ds(pl.multiple_of(core * HALF + place * 64, 64), 64)

    def half_copy(self):
        b = self.board
        rows = pl.ds(pl.multiple_of((1 - b.core) * HALF, HALF), HALF)
        return remote(
            self.gram.at[rows, :], self.core_in, self.half_s.at[0], self.half_r.at[0], b.across()
        )

    def sum_copy(self, near):
        b = self.board
        return remote(
            self.gram.at[self.part_rows(b.places[near]), :], self.plane_in[near - 1],
            self.sum_s.at[near - 1], self.sum_r.at[near - 1], b.chip(b.z, b.places[near]),
        )

    def all_copy(self, near):
        b = self.board
        view = self.mine.at[pl.ds(pl.multiple_of(b.place * 64, 64), 64), :]
        return remote(
            view, view, self.all_s.at[near - 1], self.all_r.at[near - 1],
            b.chip(b.z, b.places[near]),
        )

    def back_copy(self):
        return remote(
            self.mine, self.theirs, self.back_s.at[0], self.back_r.at[0], self.board.across()
        )

    def momentum_row(self):
        return 0.5 * self.momentum[...] + self.new_momentum[...]

    def begin(self):
        value = self.momentum_row()
        self.new_momentum[...] = value
        high, low = split(value)
        self.gram[...] = tn(high, high) + (tn(high, low) + tn(low, high))
        self.half_copy().start()

    def add_core(self):
        b = self.board
        self.half_copy().wait_recv()
        rows = pl.ds(pl.multiple_of(b.core * HALF, HALF), HALF)
        self.gram[rows, :] = self.gram[rows, :] + self.core_in[...]

    def send_sum(self):
        for near in range(1, 4):
            self.sum_copy(near).start()

    def send_all(self):
        b = self.board
        value = self.gram[self.part_rows(b.place), :]
        for near in range(1, 4):
            self.sum_copy(near).wait_recv()
            value = value + self.plane_in[near - 1][...]
        self.mine[pl.ds(pl.multiple_of(b.place * 64, 64), 64), :] = value
        for near in range(1, 4):
            self.all_copy(near).start()

    def wait_all(self):
        for near in range(1, 4):
            self.all_copy(near).wait_recv()

    def row_copy(self):
        return remote(
            self.mine, self.theirs, self.half_s.at[0], self.half_r.at[0], self.board.across()
        )

    def pair(self):
        self.mine[...] = self.momentum_row()
        self.row_copy().start()
        self.new_momentum[...] = self.mine[...]
        high, low = split(self.mine[...])
        first = tn(high, high) + (tn(high, low) + tn(low, high))
        self.row_copy().wait_recv()
        high, low = split(self.theirs[...])
        second = tn(high, high) + (tn(high, low) + tn(low, high))
        lower = self.board.core == 0
        self.gram[...] = jnp.where(lower, first, second) + jnp.where(lower, second, first)
        self.row_copy().wait_send()

    def send_back(self):
        self.back_copy().start()

    def gather(self):
        b = self.board
        self.half_copy().wait_send()
        for near in range(1, 4):
            self.sum_copy(near).wait_send()
            self.all_copy(near).wait_send()
        self.back_copy().wait()
        for core, held in ((b.core, self.mine), (1 - b.core, self.theirs)):
            self.gram[pl.ds(pl.multiple_of(core * HALF, HALF), HALF), :] = held[...]

    def iterate(self):
        gram = self.gram
        work = self.work
        current = self.new_master
        row = lax.broadcasted_iota(jnp.int32, (D, D), 0)
        col = lax.broadcasted_iota(jnp.int32, (D, D), 1)
        first = gram[...]
        square = jnp.sum(jnp.where(row == col, first, 0.0), axis=0, keepdims=True)
        divisor = jnp.sqrt(jnp.sum(square, axis=1, keepdims=True)) + 1e-07
        gram[...] = first / (divisor * divisor)
        current[...] = self.new_momentum[...] / divisor

        def polynomial():
            here = split(gram[...])
            diagonal = jnp.where(row == col, NS_A, 0.0)
            work[...] = diagonal + NS_B * gram[...] + NS_C * product(here, here)
            poly = split(work[...])
            current[...] = product(split(current[...]), poly)
            return here, poly

        def turn(step, carry):
            here, poly = polynomial()
            gram[...] = product(split(product(here, poly)), poly)
            return carry

        lax.fori_loop(0, 4, turn, 0)
        polynomial()
        stretch = jnp.where(self.board.z > 1, MUON_RATE * (FF / D) ** 0.5, MUON_RATE)
        current[...] = self.master[...] - stretch * current[...]


class VectorSum:
    def __init__(self, board, own, core_in, plane_in, line_in, total, send, recv):
        self.board = board
        self.own = own
        self.core_in = core_in
        self.plane_in = plane_in
        self.line_in = line_in
        self.total = total
        self.send = send
        self.recv = recv

    def core_copy(self):
        return remote(
            self.own, self.core_in, self.send.at[0], self.recv.at[0], self.board.across()
        )

    def plane_copy(self, near):
        b = self.board
        return remote(
            self.plane_in.at[b.place], self.plane_in.at[b.place], self.send.at[near],
            self.recv.at[near], b.chip(b.z, b.places[near]),
        )

    def line_copy(self, step):
        b = self.board
        return remote(
            self.line_in.at[b.z], self.line_in.at[b.z], self.send.at[3 + step],
            self.recv.at[3 + step], b.chip(lax.rem(b.z + step, 4), b.place),
        )

    def begin(self):
        self.core_copy().start()

    def middle(self):
        b = self.board
        self.core_copy().wait_recv()
        self.plane_in[b.place] = self.own[...] + self.core_in[...]
        for near in range(1, 4):
            self.plane_copy(near).start()

    def late(self):
        b = self.board
        for near in range(1, 4):
            self.plane_copy(near).wait_recv()
        self.line_in[b.z] = (
            (self.plane_in[0] + self.plane_in[1]) + (self.plane_in[2] + self.plane_in[3])
        )
        for step in range(1, 4):
            self.line_copy(step).start()

    def end(self):
        for step in range(1, 4):
            self.line_copy(step).wait_recv()
        value = (self.line_in[0] + self.line_in[1]) + (self.line_in[2] + self.line_in[3])
        self.total[...] = value[: self.total.shape[0], :]
        self.core_copy().wait_send()
        for near in range(1, 4):
            self.plane_copy(near).wait_send()
            self.line_copy(near).wait_send()


def layer_kernel(fused, *refs):
    tok, mem, cot, meta, vec, source, *refs = refs
    if fused:
        old_momentum, *refs = refs
    out_ref, igrad_ref, mgrad_ref, g_ref, gv_ref, *refs = refs
    if fused:
        new_master, *refs = refs
    (
        keys, metas, bias, probs_s, probs_c, flip, q_ref, cq_ref, attn_t, cross_t, grad_t, dq_t,
        parts, arrived, res_a, res_b, send_sem, recv_sem, meta_sem,
    ) = refs[:19]
    core = lax.axis_index("stream")
    other = 1 - core
    own = pl.ds(pl.multiple_of(core * ROWS, ROWS), ROWS)
    theirs = pl.ds(pl.multiple_of(other * ROWS, ROWS), ROWS)
    barrier = pltpu.get_barrier_semaphore()
    gather = scatter = vectors = None
    if fused:
        w, core_in, plane_in, line_in, vec_own, vec_core, vec_plane, vec_line = refs[19:27]
        sems = refs[27:]
        board = Board()
        gather = Gather(board, w, *sems[:10])
        sems = sems[10:]
        scatter = Scatter(board, probs_c, w, core_in, plane_in, line_in, g_ref, sems[:6])
        vectors = VectorSum(
            board, vec_own, vec_core, vec_plane, vec_line, gv_ref, sems[6], sems[7]
        )
        muon = Muon(
            board, old_momentum, source, g_ref, new_master, bias.at[0:D, :], bias.at[D : 2 * D, :],
            igrad_ref.at[0:HALF, :], igrad_ref.at[HALF:D, :], sems[8:],
        )
        w[board.half_rows(board.dp), :] = source[...].astype(BF)
        friends = [board.across()]
        friends += [board.chip(board.z, board.places[near]) for near in range(1, 4)]
        friends += [board.chip(lax.rem(board.z + step, 4), board.place) for step in range(1, 4)]
        sums = vec_own
        sums[...] = jnp.zeros_like(sums)
    else:
        w = source
        friends = [{"stream": other}]
        sums = gv_ref
    for friend in friends:
        pl.semaphore_signal(barrier, inc=1, device_id=friend, device_id_type=MESH)
    pl.semaphore_wait(barrier, len(friends))

    def swap(src, dst, index):
        return remote(src, dst, send_sem.at[index], recv_sem.at[index], {"stream": other})

    def weight(index):
        return w[index * D : (index + 1) * D, :]

    def vector(index):
        return vec[index : index + 1, :]

    def gradient(group, index, value):
        if fused:
            ref, first = scatter.home(group)
            rows = pl.ds(pl.multiple_of((group * 4 + index - first) * D, D), D)
            ref[rows, :] = value.astype(BF)
            if group > 0:
                scatter.core_copy(group + 1, index).start()
        else:
            rows = pl.ds(pl.multiple_of((group * 4 + index) * D, D), D)
            g_ref[rows, :] = value.astype(BF)

    meta_copy = remote(meta, metas, meta_sem.at[0], meta_sem.at[1], {"stream": other})
    meta_copy.start()
    if fused:
        gather.first_line()
    hid, _, _ = norm_forward(tok[...].astype(F32), vector(0), vector(1))
    attn_t[...] = hid.astype(BF)

    meta_copy.wait()
    row = lax.broadcasted_iota(jnp.int32, (ROWS, ROWS), 0)
    col = lax.broadcasted_iota(jnp.int32, (ROWS, ROWS), 1)

    def fill_bias(with_priority):
        for rows, held, own_half in ((own, meta, True), (theirs, metas, False)):
            turned = held[...].T
            visible = turned[:, 0:1] == meta[2:3, :]
            if with_priority:
                visible = visible & (turned[:, 1:2] < meta[3:4, :])
            if own_half:
                visible = visible | (row == col)
            bias[rows, :] = jnp.where(visible, 0.0, -1e30)

    fill_bias(True)
    if fused:
        gather.first_plane()
        gather.send_plane(1)
        gather.finish(0)

    copies = [swap(keys.at[index, own, :], keys.at[index, own, :], index) for index in range(4)]
    hid = attn_t[...]
    keys[0, own, :] = nn(hid, weight(1)).astype(BF)
    copies[0].start()
    keys[1, own, :] = (nn(hid, weight(2)) + vector(7)).astype(BF)
    copies[1].start()
    q_ref[...] = (nn(hid, weight(0)) + vector(6)).astype(BF)
    copies[0].wait()
    copies[1].wait()
    flip[...] = keys[1].T

    def self_forward(pair):
        attend_forward(q_ref, keys.at[0], flip, bias, probs_s, attn_t, (pair, pair + 1))

    self_forward(0)
    if fused:
        gather.pass_plane(1)
        gather.send_plane(2)
    self_forward(1)
    self_forward(2)
    if fused:
        gather.send_core(1)
    self_forward(3)
    if fused:
        gather.pass_plane(2)
        gather.send_plane(3)
    res_one = tok[...].astype(F32) + nn(attn_t[...].T, weight(3)) + vector(8)
    res_a[...] = res_one
    hid, _, _ = norm_forward(res_one, vector(2), vector(3))
    fill_bias(False)
    if fused:
        gather.finish(1)
    keys[2, own, :] = nn(mem[...], weight(5)).astype(BF)
    copies[2].start()
    keys[3, own, :] = (nn(mem[...], weight(6)) + vector(10)).astype(BF)
    copies[3].start()
    cq_ref[...] = (nn(hid.astype(BF), weight(4)) + vector(9)).astype(BF)
    copies[2].wait()
    copies[3].wait()
    flip[...] = keys[3].T
    def cross_forward(pair):
        attend_forward(cq_ref, keys.at[2], flip, bias, probs_c, cross_t, (pair, pair + 1))

    cross_forward(0)
    if fused:
        gather.send_core(2)
    cross_forward(1)
    if fused:
        gather.pass_plane(3)
    cross_forward(2)
    cross_forward(3)
    res_two = res_a[...] + nn(cross_t[...].T, weight(7)) + vector(11)
    res_b[...] = res_two
    hid, _, _ = norm_forward(res_two, vector(4), vector(5))
    grad_t[...] = hid.astype(BF)
    mgrad_ref[...] = jnp.zeros((ROWS, D), F32)
    igrad_ref[...] = res_two + vector(12)
    sums[12:13, :] = column_sum(cot[...])
    if fused:
        gather.send_core(3)
        gather.finish(2)
        gather.finish(3)
        gather.drain((2, 3))

    def ffn_body(part, carry):
        w_in = w[pl.ds(pl.multiple_of(8 * D + part * D, D), D), :]
        w_out = w[pl.ds(pl.multiple_of(8 * D + FF + part * D, D), D), :]
        h_three = grad_t[...]
        pre = nt(h_three, w_in) + vec[pl.ds(13 + part, 1), :]
        hidden = jnp.maximum(pre, 0.0).astype(BF)
        igrad_ref[...] += nn(hidden, w_out)
        grad_pre = jnp.where(pre > 0, nt(cot[...], w_out), 0.0).astype(BF)
        mgrad_ref[...] += nn(grad_pre, w_in)
        sums[pl.ds(13 + part, 1), :] = column_sum(grad_pre)
        gradient(2, part, tn(grad_pre, h_three))
        gradient(3, part, tn(hidden, cot[...]))
        return carry

    lax.fori_loop(0, FF // D, ffn_body, 0)
    out_ref[...] = igrad_ref[...].astype(BF)

    _, normed, spread = norm_forward(res_b[...], vector(4), vector(5))
    grad_in, sums[4:5, :], sums[5:6, :] = norm_backward(normed, spread, vector(4), mgrad_ref[...])
    grad_res = cot[...].astype(F32) + grad_in
    res_b[...] = grad_res
    sums[11:12, :] = column_sum(grad_res)
    dz_two = grad_res.astype(BF)
    grad_t[...] = nt(weight(7), dz_two).astype(BF)
    flip[...] = keys[2].T
    if fused:
        scatter.add_core(3)
        scatter.add_core(4)

    def cross_back(pairs):
        attend_backward(
            cq_ref, flip, keys.at[3], grad_t, cross_t, probs_c, dq_t, parts.at[0], parts.at[1], pairs
        )

    cross_back((0, 4))

    def back_copy(index, lanes, sem):
        rows = parts.at[index % 2, theirs, lanes]
        return swap(rows, arrived.at[index % arrived.shape[0], :, lanes], sem)

    whole = slice(0, D)
    back = [back_copy(2, whole, 4), back_copy(3, whole, 5)]
    back[0].start()
    back[1].start()

    def summed(index, lanes):
        mine = parts[index % 2, own, lanes].astype(F32)
        return (mine + arrived[index % arrived.shape[0], :, lanes].astype(F32)).astype(BF)

    if fused:
        scatter.pass_plane(3)
    grad_cq = dq_t[...].T
    sums[9:10, :] = column_sum(grad_cq)
    hid, normed, spread = norm_forward(res_a[...], vector(2), vector(3))
    grad_in, sums[2:3, :], sums[3:4, :] = norm_backward(
        normed, spread, vector(2), nt(grad_cq, weight(4))
    )
    back[0].wait()
    back[1].wait()
    grad_mk = summed(2, whole)
    grad_mv = summed(3, whole)
    gradient(1, 0, tn(hid.astype(BF), grad_cq))
    gradient(1, 3, nn(cross_t[...], res_b[...].astype(BF)))
    grad_res = res_b[...] + grad_in
    res_b[...] = grad_res
    sums[8:9, :] = column_sum(grad_res)
    sums[10:11, :] = column_sum(grad_mv)
    gradient(1, 1, tn(mem[...], grad_mk))
    gradient(1, 2, tn(mem[...], grad_mv))
    mgrad_ref[...] = nt(grad_mk, weight(5)) + nt(grad_mv, weight(6))
    dz_one = res_b[...].astype(BF)
    grad_t[...] = nt(weight(3), dz_one).astype(BF)
    gradient(0, 3, nn(attn_t[...], dz_one))
    flip[...] = keys[0].T
    if fused:
        scatter.pass_plane(4)
        scatter.end_plane(3)
        scatter.add_core(2)

    def self_back(pairs):
        attend_backward(
            q_ref, flip, keys.at[1], grad_t, attn_t, probs_s, dq_t, parts.at[0], parts.at[1], pairs
        )

    def send_back(half):
        lanes = slice(half * HALF, half * HALF + HALF)
        both = [back_copy(index, lanes, half * 2 + index) for index in (0, 1)]
        for copy in both:
            copy.start()
        return both

    def first_weights(half, copies):
        lanes = slice(half * HALF, half * HALF + HALF)
        low = norm_forward(tok[...].astype(F32), vector(0), vector(1))[0].astype(BF)
        grad_q = dq_t[lanes, :].T
        sums[6:7, lanes] = column_sum(grad_q)
        values = [grad_q]
        late = scatter.late if fused else g_ref
        late[0:D, lanes] = tn(low, grad_q).astype(BF)
        if fused:
            scatter.core_copy(half, 3).start()
            scatter.core_copy(half, 0).start()
        for index in (0, 1):
            copies[index].wait()
            value = summed(index, lanes)
            values.append(value)
            late[(index + 1) * D : (index + 2) * D, lanes] = tn(low, value).astype(BF)
            if fused:
                scatter.core_copy(half, index + 1).start()
        sums[7:8, lanes] = column_sum(values[2])
        total = None
        for index, value in enumerate(values):
            term = nt(value, w[index * D : (index + 1) * D, lanes])
            total = term if total is None else total + term
        if half == 0:
            res_a[...] = total
        else:
            res_a[...] += total

    self_back((0, 2))
    copies = send_back(0)
    if fused:
        scatter.end_plane(4)
    self_back((2, 3))
    first_weights(0, copies)
    if fused:
        scatter.pass_plane(2)
    self_back((3, 4))
    copies = send_back(1)
    if fused:
        scatter.add_core(0)
    first_weights(1, copies)
    if fused:
        scatter.add_core(1)
        scatter.pass_plane(0)
        scatter.end_plane(2)
    _, normed, spread = norm_forward(tok[...].astype(F32), vector(0), vector(1))
    grad_in, sums[0:1, :], sums[1:2, :] = norm_backward(normed, spread, vector(0), res_a[...])
    res_b[...] += grad_in
    if fused:
        vectors.begin()
        wide_plane = board.z > 1
        scatter.end_plane(0)

        @pl.when(wide_plane)
        def _():
            scatter.arrive(0, whole)
            muon.begin()

        scatter.pass_plane(1)
        vectors.middle()

        @pl.when(wide_plane)
        def _():
            muon.add_core()
            muon.send_sum()

        scatter.end_plane(1)
        vectors.late()

        @pl.when(board.z == 1)
        def _():
            scatter.arrive(0, whole)

        @pl.when(board.z == 0)
        def _():
            scatter.arrive(0, slice(0, HALF))
            scatter.arrive(1, slice(HALF, D))

        @pl.when(board.z < 2)
        def _():
            muon.pair()

        @pl.when(wide_plane)
        def _():
            muon.send_all()
            muon.wait_all()
            muon.send_back()
            muon.gather()

    igrad_ref[...] = res_b[...]
    if fused:
        muon.iterate()
        vectors.end()
        gather.drain((0, 1))
        scatter.drain()


def layer_call(fused, tok, mem, cot, meta, vec, source, *rest):
    shape = jax.ShapeDtypeStruct
    vmem = pl.BlockSpec(memory_space=pltpu.VMEM)
    dma = pltpu.SemaphoreType.DMA
    scratch = [
        pltpu.VMEM((4, KEYS, D), BF),
        pltpu.VMEM((8, ROWS), jnp.int32),
        pltpu.VMEM((KEYS, ROWS), F32),
        pltpu.VMEM((HEADS * KEYS, ROWS), BF),
        pltpu.VMEM((HEADS * KEYS, ROWS), BF),
        pltpu.VMEM((D, KEYS), BF),
        *[pltpu.VMEM((ROWS, D), BF) for _ in range(6)],
        pltpu.VMEM((2, KEYS, D), BF),
        pltpu.VMEM((2 if fused else 4, ROWS, D), BF),
        *[pltpu.VMEM((ROWS, D), F32) for _ in range(2)],
        dma((8,)), dma((8,)), dma((2,)),
    ]
    if fused:
        scratch += [
            pltpu.VMEM((8 * D + 2 * FF, D), BF),
            pltpu.VMEM((8, HALF, D), BF),
            pltpu.VMEM((24, 128, D), BF),
            pltpu.VMEM((3, HALF, D), BF),
            pltpu.VMEM((24, D), F32),
            pltpu.VMEM((24, D), F32),
            pltpu.VMEM((4, 24, D), F32),
            pltpu.VMEM((4, 24, D), F32),
            *[dma((count,)) for count in (4, 4, 4, 4, 12, 12, 12, 12, 20, 20)],
            *[dma((count,)) for count in (20, 20, 30, 30, 6, 6)],
            *[dma((count,)) for count in (7, 7, 1, 1, 3, 3, 3, 3, 1, 1)],
        ]
    grad_shape = shape((HALF, D), F32) if fused else shape(source.shape, BF)
    return pl.pallas_call(
        functools.partial(layer_kernel, fused),
        out_shape=[
            shape((ROWS, D), BF), shape((ROWS, D), F32), shape((ROWS, D), F32),
            grad_shape, shape(vec.shape, F32), *[shape((HALF, D), F32) for _ in rest],
        ],
        in_specs=[vmem] * (6 + len(rest)),
        out_specs=[vmem] * (5 + len(rest)),
        scratch_shapes=scratch,
        compiler_params=pltpu.CompilerParams(
            collective_id=0, has_side_effects=True, vmem_limit_bytes=63 * 1024 * 1024
        ),
        cost_estimate=pl.CostEstimate(
            flops=22_000_000_000, bytes_accessed=24_000_000, transcendentals=8_000_000
        ),
    )(tok, mem, cot, meta, vec, source, *rest)


def copy_kernel(*refs):
    count = len(refs) // 2
    for index in range(count):
        refs[count + index][...] = refs[index][...]


def copy_out(*arrays):
    vmem = pl.BlockSpec(memory_space=pltpu.VMEM)
    return pl.pallas_call(
        copy_kernel,
        out_shape=[jax.ShapeDtypeStruct(array.shape, array.dtype) for array in arrays],
        in_specs=[vmem] * len(arrays),
        out_specs=[vmem] * len(arrays),
        compiler_params=pltpu.CompilerParams(vmem_limit_bytes=62 * 1024 * 1024),
    )(*arrays)


def partner(block, axis, stride):
    count = lax.axis_size(axis)
    route = []
    for low in range(count):
        high = low | 1 << stride
        if high != low and high < count:
            route += [(low, high), (high, low)]
    return lax.ppermute(block, axis, route)


def high_dot(left_mat, right_mat):
    return jnp.dot(left_mat, right_mat, precision=lax.Precision.HIGH)


def exact_lead(left_mat, right_mat):
    return lax.dot_general(left_mat, right_mat, (((0,), (0,)), ((), ())), precision=HIGH)


def per_device(
    tokens,
    memory,
    cotangent,
    segments,
    padding,
    priority,
    threshold,
    master,
    momentum,
    vectors,
    vec_first,
    vec_second,
    step_count,
):
    meta = jnp.stack([jnp.where(padding == 0, segments, -1), priority, segments, threshold] * 2)
    matrix = vectors.reshape(-1, D)
    if lax.axis_size("dp") == 16 and lax.axis_size("stream") == 2:
        layer_out, input_grad, memory_grad, new_momentum, grad_vec, new_master = layer_call(
            True, tokens, memory, cotangent, meta, matrix, master, momentum
        )
        grad_vec = grad_vec.reshape(-1)
        layer_out, input_grad, memory_grad, new_momentum, new_master = copy_out(
            layer_out, input_grad, memory_grad, new_momentum, new_master
        )
    else:
        low_all = lax.all_gather(master.astype(BF), ("dp", "stream"), axis=0, tiled=True)
        layer_out, input_grad, memory_grad, grad_all, vec_local = layer_call(
            False, tokens, memory, cotangent, meta, matrix, low_all
        )
        grad_rows = lax.psum_scatter(
            grad_all, ("dp", "stream"), scatter_dimension=0, tiled=True
        ).astype(F32)
        grad_vec = lax.psum(vec_local.reshape(-1), ("dp", "stream"))
        opt_rows = master.shape[0]
        device_index = lax.axis_index(("dp", "stream"))
        start_row = device_index * opt_rows
        in_ffn = start_row >= 8 * D
        att_bits = (D // opt_rows).bit_length() - 1
        ffn_bits = (FF // opt_rows).bit_length() - 1
        own_bits = jnp.where(in_ffn, ffn_bits, att_bits)
        new_momentum = 0.5 * momentum + grad_rows

        def gram_total(partial_value):
            for bit_pos in range(ffn_bits):
                other = partner(partial_value, ("dp", "stream"), bit_pos)
                partial_value = partial_value + jnp.where(bit_pos < own_bits, other, 0.0)
            return partial_value

        gram_first = gram_total(exact_lead(new_momentum, new_momentum))
        divisor = jnp.sqrt(jnp.trace(gram_first)) + 1e-07
        gram = gram_first / (divisor * divisor)
        unit = jnp.eye(D, dtype=jnp.float32)
        chain = None
        for turn in range(5):
            poly = NS_A * unit + NS_B * gram + NS_C * high_dot(gram, gram)
            chain = poly if chain is None else high_dot(chain, poly)
            if turn < 4:
                gram = high_dot(high_dot(gram, poly), poly)
        current = high_dot(new_momentum / divisor, chain)
        rate = MUON_RATE * jnp.where(in_ffn, (FF / D) ** 0.5, 1.0)
        new_master = master - rate * current
    count = step_count[0].astype(jnp.float32)
    new_first = 0.5 * vec_first + 0.5 * grad_vec
    new_second = 0.999 * vec_second + 0.001 * grad_vec * grad_vec
    first_fix = new_first / (1.0 - jnp.power(0.5, count))
    second_fix = new_second / (1.0 - jnp.power(0.999, count))
    new_vectors = vectors - ADAM_RATE * (
        first_fix / (jnp.sqrt(second_fix) + 1e-08) + ADAM_DECAY * vectors
    )
    return (
        layer_out,
        input_grad,
        memory_grad,
        new_momentum,
        new_master,
        new_vectors,
        new_first,
        new_second,
    )


def solution(mesh):
    return jax.shard_map(
        per_device,
        mesh=mesh,
        in_specs=(
            P(("dp", "stream"), None),
            P(("dp", "stream"), None),
            P(("dp", "stream"), None),
            P(("dp", "stream")),
            P(("dp", "stream")),
            P(("dp", "stream")),
            P(("dp", "stream")),
            P(("dp", "stream"), None),
            P(("dp", "stream"), None),
            P(),
            P(),
            P(),
            P(),
        ),
        out_specs=(
            P(("dp", "stream"), None),
            P(("dp", "stream"), None),
            P(("dp", "stream"), None),
            P(("dp", "stream"), None),
            P(("dp", "stream"), None),
            P(),
            P(),
            P(),
        ),
        check_vma=False,
    )
```
